32 devices in a mesh: lat: 8 (over z, x), lev: 4 (over y, core).
Axes of the slice: x: 2, y: 2, z: 4, core: 2. Of those that a mesh axis runs over, the one named last changes fastest.
Arguments:
- tokens: bfloat16 [2, 4, 16, 64, 1024], P(None, 'lev', 'lat'), may hold values from -40 to 40
- key_mask: int32 [2, 16], replicated, may hold values from 0 to 1, as said below
- w_qkv: bfloat16 [1024, 3072], replicated, may hold values from -0.1875 to 0.1875
- w_mix: bfloat16 [4, 1024, 1024], P('lev'), may hold values from -0.09375 to 0.09375
- level_scale: float32 [4, 1024], P('lev'), may hold values from 0.1 to 1.9
- cotangent: bfloat16 [2, 4, 16, 64, 1024], P(None, 'lev', 'lat'), may hold values from -6 to 6
Outputs:
- output: bfloat16 [2, 4, 16, 64, 1024], P(None, 'lev', 'lat')
- d_tokens: bfloat16 [2, 4, 16, 64, 1024], P(None, 'lev', 'lat')
- mix_grad: float32 [4, 1024, 1024], P('lev', 'lat')
The draws below stay inside these ranges and needn't reach their ends.
Inputs may be any that keep to these rules, and one draw needn't show every extreme that they name: `key_mask`: each sample has 1 to 4 padded rows, all at the end of the latitude rows, and the rest real; some sample has exactly 4 padded rows.
All inputs are finite; a program needn't handle non-finite values.
Results may differ from the reference program's by a relative error of at most 0.015.
Values may be sent and summed in bfloat16 or wider, within the bound.
No kernel may reach another device: no remote copies, remote signals or barrier semaphores. Data moves between devices by JAX's collectives and lax.ppermute only.
A program may use at most 128 MiB of HBM per device.

```python
import math
import jax
import jax.numpy as jnp
from jax import lax

WIDTH = 1024
HEADS = 16
HEAD_DIM = 64
LON = 64
LAT = 16
LEV = 4
BATCH = 2
PAD_MOST = 4


def draw_tokens(key, part):
    base_key, row_key, col_key = jax.random.split(key, 3)
    full_shape = (BATCH, LEV, LAT, LON, WIDTH)
    log_low = math.log(0.3)
    log_high = math.log(3.0)
    row_scale = jnp.exp(jax.random.uniform(row_key, full_shape[:-1] + (1,), jnp.float32, log_low, log_high))
    col_scale = jnp.exp(jax.random.uniform(col_key, (WIDTH,), jnp.float32, log_low, log_high))
    base_values = jnp.clip(jax.random.normal(base_key, full_shape, jnp.float32), -4.0, 4.0)
    return (base_values * row_scale * col_scale).astype(jnp.bfloat16)


def draw_key_mask(key, part):
    count_key, pick_key = jax.random.split(key)
    pad_rows = jax.random.randint(count_key, (BATCH,), 1, PAD_MOST + 1).astype(jnp.int32)
    chosen = jax.random.randint(pick_key, (), 0, BATCH).astype(jnp.int32)
    sample_index = jnp.arange(BATCH, dtype=jnp.int32)
    pad_rows = jnp.where(sample_index == chosen, jnp.int32(PAD_MOST), pad_rows).astype(jnp.int32)
    lat_index = jnp.arange(LAT, dtype=jnp.int32)
    return (lat_index[None, :] < (LAT - pad_rows)[:, None]).astype(jnp.int32)


def block_levels(rng, shape, cuts, least, largest):
    def one(axis_at, parts):
        draws = jax.random.uniform(jax.random.fold_in(jax.random.fold_in(rng, 6), axis_at), (parts,), jnp.float32, least / len(cuts), largest / len(cuts))
        return jnp.repeat(jnp.exp(draws), shape[axis_at] // parts).reshape((-1,) + (1,) * (len(shape) - axis_at - 1))

    level = one(*cuts[0])
    for cut in cuts[1:]:
        level = level * one(*cut)
    return level


def noise(key, shape, deviation, reach, cuts=(), held_as=jnp.bfloat16):
    values = deviation * jax.random.normal(key, shape, jnp.float32)
    if cuts:
        values = values * block_levels(key, shape, cuts, -0.22, 0.18)
    return jnp.clip(values, -reach, reach).astype(held_as)


def setup_inputs(seed: int = 0) -> dict:
    seeds = jax.random.split(jax.random.key(seed), 7)
    tokens = draw_tokens(jax.random.fold_in(seeds[6], 71), 0)
    key_mask = draw_key_mask(jax.random.fold_in(seeds[6], 71), 0)
    w_qkv = noise(seeds[2], (WIDTH, 3 * WIDTH), WIDTH ** -0.5, 0.1875)
    w_mix = noise(seeds[3], (LEV, WIDTH, WIDTH), (WIDTH * LEV) ** -0.5, 0.09375, ((0, 4),))
    level_scale = jnp.clip(1.0 + 0.18 * jax.random.normal(seeds[4], (LEV, WIDTH), jnp.float32), 0.1, 1.9)
    cotangent = noise(seeds[5], (BATCH, LEV, LAT, LON, WIDTH), 1.0, 6.0, ((1, 4), (2, 8)))
    return dict(tokens=tokens, key_mask=key_mask, w_qkv=w_qkv, w_mix=w_mix, level_scale=level_scale, cotangent=cotangent)


epsilon = 1e-06
score_scale = 0.25

def rms_factor(values):
    return lax.rsqrt(lax.optimization_barrier(jnp.mean(values * values, axis=-1, keepdims=True)) + epsilon)

def norm_backward(values, factor, upstream):
    inner_mean = lax.optimization_barrier(jnp.mean(upstream * values, axis=-1, keepdims=True))
    return factor * upstream - values * (factor * factor * factor) * inner_mean

def attention_weights(query_heads, key_heads, valid_keys):
    scores = jnp.einsum('bijne,bkjne->bjnik', query_heads.astype(jnp.float32), key_heads.astype(jnp.float32)) * score_scale
    exp_scores = jnp.exp(scores) * valid_keys.astype(jnp.float32)[:, None, None, None, :]
    return exp_scores / lax.optimization_barrier(jnp.sum(exp_scores, axis=-1, keepdims=True))

def project(level_tokens, w_qkv):
    tokens_f32 = level_tokens.astype(jnp.float32)
    factor = rms_factor(tokens_f32)
    normed = (tokens_f32 * factor).astype(jnp.bfloat16)
    projected = jnp.dot(normed.reshape(-1, WIDTH), w_qkv, preferred_element_type=jnp.float32)
    head_shape = level_tokens.shape[:-1] + (HEADS, HEAD_DIM)
    query = projected[:, :WIDTH].reshape(head_shape)
    key_raw = projected[:, WIDTH:2 * WIDTH].reshape(head_shape)
    value = projected[:, 2 * WIDTH:].reshape(head_shape)
    query_factor = rms_factor(query)
    key_factor = rms_factor(key_raw)
    query_norm = (query * query_factor).astype(jnp.bfloat16)
    key_norm = (key_raw * key_factor).astype(jnp.bfloat16)
    value_cast = value.astype(jnp.bfloat16)
    return (tokens_f32, factor, normed, query, query_factor, key_raw, key_factor, query_norm, key_norm, value_cast)

def reference(tokens, key_mask, w_qkv, w_mix, level_scale, cotangent):
    by_level = jnp.moveaxis(tokens, 1, 0)
    cot_by_level = jnp.moveaxis(cotangent, 1, 0)

    def forward_level(mix_total, inputs):
        level_tokens, mixer_level = inputs
        pieces = project(level_tokens, w_qkv)
        weights = attention_weights(pieces[7], pieces[8], key_mask)
        weights_b = lax.optimization_barrier(weights.astype(jnp.bfloat16)).astype(jnp.float32)
        attended = jnp.einsum('bjnik,bkjne->bijne', weights_b, pieces[9].astype(jnp.float32)).astype(jnp.bfloat16)
        attended = attended.reshape(level_tokens.shape)
        mix_total = mix_total + jnp.dot(attended.reshape(-1, WIDTH), mixer_level, preferred_element_type=jnp.float32)
        return (mix_total, attended)
    zero_total = jnp.zeros((BATCH * LAT * LON, WIDTH), jnp.float32)
    mix_total, attended_all = lax.scan(forward_level, zero_total, (by_level, w_mix))
    level_mix = mix_total.reshape(BATCH, 1, LAT, LON, WIDTH)
    level_gain = level_scale[None, :, None, None, :]
    output = (tokens.astype(jnp.float32) + level_gain * level_mix).astype(jnp.bfloat16)
    flow_total = lax.optimization_barrier(jnp.sum(level_gain * cotangent.astype(jnp.float32), axis=1))
    flow_b = flow_total.astype(jnp.bfloat16).reshape(-1, WIDTH)
    token_total = BATCH * LAT * LON

    def backward_level(unused_carry, inputs):
        level_tokens, mixer_level, attended, level_cotangent = inputs
        grad_mix = jnp.dot(attended.reshape(-1, WIDTH).T, flow_b, preferred_element_type=jnp.float32) / math.sqrt(token_total)
        head_shape = level_tokens.shape[:-1] + (HEADS, HEAD_DIM)
        d_attended = jnp.dot(flow_b, mixer_level.T, preferred_element_type=jnp.float32).astype(jnp.bfloat16).reshape(head_shape)
        tokens_f32, factor, normed, query, query_factor, key_raw, key_factor, query_norm, key_norm, value_cast = project(level_tokens, w_qkv)
        weights = attention_weights(query_norm, key_norm, key_mask)
        weights_b = lax.optimization_barrier(weights.astype(jnp.bfloat16)).astype(jnp.float32)
        d_float = d_attended.astype(jnp.float32)
        d_value = jnp.einsum('bjnik,bijne->bkjne', weights_b, d_float).astype(jnp.bfloat16)
        d_attn = jnp.einsum('bijne,bkjne->bjnik', d_float, value_cast.astype(jnp.float32))
        d_scores = weights * (d_attn - lax.optimization_barrier(jnp.sum(weights * d_attn, axis=-1, keepdims=True)))
        d_scores_b = lax.optimization_barrier((d_scores * score_scale).astype(jnp.bfloat16)).astype(jnp.float32)
        d_query = jnp.einsum('bjnik,bkjne->bijne', d_scores_b, key_norm.astype(jnp.float32)).astype(jnp.bfloat16)
        d_key = jnp.einsum('bjnik,bijne->bkjne', d_scores_b, query_norm.astype(jnp.float32)).astype(jnp.bfloat16)
        grad_query = norm_backward(query, query_factor, d_query.astype(jnp.float32))
        grad_key = norm_backward(key_raw, key_factor, d_key.astype(jnp.float32))
        grad_proj = jnp.concatenate([grad_query.reshape(-1, WIDTH), grad_key.reshape(-1, WIDTH), d_value.astype(jnp.float32).reshape(-1, WIDTH)], axis=1).astype(jnp.bfloat16)
        d_normed = jnp.dot(grad_proj, w_qkv.T, preferred_element_type=jnp.float32).reshape(level_tokens.shape)
        d_level = (level_cotangent.astype(jnp.float32) + norm_backward(tokens_f32, factor, d_normed)).astype(jnp.bfloat16)
        return (unused_carry, (d_level, grad_mix))
    _, (d_levels, mix_grad) = lax.scan(backward_level, jnp.zeros((), jnp.float32), (by_level, w_mix, attended_all, cot_by_level))
    d_tokens = jnp.moveaxis(d_levels, 0, 1)
    return (output, d_tokens, mix_grad)
```

```python
import functools
import math

import jax
import jax.numpy as jnp
from jax import lax
from jax.experimental import pallas as pl
from jax.experimental.pallas import tpu as pltpu
from jax.sharding import PartitionSpec as P

HEADS = 16
GROUP = 256

epsilon = 1e-06
score_scale = 0.25

F32 = jnp.float32
BF16 = jnp.bfloat16


def nn(a, b):
    return lax.dot_general(a, b, (((1,), (0,)), ((), ())), preferred_element_type=F32)


def nt(a, b):
    return lax.dot_general(a, b, (((1,), (1,)), ((), ())), preferred_element_type=F32)


def tn(a, b):
    return lax.dot_general(a, b, (((0,), (0,)), ((), ())), preferred_element_type=F32)


def block_mean(head_width):
    row = lax.broadcasted_iota(jnp.int32, (GROUP, GROUP), 0) // head_width
    col = lax.broadcasted_iota(jnp.int32, (GROUP, GROUP), 1) // head_width
    return jnp.where(row == col, 1.0 / head_width, 0.0).astype(BF16)


def params():
    return pltpu.CompilerParams(vmem_limit_bytes=44 * 1024 * 1024)


def pack_tokens_kernel(sizes, tok_ref, out_ref):
    batch, rows, parts, chunk = sizes
    for b in range(batch):
        for q in range(parts):
            for r in range(rows):
                out_ref[b * parts + q, r] = tok_ref[b, r, q * chunk : (q + 1) * chunk, :]


def pack_tokens(tokens, sizes):
    batch, rows, parts, chunk = sizes
    width = tokens.shape[-1]
    return pl.pallas_call(
        functools.partial(pack_tokens_kernel, sizes),
        out_shape=jax.ShapeDtypeStruct((batch * parts, rows, chunk, width), BF16),
        grid=(4,),
        in_specs=[
            pl.BlockSpec((batch, rows, parts * chunk, width // 4), lambda i: (0, 0, 0, i))
        ],
        out_specs=pl.BlockSpec((batch * parts, rows, chunk, width // 4), lambda i: (0, 0, 0, i)),
        compiler_params=params(),
        name="pack_tokens",
    )(tokens)


def pack_cotangent_kernel(sizes, cot_ref, gain_ref, out_ref):
    batch, rows, parts, chunk = sizes
    gain = gain_ref[...]
    for b in range(batch):
        for q in range(parts):
            for r in range(rows):
                piece = cot_ref[b, r, q * chunk : (q + 1) * chunk, :].astype(F32)
                out_ref[0, b * parts + q, r] = (piece * gain).astype(BF16)


def pack_cotangent(cot, gain, sizes, levels):
    batch, rows, parts, chunk = sizes
    width = cot.shape[-1]
    share = width // levels
    return pl.pallas_call(
        functools.partial(pack_cotangent_kernel, sizes),
        out_shape=jax.ShapeDtypeStruct((levels, batch * parts, rows, chunk, share), BF16),
        grid=(levels,),
        in_specs=[
            pl.BlockSpec((batch, rows, parts * chunk, share), lambda i: (0, 0, 0, i)),
            pl.BlockSpec((1, share), lambda i: (0, i)),
        ],
        out_specs=pl.BlockSpec(
            (1, batch * parts, rows, chunk, share), lambda i: (i, 0, 0, 0, 0)
        ),
        compiler_params=params(),
        name="pack_cotangent",
    )(cot, gain)


def output_kernel(sizes, tok_ref, gain_ref, mix_ref, out_ref):
    batch, rows, parts, chunk = sizes
    gain = gain_ref[...]
    for b in range(batch):
        for q in range(parts):
            for r in range(rows):
                cells = slice(q * chunk, (q + 1) * chunk)
                mixed = mix_ref[0, b * parts + q, r].astype(F32)
                out_ref[b, r, cells, :] = (
                    tok_ref[b, r, cells, :].astype(F32) + gain * mixed
                ).astype(BF16)


def make_output(tokens, gain, mixed, sizes, levels):
    batch, rows, parts, chunk = sizes
    width = tokens.shape[-1]
    share = width // levels
    band = pl.BlockSpec((batch, rows, parts * chunk, share), lambda i: (0, 0, 0, i))
    return pl.pallas_call(
        functools.partial(output_kernel, sizes),
        out_shape=jax.ShapeDtypeStruct(tokens.shape, BF16),
        grid=(levels,),
        in_specs=[
            band,
            pl.BlockSpec((1, share), lambda i: (0, i)),
            pl.BlockSpec((1, batch * parts, rows, chunk, share), lambda i: (i, 0, 0, 0, 0)),
        ],
        out_specs=band,
        compiler_params=params(),
        name="make_output",
    )(tokens, gain, mixed)


def gradient_kernel(sizes, cot_ref, back_ref, out_ref):
    batch, rows, parts, chunk = sizes
    for b in range(batch):
        for q in range(parts):
            for r in range(rows):
                cells = slice(q * chunk, (q + 1) * chunk)
                out_ref[b, r, cells, :] = (
                    cot_ref[b, r, cells, :].astype(F32)
                    + back_ref[b * parts + q, r].astype(F32)
                ).astype(BF16)


def make_gradient(cot, back, sizes):
    batch, rows, parts, chunk = sizes
    width = cot.shape[-1]
    band = pl.BlockSpec((batch, rows, parts * chunk, width // 4), lambda i: (0, 0, 0, i))
    return pl.pallas_call(
        functools.partial(gradient_kernel, sizes),
        out_shape=jax.ShapeDtypeStruct(cot.shape, BF16),
        grid=(4,),
        in_specs=[
            band,
            pl.BlockSpec((batch * parts, rows, chunk, width // 4), lambda i: (0, 0, 0, i)),
        ],
        out_specs=band,
        compiler_params=params(),
        name="make_gradient",
    )(cot, back)


def forward_kernel(
    samples, lat_count, chunk, head_width, levels,
    tok_ref, mask_ref, wq_ref, wk_ref, wv_ref, wm_ref,
    qn_ref, kn_ref, v_ref, rq_ref, rk_ref, p_ref, att_ref, part_ref,
    normed_ref, acc_ref, keep_ref,
):
    step = pl.program_id(0)
    count, width = tok_ref.shape

    @pl.when(step == 0)
    def _():
        x = tok_ref[...].astype(F32)
        rx = lax.rsqrt(jnp.mean(x * x, axis=-1, keepdims=True) + epsilon)
        normed_ref[...] = (x * rx).astype(BF16)
        acc_ref[...] = jnp.zeros_like(acc_ref)
        spread = (
            lax.broadcasted_iota(jnp.int32, (lat_count, count), 0)
            == lax.broadcasted_iota(jnp.int32, (lat_count, count), 1) // chunk
        ).astype(F32)
        per_sample = nn(mask_ref[...].astype(F32), spread)
        parts = lax.axis_size("lat") // samples
        mine = lax.axis_index("lat") // parts
        pick = lax.broadcasted_iota(jnp.int32, (samples, count), 0) == mine
        valid = jnp.sum(jnp.where(pick, per_sample, 0.0), axis=0, keepdims=True)
        same = (
            lax.broadcasted_iota(jnp.int32, (count, count), 0) % chunk
            == lax.broadcasted_iota(jnp.int32, (count, count), 1) % chunk
        )
        keep_ref[...] = jnp.where(same, valid, 0.0)

    normed = normed_ref[...]
    mean_mat = block_mean(head_width)
    q = nn(normed, wq_ref[...])
    k = nn(normed, wk_ref[...])
    v = nn(normed, wv_ref[...]).astype(BF16)
    rq = lax.rsqrt(nn((q * q).astype(BF16), mean_mat) + epsilon)
    rk = lax.rsqrt(nn((k * k).astype(BF16), mean_mat) + epsilon)
    qn = (q * rq).astype(BF16)
    kn = (k * rk).astype(BF16)
    qn_ref[...] = qn
    kn_ref[...] = kn
    v_ref[...] = v
    rq_ref[...] = rq
    rk_ref[...] = rk
    keep = keep_ref[...]
    lane = lax.broadcasted_iota(jnp.int32, (count, 128), 1) // head_width
    per_tile = 128 // head_width
    tiles = []
    for t in range(GROUP // 128):
        cols = slice(t * 128, (t + 1) * 128)
        q_t, k_t, v_t = qn[:, cols], kn[:, cols], v[:, cols]
        total = None
        for h in range(per_tile):
            q_h = jnp.where(lane == h, q_t * score_scale, jnp.zeros_like(q_t))
            e = jnp.exp(nt(q_h, k_t)) * keep
            p = (e * (1.0 / jnp.sum(e, axis=-1, keepdims=True))).astype(BF16)
            p_ref[t * per_tile + h] = p
            o = nn(p, v_t)
            total = o if total is None else jnp.where(lane == h, o, total)
        tiles.append(total)
    att = jnp.concatenate(tiles, axis=1).astype(BF16)
    att_ref[...] = att
    acc_ref[...] += nn(att, wm_ref[...])

    @pl.when(step == pl.num_programs(0) - 1)
    def _():
        share = width // levels
        for l in range(levels):
            part_ref[l] = acc_ref[:, l * share : (l + 1) * share].astype(BF16)


def forward(tok_col, key_mask, w_qkv, w_mix, chunk, levels):
    count, width = tok_col.shape
    samples, lat_count = key_mask.shape
    head_width = width // HEADS
    steps = width // GROUP
    per_step = GROUP // head_width
    share = width // levels
    whole = pl.BlockSpec((count, width), lambda i: (0, 0))
    cols = pl.BlockSpec((count, GROUP), lambda i: (0, i))
    weight = lambda which: pl.BlockSpec((width, GROUP), lambda i: (0, i + which * steps))
    return pl.pallas_call(
        functools.partial(forward_kernel, samples, lat_count, chunk, head_width, levels),
        out_shape=(
            jax.ShapeDtypeStruct((count, width), BF16),
            jax.ShapeDtypeStruct((count, width), BF16),
            jax.ShapeDtypeStruct((count, width), BF16),
            jax.ShapeDtypeStruct((count, width), F32),
            jax.ShapeDtypeStruct((count, width), F32),
            jax.ShapeDtypeStruct((HEADS, count, count), BF16),
            jax.ShapeDtypeStruct((count, width), BF16),
            jax.ShapeDtypeStruct((levels, count, share), BF16),
        ),
        grid=(steps,),
        in_specs=[
            whole,
            pl.BlockSpec((samples, lat_count), lambda i: (0, 0)),
            weight(0),
            weight(1),
            weight(2),
            pl.BlockSpec((GROUP, width), lambda i: (i, 0)),
        ],
        out_specs=(
            cols,
            cols,
            cols,
            cols,
            cols,
            pl.BlockSpec((per_step, count, count), lambda i: (i, 0, 0)),
            cols,
            pl.BlockSpec((levels, count, share), lambda i: (0, 0, 0)),
        ),
        scratch_shapes=[
            pltpu.VMEM((count, width), BF16),
            pltpu.VMEM((count, width), F32),
            pltpu.VMEM((count, count), F32),
        ],
        compiler_params=params(),
        cost_estimate=pl.CostEstimate(
            flops=2 * count * width * (4 * width + 2 * count * 4),
            bytes_accessed=20 * count * width + 8 * width * width,
            transcendentals=HEADS * count * count,
        ),
        name="forward",
    )(tok_col, key_mask, w_qkv, w_qkv, w_qkv, w_mix)


def backward_kernel(
    head_width, levels,
    tok_ref, flow_ref, wm_ref, wq_ref, wk_ref, wv_ref,
    qn_ref, kn_ref, v_ref, rq_ref, rk_ref, p_ref,
    out_ref, acc_ref,
):
    step = pl.program_id(0)
    count, width = tok_ref.shape
    share = width // levels
    d_att = None
    for l in range(levels):
        term = nt(flow_ref[l], wm_ref[:, l * share : (l + 1) * share])
        d_att = term if d_att is None else d_att + term
    d_att = d_att.astype(BF16)
    qn, kn, v = qn_ref[...], kn_ref[...], v_ref[...]
    lane = lax.broadcasted_iota(jnp.int32, (count, 128), 1) // head_width
    per_tile = 128 // head_width
    dq_tiles, dk_tiles, dv_tiles = [], [], []
    for t in range(GROUP // 128):
        cols = slice(t * 128, (t + 1) * 128)
        q_t, k_t, v_t, d_t = qn[:, cols], kn[:, cols], v[:, cols], d_att[:, cols]
        dq = dk = dv = None
        for h in range(per_tile):
            d_h = jnp.where(lane == h, d_t, jnp.zeros_like(d_t))
            d_p = nt(d_h, v_t)
            p_b = p_ref[t * per_tile + h]
            p = p_b.astype(F32)
            pd = p * d_p
            d_s = ((pd - p * jnp.sum(pd, axis=-1, keepdims=True)) * score_scale).astype(BF16)
            dq_h, dk_h, dv_h = nn(d_s, k_t), tn(d_s, q_t), tn(p_b, d_t)
            if dq is None:
                dq, dk, dv = dq_h, dk_h, dv_h
            else:
                dq = jnp.where(lane == h, dq_h, dq)
                dk = jnp.where(lane == h, dk_h, dk)
                dv = jnp.where(lane == h, dv_h, dv)
        dq_tiles.append(dq)
        dk_tiles.append(dk)
        dv_tiles.append(dv)
    mean_mat = block_mean(head_width)
    dq = jnp.concatenate(dq_tiles, axis=1)
    dk = jnp.concatenate(dk_tiles, axis=1)
    dv = jnp.concatenate(dv_tiles, axis=1).astype(BF16)

    def through_norm(upstream, unit, factor):
        unit = unit.astype(F32)
        inner = nn((upstream * unit).astype(BF16), mean_mat)
        return (factor * (upstream - unit * inner)).astype(BF16)

    gq = through_norm(dq, qn, rq_ref[...])
    gk = through_norm(dk, kn, rk_ref[...])
    total = nt(gq, wq_ref[...]) + nt(gk, wk_ref[...]) + nt(dv, wv_ref[...])

    @pl.when(step == 0)
    def _():
        acc_ref[...] = total

    @pl.when(step > 0)
    def _():
        acc_ref[...] += total

    @pl.when(step == pl.num_programs(0) - 1)
    def _():
        x = tok_ref[...].astype(F32)
        rx = lax.rsqrt(jnp.mean(x * x, axis=-1, keepdims=True) + epsilon)
        d = acc_ref[...]
        inner = jnp.mean(d * x, axis=-1, keepdims=True)
        out_ref[...] = (rx * d - x * (rx * rx * rx * inner)).astype(BF16)


def backward(tok_col, flow, w_mix, w_qkv, saved, levels):
    count, width = tok_col.shape
    head_width = width // HEADS
    steps = width // GROUP
    per_step = GROUP // head_width
    share = width // levels
    whole = pl.BlockSpec((count, width), lambda i: (0, 0))
    cols = pl.BlockSpec((count, GROUP), lambda i: (0, i))
    weight = lambda which: pl.BlockSpec((width, GROUP), lambda i: (0, i + which * steps))
    return pl.pallas_call(
        functools.partial(backward_kernel, head_width, levels),
        out_shape=jax.ShapeDtypeStruct((count, width), BF16),
        grid=(steps,),
        in_specs=[
            whole,
            pl.BlockSpec((levels, count, share), lambda i: (0, 0, 0)),
            pl.BlockSpec((GROUP, width), lambda i: (i, 0)),
            weight(0),
            weight(1),
            weight(2),
            cols,
            cols,
            cols,
            cols,
            cols,
            pl.BlockSpec((per_step, count, count), lambda i: (i, 0, 0)),
        ],
        out_specs=whole,
        scratch_shapes=[pltpu.VMEM((count, width), F32)],
        compiler_params=params(),
        cost_estimate=pl.CostEstimate(
            flops=2 * count * width * (4 * width + 4 * count * 4),
            bytes_accessed=20 * count * width + 8 * width * width,
            transcendentals=0,
        ),
        name="backward",
    )(tok_col, flow, w_mix, w_qkv, w_qkv, w_qkv, *saved)


def mix_gradient_kernel(levels, factor, att_ref, flow_ref, out_ref):
    share = out_ref.shape[1] // levels
    att = att_ref[...]
    for l in range(levels):
        out_ref[:, l * share : (l + 1) * share] = (tn(att, flow_ref[l]) * factor).astype(BF16)


def mix_gradient(attended, flow, factor, levels):
    count, width = attended.shape
    return pl.pallas_call(
        functools.partial(mix_gradient_kernel, levels, factor),
        out_shape=jax.ShapeDtypeStruct((width, width), BF16),
        grid=(width // GROUP,),
        in_specs=[
            pl.BlockSpec((count, GROUP), lambda i: (0, i)),
            pl.BlockSpec((levels, count, width // levels), lambda i: (0, 0, 0)),
        ],
        out_specs=pl.BlockSpec((GROUP, width), lambda i: (i, 0)),
        compiler_params=params(),
        cost_estimate=pl.CostEstimate(
            flops=2 * count * width * width,
            bytes_accessed=4 * count * width + 2 * width * width,
            transcendentals=0,
        ),
        name="mix_gradient",
    )(attended, flow)


def swap(block, axis):
    return lax.all_to_all(block, axis, split_axis=0, concat_axis=0, tiled=True)


def level_sum(received):
    return jnp.sum(received.astype(F32), axis=0).astype(BF16)


def on_device(tokens, key_mask, w_qkv, w_mix, level_scale, cotangent):
    batch, _, rows, lon, width = tokens.shape
    owners = lax.axis_size("lat")
    levels = lax.axis_size("lev")
    parts = owners // batch
    chunk = lon // parts
    sizes = (batch, rows, parts, chunk)
    share = width // levels
    count = batch * rows * lon
    tok_band = tokens.reshape(batch, rows, lon, width)
    cot_band = cotangent.reshape(batch, rows, lon, width)
    w_mix = w_mix.reshape(width, width)

    tok_col = swap(pack_tokens(tok_band, sizes), "lat").reshape(count, width)
    cot_parts = swap(pack_cotangent(cot_band, level_scale, sizes, levels), "lev")
    flow_share = level_sum(cot_parts)
    flow_share_col = swap(flow_share, "lat").reshape(count, share)
    flow = lax.all_gather(flow_share_col, "lev", axis=0)

    *saved, attended, partial = forward(tok_col, key_mask, w_qkv, w_mix, chunk, levels)
    mix_share = level_sum(swap(partial, "lev"))
    mix_share_band = swap(mix_share.reshape(owners, rows, chunk, share), "lat")
    mixed = lax.all_gather(mix_share_band, "lev", axis=0)
    output = make_output(tok_band, level_scale, mixed, sizes, levels)

    factor = 1.0 / math.sqrt(count * owners)
    mix_term = mix_gradient(attended, flow, factor, levels)
    mix_grad = lax.psum_scatter(mix_term, "lat", scatter_dimension=0, tiled=True).astype(F32)

    back_col = backward(tok_col, flow, w_mix, w_qkv, saved, levels)
    back = swap(back_col.reshape(owners, rows, chunk, width), "lat")
    d_tokens = make_gradient(cot_band, back, sizes)
    return (
        output.reshape(tokens.shape),
        d_tokens.reshape(tokens.shape),
        mix_grad.reshape(1, width // owners, width),
    )


def solution(mesh):
    return jax.shard_map(
        on_device,
        mesh=mesh,
        in_specs=(
            P(None, "lev", "lat", None, None),
            P(),
            P(),
            P("lev", None, None),
            P("lev", None),
            P(None, "lev", "lat", None, None),
        ),
        out_specs=(
            P(None, "lev", "lat", None, None),
            P(None, "lev", "lat", None, None),
            P("lev", "lat", None),
        ),
        check_vma=False,
    )
```

```python
import functools
import math

import jax
import jax.numpy as jnp
from jax import lax
from jax.experimental import pallas as pl
from jax.experimental.pallas import tpu as pltpu
from jax.sharding import PartitionSpec as P

HEADS = 16
GROUP = 256

epsilon = 1e-06
score_scale = 0.25

F32 = jnp.float32
BF16 = jnp.bfloat16


def nn(a, b):
    return lax.dot_general(a, b, (((1,), (0,)), ((), ())), preferred_element_type=F32)


def nt(a, b):
    return lax.dot_general(a, b, (((1,), (1,)), ((), ())), preferred_element_type=F32)


def tn(a, b):
    return lax.dot_general(a, b, (((0,), (0,)), ((), ())), preferred_element_type=F32)


def block_mean(head_width):
    row = lax.broadcasted_iota(jnp.int32, (GROUP, GROUP), 0) // head_width
    col = lax.broadcasted_iota(jnp.int32, (GROUP, GROUP), 1) // head_width
    return jnp.where(row == col, 1.0 / head_width, 0.0).astype(BF16)


def params():
    return pltpu.CompilerParams(vmem_limit_bytes=44 * 1024 * 1024)


def pack_kernel(sizes, levels, tok_ref, cot_ref, gain_ref, tok_out, *cot_outs):
    batch, rows, parts, chunk = sizes
    share = tok_ref.shape[-1] // levels
    mine = lax.axis_index("lev")
    for b in range(batch):
        for q in range(parts):
            for r in range(rows):
                tok_out[b * parts + q, r] = tok_ref[b, r, q * chunk : (q + 1) * chunk, :]
    for s in range(levels):
        cols = pl.ds(pl.multiple_of((mine ^ s) * share, share), share)
        gain = gain_ref[:, cols]
        for b in range(batch):
            for q in range(parts):
                for r in range(rows):
                    piece = cot_ref[b, r, q * chunk : (q + 1) * chunk, cols].astype(F32)
                    cot_outs[s][b * parts + q, r] = (piece * gain).astype(BF16)


def pack(tokens, cot, gain, sizes, levels):
    batch, rows, parts, chunk = sizes
    width = tokens.shape[-1]
    part = jax.ShapeDtypeStruct((batch * parts, rows, chunk, width // levels), BF16)
    tok_out, *cot_outs = pl.pallas_call(
        functools.partial(pack_kernel, sizes, levels),
        out_shape=(
            jax.ShapeDtypeStruct((batch * parts, rows, chunk, width), BF16),
            *([part] * levels),
        ),
        compiler_params=params(),
        name="pack",
    )(tokens, cot, gain)
    return tok_out, cot_outs


def output_kernel(sizes, levels, tok_ref, gain_ref, *refs):
    batch, rows, parts, chunk = sizes
    out_ref = refs[-1]
    share = tok_ref.shape[-1] // levels
    mine = lax.axis_index("lev")
    for s in range(levels):
        cols = pl.ds(pl.multiple_of((mine ^ s) * share, share), share)
        gain = gain_ref[:, cols]
        for b in range(batch):
            for q in range(parts):
                for r in range(rows):
                    cells = slice(q * chunk, (q + 1) * chunk)
                    mixed = refs[s][b * parts + q, r].astype(F32)
                    out_ref[b, r, cells, cols] = (
                        tok_ref[b, r, cells, cols].astype(F32) + gain * mixed
                    ).astype(BF16)


def make_output(tokens, gain, mixed, sizes, levels):
    return pl.pallas_call(
        functools.partial(output_kernel, sizes, levels),
        out_shape=jax.ShapeDtypeStruct(tokens.shape, BF16),
        compiler_params=params(),
        name="make_output",
    )(tokens, gain, *mixed)


def gradient_kernel(sizes, cot_ref, back_ref, out_ref):
    batch, rows, parts, chunk = sizes
    for b in range(batch):
        for q in range(parts):
            for r in range(rows):
                cells = slice(q * chunk, (q + 1) * chunk)
                out_ref[b, r, cells, :] = (
                    cot_ref[b, r, cells, :].astype(F32)
                    + back_ref[b * parts + q, r].astype(F32)
                ).astype(BF16)


def make_gradient(cot, back, sizes):
    batch, rows, parts, chunk = sizes
    width = cot.shape[-1]
    band = pl.BlockSpec((batch, rows, parts * chunk, width // 4), lambda i: (0, 0, 0, i))
    return pl.pallas_call(
        functools.partial(gradient_kernel, sizes),
        out_shape=jax.ShapeDtypeStruct(cot.shape, BF16),
        grid=(4,),
        in_specs=[
            band,
            pl.BlockSpec((batch * parts, rows, chunk, width // 4), lambda i: (0, 0, 0, i)),
        ],
        out_specs=band,
        compiler_params=params(),
        name="make_gradient",
    )(cot, back)


def forward_kernel(
    samples, lat_count, chunk, head_width, levels,
    tok_ref, mask_ref, wq_ref, wk_ref, wv_ref, wm_ref,
    qn_ref, kn_ref, v_ref, rq_ref, rk_ref, p_ref, att_ref, *rest,
):
    part_refs = rest[:levels]
    normed_ref, acc_ref, keep_ref = rest[levels:]
    step = pl.program_id(0)
    count, width = tok_ref.shape

    @pl.when(step == 0)
    def _():
        x = tok_ref[...].astype(F32)
        rx = lax.rsqrt(jnp.mean(x * x, axis=-1, keepdims=True) + epsilon)
        normed_ref[...] = (x * rx).astype(BF16)
        acc_ref[...] = jnp.zeros_like(acc_ref)
        spread = (
            lax.broadcasted_iota(jnp.int32, (lat_count, count), 0)
            == lax.broadcasted_iota(jnp.int32, (lat_count, count), 1) // chunk
        ).astype(F32)
        per_sample = nn(mask_ref[...].astype(F32), spread)
        parts = lax.axis_size("lat") // samples
        mine = lax.axis_index("lat") // parts
        pick = lax.broadcasted_iota(jnp.int32, (samples, count), 0) == mine
        valid = jnp.sum(jnp.where(pick, per_sample, 0.0), axis=0, keepdims=True)
        same = (
            lax.broadcasted_iota(jnp.int32, (count, count), 0) % chunk
            == lax.broadcasted_iota(jnp.int32, (count, count), 1) % chunk
        )
        keep_ref[...] = jnp.where(same, valid, 0.0)

    normed = normed_ref[...]
    mean_mat = block_mean(head_width)
    q = nn(normed, wq_ref[...])
    k = nn(normed, wk_ref[...])
    v = nn(normed, wv_ref[...]).astype(BF16)
    rq = lax.rsqrt(nn((q * q).astype(BF16), mean_mat) + epsilon)
    rk = lax.rsqrt(nn((k * k).astype(BF16), mean_mat) + epsilon)
    qn = (q * rq).astype(BF16)
    kn = (k * rk).astype(BF16)
    qn_ref[...] = qn
    kn_ref[...] = kn
    v_ref[...] = v
    rq_ref[...] = rq
    rk_ref[...] = rk
    keep = keep_ref[...]
    lane = lax.broadcasted_iota(jnp.int32, (count, 128), 1) // head_width
    per_tile = 128 // head_width
    tiles = []
    for t in range(GROUP // 128):
        cols = slice(t * 128, (t + 1) * 128)
        q_t, k_t, v_t = qn[:, cols], kn[:, cols], v[:, cols]
        total = None
        for h in range(per_tile):
            q_h = jnp.where(lane == h, q_t * score_scale, jnp.zeros_like(q_t))
            e = jnp.exp(nt(q_h, k_t)) * keep
            p = (e * (1.0 / jnp.sum(e, axis=-1, keepdims=True))).astype(BF16)
            p_ref[t * per_tile + h] = p
            o = nn(p, v_t)
            total = o if total is None else jnp.where(lane == h, o, total)
        tiles.append(total)
    att = jnp.concatenate(tiles, axis=1).astype(BF16)
    features = att_ref.shape[-1]
    for f in range(GROUP // features):
        att_ref[f] = att[:, f * features : (f + 1) * features]
    acc_ref[...] += nn(att, wm_ref[...])

    @pl.when(step == pl.num_programs(0) - 1)
    def _():
        share = width // levels
        level = lax.axis_index("lev")
        for s in range(levels):
            cols = pl.ds(pl.multiple_of((level ^ s) * share, share), share)
            part_refs[s][...] = acc_ref[:, cols].astype(BF16)


def forward(tok_col, key_mask, w_qkv, w_mix, chunk, owners, levels):
    count, width = tok_col.shape
    samples, lat_count = key_mask.shape
    head_width = width // HEADS
    steps = width // GROUP
    per_step = GROUP // head_width
    share = width // levels
    features = width // owners
    whole = pl.BlockSpec((count, width), lambda i: (0, 0))
    cols = pl.BlockSpec((count, GROUP), lambda i: (0, i))
    weight = lambda which: pl.BlockSpec((width, GROUP), lambda i: (0, i + which * steps))
    return pl.pallas_call(
        functools.partial(forward_kernel, samples, lat_count, chunk, head_width, levels),
        out_shape=(
            jax.ShapeDtypeStruct((count, width), BF16),
            jax.ShapeDtypeStruct((count, width), BF16),
            jax.ShapeDtypeStruct((count, width), BF16),
            jax.ShapeDtypeStruct((count, width), F32),
            jax.ShapeDtypeStruct((count, width), F32),
            jax.ShapeDtypeStruct((HEADS, count, count), BF16),
            jax.ShapeDtypeStruct((owners, count, features), BF16),
            *([jax.ShapeDtypeStruct((count, share), BF16)] * levels),
        ),
        grid=(steps,),
        in_specs=[
            whole,
            pl.BlockSpec((samples, lat_count), lambda i: (0, 0)),
            weight(0),
            weight(1),
            weight(2),
            pl.BlockSpec((GROUP, width), lambda i: (i, 0)),
        ],
        out_specs=(
            cols,
            cols,
            cols,
            cols,
            cols,
            pl.BlockSpec((per_step, count, count), lambda i: (i, 0, 0)),
            pl.BlockSpec((GROUP // features, count, features), lambda i: (i, 0, 0)),
            *([pl.BlockSpec((count, share), lambda i: (0, 0))] * levels),
        ),
        scratch_shapes=[
            pltpu.VMEM((count, width), BF16),
            pltpu.VMEM((count, width), F32),
            pltpu.VMEM((count, count), F32),
        ],
        compiler_params=params(),
        cost_estimate=pl.CostEstimate(
            flops=2 * count * width * (4 * width + 2 * count * 4),
            bytes_accessed=20 * count * width + 8 * width * width,
            transcendentals=HEADS * count * count,
        ),
        name="forward",
    )(tok_col, key_mask, w_qkv, w_qkv, w_qkv, w_mix)


def backward_kernel(
    head_width, levels, mine_ref,
    tok_ref, flow_ref, wm_ref, wq_ref, wk_ref, wv_ref,
    qn_ref, kn_ref, v_ref, rq_ref, rk_ref, p_ref,
    out_ref, acc_ref,
):
    step = pl.program_id(0)
    count, width = tok_ref.shape
    share = width // levels
    d_att = None
    for l in range(levels):
        flow = flow_ref[:, l].reshape(count, share)
        term = nt(flow, wm_ref[:, l * share : (l + 1) * share])
        d_att = term if d_att is None else d_att + term
    d_att = d_att.astype(BF16)
    qn, kn, v = qn_ref[...], kn_ref[...], v_ref[...]
    lane = lax.broadcasted_iota(jnp.int32, (count, 128), 1) // head_width
    per_tile = 128 // head_width
    dq_tiles, dk_tiles, dv_tiles = [], [], []
    for t in range(GROUP // 128):
        cols = slice(t * 128, (t + 1) * 128)
        q_t, k_t, v_t, d_t = qn[:, cols], kn[:, cols], v[:, cols], d_att[:, cols]
        dq = dk = dv = None
        for h in range(per_tile):
            d_h = jnp.where(lane == h, d_t, jnp.zeros_like(d_t))
            d_p = nt(d_h, v_t)
            p_b = p_ref[t * per_tile + h]
            p = p_b.astype(F32)
            pd = p * d_p
            d_s = ((pd - p * jnp.sum(pd, axis=-1, keepdims=True)) * score_scale).astype(BF16)
            dq_h, dk_h, dv_h = nn(d_s, k_t), tn(d_s, q_t), tn(p_b, d_t)
            if dq is None:
                dq, dk, dv = dq_h, dk_h, dv_h
            else:
                dq = jnp.where(lane == h, dq_h, dq)
                dk = jnp.where(lane == h, dk_h, dk)
                dv = jnp.where(lane == h, dv_h, dv)
        dq_tiles.append(dq)
        dk_tiles.append(dk)
        dv_tiles.append(dv)
    mean_mat = block_mean(head_width)
    dq = jnp.concatenate(dq_tiles, axis=1)
    dk = jnp.concatenate(dk_tiles, axis=1)
    dv = jnp.concatenate(dv_tiles, axis=1).astype(BF16)

    def through_norm(upstream, unit, factor):
        unit = unit.astype(F32)
        inner = nn((upstream * unit).astype(BF16), mean_mat)
        return (factor * (upstream - unit * inner)).astype(BF16)

    gq = through_norm(dq, qn, rq_ref[...])
    gk = through_norm(dk, kn, rk_ref[...])
    total = nt(gq, wq_ref[...]) + nt(gk, wk_ref[...]) + nt(dv, wv_ref[...])

    @pl.when(step == 0)
    def _():
        acc_ref[...] = total

    @pl.when(step > 0)
    def _():
        acc_ref[...] += total

    @pl.when(step == pl.num_programs(0) - 1)
    def _():
        x = tok_ref[...].astype(F32)
        rx = lax.rsqrt(jnp.mean(x * x, axis=-1, keepdims=True) + epsilon)
        d = acc_ref[...]
        inner = jnp.mean(d * x, axis=-1, keepdims=True)
        out_ref[...] = (rx * d - x * (rx * rx * rx * inner)).astype(BF16)


def backward(tok_col, flow_all, w_mix, w_qkv, saved, levels):
    count, width = tok_col.shape
    head_width = width // HEADS
    steps = width // GROUP
    per_step = GROUP // head_width
    owners, _, _, rows, chunk, share = flow_all.shape
    whole = pl.BlockSpec((count, width), lambda i, m: (0, 0))
    cols = pl.BlockSpec((count, GROUP), lambda i, m: (0, i))
    weight = lambda which: pl.BlockSpec((width, GROUP), lambda i, m: (0, i + which * steps))
    mine = lax.axis_index("lat").astype(jnp.int32).reshape(1)
    return pl.pallas_call(
        functools.partial(backward_kernel, head_width, levels),
        out_shape=jax.ShapeDtypeStruct((count, width), BF16),
        grid_spec=pltpu.PrefetchScalarGridSpec(
            num_scalar_prefetch=1,
            grid=(steps,),
            in_specs=[
                whole,
                pl.BlockSpec(
                    (owners, levels, None, rows, chunk, share),
                    lambda i, m: (0, 0, m[0], 0, 0, 0),
                ),
                pl.BlockSpec((GROUP, width), lambda i, m: (i, 0)),
                weight(0),
                weight(1),
                weight(2),
                cols,
                cols,
                cols,
                cols,
                cols,
                pl.BlockSpec((per_step, count, count), lambda i, m: (i, 0, 0)),
            ],
            out_specs=whole,
            scratch_shapes=[pltpu.VMEM((count, width), F32)],
        ),
        compiler_params=params(),
        cost_estimate=pl.CostEstimate(
            flops=2 * count * width * (4 * width + 4 * count * 4),
            bytes_accessed=20 * count * width + 8 * width * width,
            transcendentals=0,
        ),
        name="backward",
    )(mine, tok_col, flow_all, w_mix, w_qkv, w_qkv, w_qkv, *saved)


def mix_gradient_kernel(levels, factor, att_ref, flow_ref, out_ref):
    step = pl.program_id(0)
    owners, cells, features = att_ref.shape
    share = out_ref.shape[1] // levels
    att = att_ref[...].reshape(owners * cells, features)
    for l in range(levels):
        cols = slice(l * share, (l + 1) * share)
        term = tn(att, flow_ref[l].reshape(owners * cells, share)) * factor

        @pl.when(step == 0)
        def _():
            out_ref[:, cols] = term

        @pl.when(step > 0)
        def _():
            out_ref[:, cols] += term


def mix_gradient(attended, flow_all, factor):
    owners, levels, _, rows, chunk, share = flow_all.shape
    _, count, features = attended.shape
    width = levels * share
    return pl.pallas_call(
        functools.partial(mix_gradient_kernel, levels, factor),
        out_shape=jax.ShapeDtypeStruct((features, width), F32),
        grid=(owners,),
        in_specs=[
            pl.BlockSpec((owners, rows * chunk, features), lambda i: (0, i, 0)),
            pl.BlockSpec((None, levels, owners, rows, chunk, share), lambda i: (i, 0, 0, 0, 0, 0)),
        ],
        out_specs=pl.BlockSpec((features, width), lambda i: (0, 0)),
        compiler_params=params(),
        cost_estimate=pl.CostEstimate(
            flops=2 * count * width * width,
            bytes_accessed=2 * owners * count * width,
            transcendentals=0,
        ),
        name="mix_gradient",
    )(attended, flow_all)


def swap(block, axis):
    return lax.all_to_all(block, axis, split_axis=0, concat_axis=0, tiled=True)


def from_level(block, offset, levels):
    return lax.ppermute(block, "lev", [(i, i ^ offset) for i in range(levels)])


def level_sum(parts):
    levels = len(parts)
    total = parts[0].astype(F32)
    for s in range(1, levels):
        total += from_level(parts[s], s, levels).astype(F32)
    return total.astype(BF16)


def level_gather(block, levels):
    return [block] + [from_level(block, s, levels) for s in range(1, levels)]


def on_device(tokens, key_mask, w_qkv, w_mix, level_scale, cotangent):
    batch, _, rows, lon, width = tokens.shape
    owners = lax.axis_size("lat")
    levels = lax.axis_size("lev")
    parts = owners // batch
    chunk = lon // parts
    sizes = (batch, rows, parts, chunk)
    share = width // levels
    count = batch * rows * lon
    tok_band = tokens.reshape(batch, rows, lon, width)
    cot_band = cotangent.reshape(batch, rows, lon, width)
    w_mix = w_mix.reshape(width, width)

    tok_send, cot_parts = pack(tok_band, cot_band, level_scale, sizes, levels)
    tok_col = swap(tok_send, "lat").reshape(count, width)
    flow_share = level_sum(cot_parts)
    flow_all = lax.all_gather(flow_share, ("lat", "lev"), axis=0)
    flow_all = flow_all.reshape(owners, levels, owners, rows, chunk, share)

    results = forward(tok_col, key_mask, w_qkv, w_mix, chunk, owners, levels)
    saved, attended, partial = results[:6], results[6], results[7:]
    attended_all = swap(attended, "lat")
    mix_share = level_sum(partial)
    mix_share_band = swap(mix_share.reshape(owners, rows, chunk, share), "lat")
    mixed = level_gather(mix_share_band, levels)
    output = make_output(tok_band, level_scale, mixed, sizes, levels)

    back_col = backward(tok_col, flow_all, w_mix, w_qkv, saved, levels)
    back = swap(back_col.reshape(owners, rows, chunk, width), "lat")
    d_tokens = make_gradient(cot_band, back, sizes)
    factor = 1.0 / math.sqrt(count * owners)
    mix_grad = mix_gradient(attended_all, flow_all, factor)
    return (
        output.reshape(tokens.shape),
        d_tokens.reshape(tokens.shape),
        mix_grad.reshape(1, width // owners, width),
    )


def solution(mesh):
    return jax.shard_map(
        on_device,
        mesh=mesh,
        in_specs=(
            P(None, "lev", "lat", None, None),
            P(),
            P(),
            P("lev", None, None),
            P("lev", None),
            P(None, "lev", "lat", None, None),
        ),
        out_specs=(
            P(None, "lev", "lat", None, None),
            P(None, "lev", "lat", None, None),
            P("lev", "lat", None),
        ),
        check_vma=False,
    )
```

```python
import functools
import math

import jax
import jax.numpy as jnp
from jax import lax
from jax.experimental import pallas as pl
from jax.experimental.pallas import tpu as pltpu
from jax.sharding import PartitionSpec as P

HEADS = 16
GROUP = 256

epsilon = 1e-06
score_scale = 0.25

F32 = jnp.float32
BF16 = jnp.bfloat16


def nn(a, b):
    return lax.dot_general(a, b, (((1,), (0,)), ((), ())), preferred_element_type=F32)


def nt(a, b):
    return lax.dot_general(a, b, (((1,), (1,)), ((), ())), preferred_element_type=F32)


def tn(a, b):
    return lax.dot_general(a, b, (((0,), (0,)), ((), ())), preferred_element_type=F32)


def block_mean(head_width):
    row = lax.broadcasted_iota(jnp.int32, (GROUP, GROUP), 0) // head_width
    col = lax.broadcasted_iota(jnp.int32, (GROUP, GROUP), 1) // head_width
    return jnp.where(row == col, 1.0 / head_width, 0.0).astype(BF16)


def params():
    return pltpu.CompilerParams(vmem_limit_bytes=36 * 1024 * 1024)


def level_cols(s, share):
    return pl.ds(pl.multiple_of((lax.axis_index("lev") ^ s) * share, share), share)


def owner_cell(s, parts):
    owner = lax.axis_index("lat") ^ s
    return owner // parts, owner % parts


def call(kernel, name, out_shape, *operands):
    return pl.pallas_call(
        kernel, out_shape=out_shape, compiler_params=params(), name=name
    )(*operands)


def pack_kernel(owners, levels, tok_ref, cot_ref, gain_ref, *outs):
    batch, rows, parts, chunk, width = tok_ref.shape
    share = width // levels
    for t in range(owners):
        b, q = owner_cell(t, parts)
        for r in range(rows):
            outs[t][r * chunk : (r + 1) * chunk, :] = tok_ref[b, r, q]
    for s in range(levels):
        cols = level_cols(s, share)
        gain = gain_ref[:, cols]
        for t in range(owners):
            b, q = owner_cell(t, parts)
            for r in range(rows):
                at = (t * rows + r) * chunk
                piece = cot_ref[b, r, q, :, cols].astype(F32)
                outs[owners + s][at : at + chunk, :] = (piece * gain).astype(BF16)


def pack(tokens, cot, gain, owners, levels):
    batch, rows, parts, chunk, width = tokens.shape
    cells = rows * chunk
    outs = call(
        functools.partial(pack_kernel, owners, levels),
        "pack",
        [jax.ShapeDtypeStruct((cells, width), BF16)] * owners
        + [jax.ShapeDtypeStruct((owners * cells, width // levels), BF16)] * levels,
        tokens,
        cot,
        gain,
    )
    return outs[:owners], outs[owners:]


def output_kernel(owners, levels, tok_ref, gain_ref, *refs):
    batch, rows, parts, chunk, width = tok_ref.shape
    out_ref = refs[-1]
    for s in range(levels):
        cols = level_cols(s, width // levels)
        gain = gain_ref[:, cols]
        for t in range(owners):
            b, q = owner_cell(t, parts)
            for r in range(rows):
                at = (t * rows + r) * chunk
                mixed = refs[s][at : at + chunk, :].astype(F32)
                out_ref[b, r, q, :, cols] = (
                    tok_ref[b, r, q, :, cols].astype(F32) + gain * mixed
                ).astype(BF16)


def make_output(tokens, gain, mixed, owners, levels):
    return call(
        functools.partial(output_kernel, owners, levels),
        "make_output",
        jax.ShapeDtypeStruct(tokens.shape, BF16),
        tokens,
        gain,
        *mixed,
    )


def gradient_kernel(owners, cot_ref, *refs):
    batch, rows, parts, chunk, width = cot_ref.shape
    out_ref = refs[-1]
    for t in range(owners):
        b, q = owner_cell(t, parts)
        for r in range(rows):
            back = refs[t][r * chunk : (r + 1) * chunk, :].astype(F32)
            out_ref[b, r, q] = (cot_ref[b, r, q].astype(F32) + back).astype(BF16)


def make_gradient(cot, back):
    return call(
        functools.partial(gradient_kernel, len(back)),
        "make_gradient",
        jax.ShapeDtypeStruct(cot.shape, BF16),
        cot,
        *back,
    )


def sum_kernel(levels, *refs):
    outs = refs[levels:]
    cells = outs[0].shape[0]
    for t, out in enumerate(outs):
        at = slice(t * cells, (t + 1) * cells)
        total = refs[0][at, :].astype(F32)
        for s in range(1, levels):
            total += refs[s][at, :].astype(F32)
        out[...] = total.astype(BF16)


def sum_levels(parts, owners):
    count, share = parts[0].shape
    return call(
        functools.partial(sum_kernel, len(parts)),
        "sum_levels",
        [jax.ShapeDtypeStruct((count // owners, share), BF16)] * owners,
        *parts,
    )


def join_kernel(*refs):
    cells = refs[0].shape[0]
    for t, ref in enumerate(refs[:-1]):
        refs[-1][t * cells : (t + 1) * cells, :] = ref[...]


def join(parts):
    cells, share = parts[0].shape
    return call(
        join_kernel, "join", jax.ShapeDtypeStruct((len(parts) * cells, share), BF16), *parts
    )


def flow_rows_kernel(levels, *refs):
    out_ref = refs[-1]
    count, width = out_ref.shape
    at = pl.ds(pl.multiple_of(lax.axis_index("lev") * count, count), count)
    for s in range(levels):
        out_ref[:, level_cols(s, width // levels)] = refs[s][at, :]


def flow_rows(flow):
    levels = len(flow)
    count, share = flow[0].shape
    return call(
        functools.partial(flow_rows_kernel, levels),
        "flow_rows",
        jax.ShapeDtypeStruct((count // levels, share * levels), BF16),
        *flow,
    )


def forward_kernel(
    samples, lat_count, chunk, owners, levels,
    mask_ref, wq_ref, wk_ref, wv_ref, wm_ref, *rest,
):
    tok_refs, rest = rest[:owners], rest[owners:]
    qn_ref, kn_ref, v_ref, rq_ref, rk_ref, p_ref = rest[:6]
    att_refs, rest = rest[6 : 6 + owners], rest[6 + owners :]
    part_refs, (normed_ref, acc_ref, keep_ref, att_scr) = rest[:levels], rest[levels:]
    step = pl.program_id(0)
    count, width = normed_ref.shape
    head_width = width // HEADS
    cells = count // owners

    @pl.when(step == 0)
    def _():
        for t in range(owners):
            x = tok_refs[t][...].astype(F32)
            rx = lax.rsqrt(jnp.mean(x * x, axis=-1, keepdims=True) + epsilon)
            normed_ref[t * cells : (t + 1) * cells, :] = (x * rx).astype(BF16)
        acc_ref[...] = jnp.zeros_like(acc_ref)
        me = lax.axis_index("lat")
        key = lax.broadcasted_iota(jnp.int32, (lat_count, count), 1)
        lat_of_key = (me ^ (key // cells)) * (cells // chunk) + key % cells // chunk
        spread = (lax.broadcasted_iota(jnp.int32, (lat_count, count), 0) == lat_of_key).astype(F32)
        per_sample = nn(mask_ref[...].astype(F32), spread)
        mine = me // (owners // samples)
        pick = lax.broadcasted_iota(jnp.int32, (samples, count), 0) == mine
        valid = jnp.sum(jnp.where(pick, per_sample, 0.0), axis=0, keepdims=True)
        same = (
            lax.broadcasted_iota(jnp.int32, (count, count), 0) % chunk
            == lax.broadcasted_iota(jnp.int32, (count, count), 1) % chunk
        )
        keep_ref[...] = jnp.where(same, valid, 0.0)

    normed = normed_ref[...]
    mean_mat = block_mean(head_width)
    q = nn(normed, wq_ref[...])
    k = nn(normed, wk_ref[...])
    v = nn(normed, wv_ref[...]).astype(BF16)
    rq = lax.rsqrt(nn((q * q).astype(BF16), mean_mat) + epsilon)
    rk = lax.rsqrt(nn((k * k).astype(BF16), mean_mat) + epsilon)
    qn = (q * rq).astype(BF16)
    kn = (k * rk).astype(BF16)
    qn_ref[...] = qn
    kn_ref[...] = kn
    v_ref[...] = v
    rq_ref[...] = rq
    rk_ref[...] = rk
    keep = keep_ref[...]
    lane = lax.broadcasted_iota(jnp.int32, (count, 128), 1) // head_width
    per_tile = 128 // head_width
    tiles = []
    for t in range(GROUP // 128):
        cols = slice(t * 128, (t + 1) * 128)
        q_t, k_t, v_t = qn[:, cols], kn[:, cols], v[:, cols]
        total = None
        for h in range(per_tile):
            q_h = jnp.where(lane == h, q_t * score_scale, jnp.zeros_like(q_t))
            e = jnp.exp(nt(q_h, k_t)) * keep
            p = (e * (1.0 / jnp.sum(e, axis=-1, keepdims=True))).astype(BF16)
            p_ref[t * per_tile + h] = p
            o = nn(p, v_t)
            total = o if total is None else jnp.where(lane == h, o, total)
        tiles.append(total)
    att = jnp.concatenate(tiles, axis=1).astype(BF16)
    features = width // owners
    per_group = GROUP // features
    for f in range(per_group):
        att_scr[step * per_group + f] = att[:, f * features : (f + 1) * features]
    acc_ref[...] += nn(att, wm_ref[...])

    @pl.when(step == pl.num_programs(0) - 1)
    def _():
        for s in range(levels):
            part_refs[s][...] = acc_ref[:, level_cols(s, width // levels)].astype(BF16)
        for t in range(owners):
            att_refs[t][...] = att_scr[lax.axis_index("lat") ^ t]


def forward(tok_col, key_mask, w_qkv, w_mix, chunk, levels):
    owners = len(tok_col)
    cells, width = tok_col[0].shape
    count = cells * owners
    samples, lat_count = key_mask.shape
    steps = width // GROUP
    per_step = GROUP // (width // HEADS)
    share = width // levels
    features = width // owners
    same = lambda shape: pl.BlockSpec(shape, lambda i: (0, 0))
    cols = pl.BlockSpec((count, GROUP), lambda i: (0, i))
    weight = lambda which: pl.BlockSpec((width, GROUP), lambda i: (0, i + which * steps))
    outs = pl.pallas_call(
        functools.partial(forward_kernel, samples, lat_count, chunk, owners, levels),
        out_shape=(
            [jax.ShapeDtypeStruct((count, width), BF16)] * 3
            + [jax.ShapeDtypeStruct((count, width), F32)] * 2
            + [jax.ShapeDtypeStruct((HEADS, count, count), BF16)]
            + [jax.ShapeDtypeStruct((count, features), BF16)] * owners
            + [jax.ShapeDtypeStruct((count, share), BF16)] * levels
        ),
        grid=(steps,),
        in_specs=[
            same((samples, lat_count)),
            weight(0),
            weight(1),
            weight(2),
            pl.BlockSpec((GROUP, width), lambda i: (i, 0)),
        ]
        + [same((cells, width))] * owners,
        out_specs=(
            [cols] * 5
            + [pl.BlockSpec((per_step, count, count), lambda i: (i, 0, 0))]
            + [same((count, features))] * owners
            + [same((count, share))] * levels
        ),
        scratch_shapes=[
            pltpu.VMEM((count, width), BF16),
            pltpu.VMEM((count, width), F32),
            pltpu.VMEM((count, count), F32),
            pltpu.VMEM((owners, count, features), BF16),
        ],
        compiler_params=params(),
        cost_estimate=pl.CostEstimate(
            flops=2 * count * width * (4 * width + 2 * count * 4),
            bytes_accessed=20 * count * width + 8 * width * width,
            transcendentals=HEADS * count * count,
        ),
        name="forward",
    )(key_mask, w_qkv, w_qkv, w_qkv, w_mix, *tok_col)
    return outs[:6], outs[6 : 6 + owners], outs[6 + owners :]


def backward_kernel(
    owners, levels,
    wm_ref, wq_ref, wk_ref, wv_ref, qn_ref, kn_ref, v_ref, rq_ref, rk_ref, p_ref, *rest,
):
    tok_refs, rest = rest[:owners], rest[owners:]
    flow_refs, rest = rest[:levels], rest[levels:]
    out_refs, acc_ref = rest[:owners], rest[owners]
    step = pl.program_id(0)
    count, width = acc_ref.shape
    head_width = width // HEADS
    cells = count // owners
    d_att = None
    for s in range(levels):
        term = nt(flow_refs[s][...], wm_ref[:, level_cols(s, width // levels)])
        d_att = term if d_att is None else d_att + term
    d_att = d_att.astype(BF16)
    qn, kn, v = qn_ref[...], kn_ref[...], v_ref[...]
    lane = lax.broadcasted_iota(jnp.int32, (count, 128), 1) // head_width
    per_tile = 128 // head_width
    dq_tiles, dk_tiles, dv_tiles = [], [], []
    for t in range(GROUP // 128):
        cols = slice(t * 128, (t + 1) * 128)
        q_t, k_t, v_t, d_t = qn[:, cols], kn[:, cols], v[:, cols], d_att[:, cols]
        dq = dk = dv = None
        for h in range(per_tile):
            d_h = jnp.where(lane == h, d_t, jnp.zeros_like(d_t))
            d_p = nt(d_h, v_t)
            p_b = p_ref[t * per_tile + h]
            p = p_b.astype(F32)
            pd = p * d_p
            d_s = ((pd - p * jnp.sum(pd, axis=-1, keepdims=True)) * score_scale).astype(BF16)
            dq_h, dk_h, dv_h = nn(d_s, k_t), tn(d_s, q_t), tn(p_b, d_t)
            if dq is None:
                dq, dk, dv = dq_h, dk_h, dv_h
            else:
                dq = jnp.where(lane == h, dq_h, dq)
                dk = jnp.where(lane == h, dk_h, dk)
                dv = jnp.where(lane == h, dv_h, dv)
        dq_tiles.append(dq)
        dk_tiles.append(dk)
        dv_tiles.append(dv)
    mean_mat = block_mean(head_width)
    dq = jnp.concatenate(dq_tiles, axis=1)
    dk = jnp.concatenate(dk_tiles, axis=1)
    dv = jnp.concatenate(dv_tiles, axis=1).astype(BF16)

    def through_norm(upstream, unit, factor):
        unit = unit.astype(F32)
        inner = nn((upstream * unit).astype(BF16), mean_mat)
        return (factor * (upstream - unit * inner)).astype(BF16)

    gq = through_norm(dq, qn, rq_ref[...])
    gk = through_norm(dk, kn, rk_ref[...])
    total = nt(gq, wq_ref[...]) + nt(gk, wk_ref[...]) + nt(dv, wv_ref[...])

    @pl.when(step == 0)
    def _():
        acc_ref[...] = total

    @pl.when(step > 0)
    def _():
        acc_ref[...] += total

    @pl.when(step == pl.num_programs(0) - 1)
    def _():
        for t in range(owners):
            x = tok_refs[t][...].astype(F32)
            rx = lax.rsqrt(jnp.mean(x * x, axis=-1, keepdims=True) + epsilon)
            d = acc_ref[t * cells : (t + 1) * cells, :]
            inner = jnp.mean(d * x, axis=-1, keepdims=True)
            out_refs[t][...] = (rx * d - x * (rx * rx * rx * inner)).astype(BF16)


def backward(tok_col, flow, w_mix, w_qkv, saved):
    owners, levels = len(tok_col), len(flow)
    cells, width = tok_col[0].shape
    count = cells * owners
    steps = width // GROUP
    per_step = GROUP // (width // HEADS)
    same = lambda shape: pl.BlockSpec(shape, lambda i: (0, 0))
    cols = pl.BlockSpec((count, GROUP), lambda i: (0, i))
    weight = lambda which: pl.BlockSpec((width, GROUP), lambda i: (0, i + which * steps))
    return pl.pallas_call(
        functools.partial(backward_kernel, owners, levels),
        out_shape=[jax.ShapeDtypeStruct((cells, width), BF16)] * owners,
        grid=(steps,),
        in_specs=[
            pl.BlockSpec((GROUP, width), lambda i: (i, 0)),
            weight(0),
            weight(1),
            weight(2),
            *([cols] * 5),
            pl.BlockSpec((per_step, count, count), lambda i: (i, 0, 0)),
        ]
        + [same((cells, width))] * owners
        + [same((count, width // levels))] * levels,
        out_specs=[same((cells, width))] * owners,
        scratch_shapes=[pltpu.VMEM((count, width), F32)],
        compiler_params=params(),
        cost_estimate=pl.CostEstimate(
            flops=2 * count * width * (4 * width + 4 * count * 4),
            bytes_accessed=20 * count * width + 8 * width * width,
            transcendentals=0,
        ),
        name="backward",
    )(w_mix, w_qkv, w_qkv, w_qkv, *saved, *tok_col, *flow)


def mix_gradient_kernel(owners, levels, factor, flow_ref, *rest):
    att_refs, out_refs, flow_scr = rest[:levels], rest[levels:-1], rest[-1]
    cells, width = flow_ref.shape[1:]
    for t in range(owners):
        flow_scr[t * cells : (t + 1) * cells, :] = flow_ref[lax.axis_index("lat") ^ t]
    flow = flow_scr[...]
    for s in range(levels):
        out_refs[s][...] = (tn(att_refs[s][...], flow) * factor).astype(out_refs[s].dtype)


def mix_gradient(attended, flow_all, factor):
    levels = len(attended)
    owners, cells, width = flow_all.shape
    count, features = attended[0].shape
    return pl.pallas_call(
        functools.partial(mix_gradient_kernel, owners, levels, factor),
        out_shape=[jax.ShapeDtypeStruct((features, width), F32)]
        + [jax.ShapeDtypeStruct((features, width), BF16)] * (levels - 1),
        scratch_shapes=[pltpu.VMEM((owners * cells, width), BF16)],
        compiler_params=params(),
        cost_estimate=pl.CostEstimate(
            flops=2 * count * features * levels * width,
            bytes_accessed=2 * owners * cells * width * 2,
            transcendentals=0,
        ),
        name="mix_gradient",
    )(flow_all, *attended)


def regroup_kernel(owners, levels, *refs):
    outs = refs[owners:]
    cells = refs[0].shape[0] // levels
    for s in range(levels):
        at = pl.ds(pl.multiple_of((lax.axis_index("lev") ^ s) * cells, cells), cells)
        for t in range(owners):
            outs[s][t * cells : (t + 1) * cells, :] = refs[t][at, :]


def regroup(attended, levels):
    owners = len(attended)
    count, features = attended[0].shape
    return call(
        functools.partial(regroup_kernel, owners, levels),
        "regroup",
        [jax.ShapeDtypeStruct((owners * count // levels, features), BF16)] * levels,
        *attended,
    )


def exchange(parts, axis):
    size = len(parts)
    return [parts[0]] + [
        lax.ppermute(parts[s], axis, [(i, i ^ s) for i in range(size)]) for s in range(1, size)
    ]


def on_device(tokens, key_mask, w_qkv, w_mix, level_scale, cotangent):
    batch, _, rows, lon, width = tokens.shape
    owners = lax.axis_size("lat")
    levels = lax.axis_size("lev")
    parts = owners // batch
    chunk = lon // parts
    count = batch * rows * lon
    tok_band = tokens.reshape(batch, rows, parts, chunk, width)
    cot_band = cotangent.reshape(batch, rows, parts, chunk, width)
    w_mix = w_mix.reshape(width, width)

    tok_send, cot_parts = pack(tok_band, cot_band, level_scale, owners, levels)
    tok_col = exchange(tok_send, "lat")
    flow_share = sum_levels(exchange(cot_parts, "lev"), owners)
    flow = exchange([join(exchange(flow_share, "lat"))] * levels, "lev")
    flow_all = lax.all_gather(flow_rows(flow), "lat", axis=0)

    saved, attended, partial = forward(tok_col, key_mask, w_qkv, w_mix, chunk, levels)
    attended = exchange(attended, "lat")
    mix_share = sum_levels(exchange(partial, "lev"), owners)
    back = exchange(backward(tok_col, flow, w_mix, w_qkv, saved), "lat")
    mixed = exchange([join(exchange(mix_share, "lat"))] * levels, "lev")
    output = make_output(tok_band, level_scale, mixed, owners, levels)
    d_tokens = make_gradient(cot_band, back)

    factor = 1.0 / math.sqrt(count * owners)
    mix_parts = mix_gradient(exchange(regroup(attended, levels), "lev"), flow_all, factor)
    mix_grad = sum(part.astype(F32) for part in exchange(mix_parts, "lev"))
    return (
        output.reshape(tokens.shape),
        d_tokens.reshape(tokens.shape),
        mix_grad.reshape(1, width // owners, width),
    )


def solution(mesh):
    return jax.shard_map(
        on_device,
        mesh=mesh,
        in_specs=(
            P(None, "lev", "lat", None, None),
            P(),
            P(),
            P("lev", None, None),
            P("lev", None),
            P(None, "lev", "lat", None, None),
        ),
        out_specs=(
            P(None, "lev", "lat", None, None),
            P(None, "lev", "lat", None, None),
            P("lev", "lat", None),
        ),
        check_vma=False,
    )
```

```python
import functools
import math

import jax
import jax.numpy as jnp
from jax import lax
from jax.experimental import pallas as pl
from jax.experimental.pallas import tpu as pltpu
from jax.sharding import PartitionSpec as P

HEADS = 16
GROUP = 256

epsilon = 1e-06
score_scale = 0.25

F32 = jnp.float32
BF16 = jnp.bfloat16


def nn(a, b):
    return lax.dot_general(a, b, (((1,), (0,)), ((), ())), preferred_element_type=F32)


def nt(a, b):
    return lax.dot_general(a, b, (((1,), (1,)), ((), ())), preferred_element_type=F32)


def tn(a, b):
    return lax.dot_general(a, b, (((0,), (0,)), ((), ())), preferred_element_type=F32)


def block_mean(head_width):
    row = lax.broadcasted_iota(jnp.int32, (GROUP, GROUP), 0) // head_width
    col = lax.broadcasted_iota(jnp.int32, (GROUP, GROUP), 1) // head_width
    return jnp.where(row == col, 1.0 / head_width, 0.0).astype(BF16)


def params():
    return pltpu.CompilerParams(vmem_limit_bytes=36 * 1024 * 1024)


def half_cols(which, width):
    half = width // 2
    core = lax.axis_index("lev") % 2
    return pl.ds(pl.multiple_of((core ^ which) * half, half), half)


def call(kernel, name, out_shape, *operands):
    return pl.pallas_call(
        kernel, out_shape=out_shape, compiler_params=params(), name=name
    )(*operands)


def pack_kernel(tok_ref, cot_ref, gain_ref, tok_out, *cot_outs):
    batch, rows, parts, chunk, width = tok_ref.shape
    for b in range(batch):
        for q in range(parts):
            for r in range(rows):
                tok_out[b * parts + q, r * chunk : (r + 1) * chunk, :] = tok_ref[b, r, q]
    for s in range(2):
        cols = half_cols(s, width)
        gain = gain_ref[:, cols]
        for b in range(batch):
            for q in range(parts):
                for r in range(rows):
                    piece = cot_ref[b, r, q, :, cols].astype(F32)
                    cot_outs[s][b * parts + q, r * chunk : (r + 1) * chunk, :] = (
                        piece * gain
                    ).astype(BF16)


def pack(tokens, cot, gain):
    batch, rows, parts, chunk, width = tokens.shape
    shape = (batch * parts, rows * chunk)
    return call(
        pack_kernel,
        "pack",
        [jax.ShapeDtypeStruct(shape + (width,), BF16)]
        + [jax.ShapeDtypeStruct(shape + (width // 2,), BF16)] * 2,
        tokens,
        cot,
        gain,
    )


def output_kernel(tok_ref, gain_ref, own_ref, other_ref, out_ref):
    batch, rows, parts, chunk, width = tok_ref.shape
    for s, ref in enumerate((own_ref, other_ref)):
        cols = half_cols(s, width)
        gain = gain_ref[:, cols]
        for b in range(batch):
            for q in range(parts):
                for r in range(rows):
                    mixed = ref[b * parts + q, r * chunk : (r + 1) * chunk, :].astype(F32)
                    out_ref[b, r, q, :, cols] = (
                        tok_ref[b, r, q, :, cols].astype(F32) + gain * mixed
                    ).astype(BF16)


def make_output(tokens, gain, mixed):
    return call(
        output_kernel,
        "make_output",
        jax.ShapeDtypeStruct(tokens.shape, BF16),
        tokens,
        gain,
        *mixed,
    )


def gradient_kernel(cot_ref, back_ref, out_ref):
    batch, rows, parts, chunk, width = cot_ref.shape
    for b in range(batch):
        for q in range(parts):
            for r in range(rows):
                back = back_ref[b * parts + q, r * chunk : (r + 1) * chunk, :].astype(F32)
                out_ref[b, r, q] = (cot_ref[b, r, q].astype(F32) + back).astype(BF16)


def make_gradient(cot, back):
    return call(
        gradient_kernel, "make_gradient", jax.ShapeDtypeStruct(cot.shape, BF16), cot, back
    )


def forward_kernel(
    samples, lat_count, chunk, owners,
    tok_ref, mask_ref, wq_ref, wk_ref, wv_ref, wm_ref,
    qn_ref, kn_ref, v_ref, rq_ref, rk_ref, p_ref, att_ref, own_ref, other_ref,
    normed_ref, acc_ref, keep_ref,
):
    step = pl.program_id(0)
    count, width = normed_ref.shape
    head_width = width // HEADS

    @pl.when(step == 0)
    def _():
        x = tok_ref[...].astype(F32)
        rx = lax.rsqrt(jnp.mean(x * x, axis=-1, keepdims=True) + epsilon)
        normed_ref[...] = (x * rx).astype(BF16)
        acc_ref[...] = jnp.zeros_like(acc_ref)
        spread = (
            lax.broadcasted_iota(jnp.int32, (lat_count, count), 0)
            == lax.broadcasted_iota(jnp.int32, (lat_count, count), 1) // chunk
        ).astype(F32)
        per_sample = nn(mask_ref[...].astype(F32), spread)
        mine = lax.axis_index("lat") // (owners // samples)
        pick = lax.broadcasted_iota(jnp.int32, (samples, count), 0) == mine
        valid = jnp.sum(jnp.where(pick, per_sample, 0.0), axis=0, keepdims=True)
        same = (
            lax.broadcasted_iota(jnp.int32, (count, count), 0) % chunk
            == lax.broadcasted_iota(jnp.int32, (count, count), 1) % chunk
        )
        keep_ref[...] = jnp.where(same, valid, 0.0)

    normed = normed_ref[...]
    mean_mat = block_mean(head_width)
    q = nn(normed, wq_ref[...])
    k = nn(normed, wk_ref[...])
    v = nn(normed, wv_ref[...]).astype(BF16)
    rq = lax.rsqrt(nn((q * q).astype(BF16), mean_mat) + epsilon)
    rk = lax.rsqrt(nn((k * k).astype(BF16), mean_mat) + epsilon)
    qn = (q * rq).astype(BF16)
    kn = (k * rk).astype(BF16)
    qn_ref[...] = qn
    kn_ref[...] = kn
    v_ref[...] = v
    rq_ref[...] = rq
    rk_ref[...] = rk
    keep = keep_ref[...]
    lane = lax.broadcasted_iota(jnp.int32, (count, 128), 1) // head_width
    per_tile = 128 // head_width
    tiles = []
    for t in range(GROUP // 128):
        cols = slice(t * 128, (t + 1) * 128)
        q_t, k_t, v_t = qn[:, cols], kn[:, cols], v[:, cols]
        total = None
        for h in range(per_tile):
            q_h = jnp.where(lane == h, q_t * score_scale, jnp.zeros_like(q_t))
            e = jnp.exp(nt(q_h, k_t)) * keep
            p = (e * (1.0 / jnp.sum(e, axis=-1, keepdims=True))).astype(BF16)
            p_ref[t * per_tile + h] = p
            o = nn(p, v_t)
            total = o if total is None else jnp.where(lane == h, o, total)
        tiles.append(total)
    att = jnp.concatenate(tiles, axis=1).astype(BF16)
    features = att_ref.shape[-1]
    for f in range(GROUP // features):
        att_ref[f] = att[:, f * features : (f + 1) * features]
    acc_ref[...] += nn(att, wm_ref[...])

    @pl.when(step == pl.num_programs(0) - 1)
    def _():
        for s, ref in enumerate((own_ref, other_ref)):
            ref[...] = acc_ref[:, half_cols(s, width)].astype(BF16)


def forward(tok_col, key_mask, w_qkv, w_mix, chunk, owners):
    count, width = tok_col.shape
    samples, lat_count = key_mask.shape
    steps = width // GROUP
    per_step = GROUP // (width // HEADS)
    features = width // owners
    same = lambda shape: pl.BlockSpec(shape, lambda i: (0, 0))
    cols = pl.BlockSpec((count, GROUP), lambda i: (0, i))
    weight = lambda which: pl.BlockSpec((width, GROUP), lambda i: (0, i + which * steps))
    return pl.pallas_call(
        functools.partial(forward_kernel, samples, lat_count, chunk, owners),
        out_shape=(
            [jax.ShapeDtypeStruct((count, width), BF16)] * 3
            + [jax.ShapeDtypeStruct((count, width), F32)] * 2
            + [jax.ShapeDtypeStruct((HEADS, count, count), BF16)]
            + [jax.ShapeDtypeStruct((owners, count, features), BF16)]
            + [jax.ShapeDtypeStruct((count, width // 2), BF16)] * 2
        ),
        grid=(steps,),
        in_specs=[
            same((count, width)),
            same((samples, lat_count)),
            weight(0),
            weight(1),
            weight(2),
            pl.BlockSpec((GROUP, width), lambda i: (i, 0)),
        ],
        out_specs=(
            [cols] * 5
            + [pl.BlockSpec((per_step, count, count), lambda i: (i, 0, 0))]
            + [pl.BlockSpec((GROUP // features, count, features), lambda i: (i, 0, 0))]
            + [same((count, width // 2))] * 2
        ),
        scratch_shapes=[
            pltpu.VMEM((count, width), BF16),
            pltpu.VMEM((count, width), F32),
            pltpu.VMEM((count, count), F32),
        ],
        compiler_params=params(),
        cost_estimate=pl.CostEstimate(
            flops=2 * count * width * (4 * width + 2 * count * 4),
            bytes_accessed=20 * count * width + 8 * width * width,
            transcendentals=HEADS * count * count,
        ),
        name="forward",
    )(tok_col, key_mask, w_qkv, w_qkv, w_qkv, w_mix)


def backward_kernel(
    tok_ref, own_ref, other_ref, wm_ref, wq_ref, wk_ref, wv_ref,
    qn_ref, kn_ref, v_ref, rq_ref, rk_ref, p_ref,
    out_ref, acc_ref,
):
    step = pl.program_id(0)
    count, width = acc_ref.shape
    head_width = width // HEADS
    d_att = nt(own_ref[...], wm_ref[:, half_cols(0, width)])
    d_att += nt(other_ref[...], wm_ref[:, half_cols(1, width)])
    d_att = d_att.astype(BF16)
    qn, kn, v = qn_ref[...], kn_ref[...], v_ref[...]
    lane = lax.broadcasted_iota(jnp.int32, (count, 128), 1) // head_width
    per_tile = 128 // head_width
    dq_tiles, dk_tiles, dv_tiles = [], [], []
    for t in range(GROUP // 128):
        cols = slice(t * 128, (t + 1) * 128)
        q_t, k_t, v_t, d_t = qn[:, cols], kn[:, cols], v[:, cols], d_att[:, cols]
        dq = dk = dv = None
        for h in range(per_tile):
            d_h = jnp.where(lane == h, d_t, jnp.zeros_like(d_t))
            d_p = nt(d_h, v_t)
            p_b = p_ref[t * per_tile + h]
            p = p_b.astype(F32)
            pd = p * d_p
            d_s = ((pd - p * jnp.sum(pd, axis=-1, keepdims=True)) * score_scale).astype(BF16)
            dq_h, dk_h, dv_h = nn(d_s, k_t), tn(d_s, q_t), tn(p_b, d_t)
            if dq is None:
                dq, dk, dv = dq_h, dk_h, dv_h
            else:
                dq = jnp.where(lane == h, dq_h, dq)
                dk = jnp.where(lane == h, dk_h, dk)
                dv = jnp.where(lane == h, dv_h, dv)
        dq_tiles.append(dq)
        dk_tiles.append(dk)
        dv_tiles.append(dv)
    mean_mat = block_mean(head_width)
    dq = jnp.concatenate(dq_tiles, axis=1)
    dk = jnp.concatenate(dk_tiles, axis=1)
    dv = jnp.concatenate(dv_tiles, axis=1).astype(BF16)

    def through_norm(upstream, unit, factor):
        unit = unit.astype(F32)
        inner = nn((upstream * unit).astype(BF16), mean_mat)
        return (factor * (upstream - unit * inner)).astype(BF16)

    gq = through_norm(dq, qn, rq_ref[...])
    gk = through_norm(dk, kn, rk_ref[...])
    total = nt(gq, wq_ref[...]) + nt(gk, wk_ref[...]) + nt(dv, wv_ref[...])

    @pl.when(step == 0)
    def _():
        acc_ref[...] = total

    @pl.when(step > 0)
    def _():
        acc_ref[...] += total

    @pl.when(step == pl.num_programs(0) - 1)
    def _():
        x = tok_ref[...].astype(F32)
        rx = lax.rsqrt(jnp.mean(x * x, axis=-1, keepdims=True) + epsilon)
        d = acc_ref[...]
        inner = jnp.mean(d * x, axis=-1, keepdims=True)
        out_ref[...] = (rx * d - x * (rx * rx * rx * inner)).astype(BF16)


def backward(tok_col, flow, w_mix, w_qkv, saved):
    count, width = tok_col.shape
    steps = width // GROUP
    per_step = GROUP // (width // HEADS)
    same = lambda shape: pl.BlockSpec(shape, lambda i: (0, 0))
    cols = pl.BlockSpec((count, GROUP), lambda i: (0, i))
    weight = lambda which: pl.BlockSpec((width, GROUP), lambda i: (0, i + which * steps))
    return pl.pallas_call(
        backward_kernel,
        out_shape=jax.ShapeDtypeStruct((count, width), BF16),
        grid=(steps,),
        in_specs=[
            same((count, width)),
            same((count, width // 2)),
            same((count, width // 2)),
            pl.BlockSpec((GROUP, width), lambda i: (i, 0)),
            weight(0),
            weight(1),
            weight(2),
            *([cols] * 5),
            pl.BlockSpec((per_step, count, count), lambda i: (i, 0, 0)),
        ],
        out_specs=same((count, width)),
        scratch_shapes=[pltpu.VMEM((count, width), F32)],
        compiler_params=params(),
        cost_estimate=pl.CostEstimate(
            flops=2 * count * width * (4 * width + 4 * count * 4),
            bytes_accessed=20 * count * width + 8 * width * width,
            transcendentals=0,
        ),
        name="backward",
    )(tok_col, *flow, w_mix, w_qkv, w_qkv, w_qkv, *saved)


def mix_gradient_kernel(factor, own_ref, other_ref, flow_ref, own_out, other_out, flow_scr):
    bands, owners, cells, half = flow_ref.shape
    count = bands * cells
    features = own_ref.shape[-1]
    for j in range(owners):
        for p in range(bands):
            at = j * count + p * cells
            flow_scr[at : at + cells, :] = flow_ref[p, j]
    flow = flow_scr[...]
    own = own_ref[...].reshape(owners * count, features)
    other = other_ref[...].reshape(owners * count, features)
    own_out[...] = tn(own, flow) * factor
    other_out[...] = (tn(other, flow) * factor).astype(BF16)


def mix_gradient(own, other, flow_all, factor):
    owners, count, features = own.shape
    half = flow_all.shape[-1]
    return pl.pallas_call(
        functools.partial(mix_gradient_kernel, factor),
        out_shape=[
            jax.ShapeDtypeStruct((features, half), F32),
            jax.ShapeDtypeStruct((features, half), BF16),
        ],
        scratch_shapes=[pltpu.VMEM((owners * count, half), BF16)],
        compiler_params=params(),
        cost_estimate=pl.CostEstimate(
            flops=4 * owners * count * features * half,
            bytes_accessed=2 * owners * count * (2 * features + half),
            transcendentals=0,
        ),
        name="mix_gradient",
    )(own, other, flow_all)


def place_kernel(own_ref, other_ref, out_ref):
    width = out_ref.shape[-1]
    out_ref[:, half_cols(0, width)] = own_ref[...]
    out_ref[:, half_cols(1, width)] = other_ref[...].astype(F32)


def place(own, other):
    rows, half = own.shape
    return call(place_kernel, "place", jax.ShapeDtypeStruct((rows, 2 * half), F32), own, other)


def swap(block):
    return lax.all_to_all(block, "lat", split_axis=0, concat_axis=0, tiled=True)


def from_level(block, offset):
    return lax.ppermute(block, "lev", [(i, i ^ offset) for i in range(lax.axis_size("lev"))])


def level_total(own, other):
    total = own
    received = from_level(other, 1)
    offset = 1
    while True:
        total = (total.astype(F32) + received.astype(F32)).astype(BF16)
        offset *= 2
        if offset == lax.axis_size("lev"):
            return total
        received = from_level(total, offset)


def on_device(tokens, key_mask, w_qkv, w_mix, level_scale, cotangent):
    batch, _, rows, lon, width = tokens.shape
    owners = lax.axis_size("lat")
    parts = owners // batch
    chunk = lon // parts
    cells = rows * chunk
    count = batch * rows * lon
    half = width // 2
    tok_band = tokens.reshape(batch, rows, parts, chunk, width)
    cot_band = cotangent.reshape(batch, rows, parts, chunk, width)
    w_mix = w_mix.reshape(width, width)

    tok_send, cot_own, cot_other = pack(tok_band, cot_band, level_scale)
    tok_col = swap(tok_send).reshape(count, width)
    flow_band = level_total(cot_own, cot_other)
    flow_own = swap(flow_band).reshape(count, half)
    flow = (flow_own, from_level(flow_own, 1))
    flow_all = lax.all_gather(flow_band, "lat", axis=0)

    *saved, attended, mix_own, mix_other = forward(
        tok_col, key_mask, w_qkv, w_mix, chunk, owners
    )
    attended = swap(attended)
    mix_half = level_total(mix_own, mix_other)
    back_col = backward(tok_col, flow, w_mix, w_qkv, saved)
    back = swap(back_col.reshape(owners, cells, width))
    mix_band = swap(mix_half.reshape(owners, cells, half))
    output = make_output(tok_band, level_scale, (mix_band, from_level(mix_band, 1)))
    d_tokens = make_gradient(cot_band, back)

    factor = 1.0 / math.sqrt(count * owners)
    grad_own, grad_other = mix_gradient(attended, from_level(attended, 1), flow_all, factor)
    mix_grad = place(grad_own, from_level(grad_other, 1))
    return (
        output.reshape(tokens.shape),
        d_tokens.reshape(tokens.shape),
        mix_grad.reshape(1, width // owners, width),
    )


def solution(mesh):
    return jax.shard_map(
        on_device,
        mesh=mesh,
        in_specs=(
            P(None, "lev", "lat", None, None),
            P(),
            P(),
            P("lev", None, None),
            P("lev", None),
            P(None, "lev", "lat", None, None),
        ),
        out_specs=(
            P(None, "lev", "lat", None, None),
            P(None, "lev", "lat", None, None),
            P("lev", "lat", None),
        ),
        check_vma=False,
    )
```

```python
import functools
import math

import jax
import jax.numpy as jnp
from jax import lax
from jax.experimental import pallas as pl
from jax.experimental.pallas import tpu as pltpu
from jax.sharding import PartitionSpec as P

HEADS = 16
GROUP = 256

epsilon = 1e-06
score_scale = 0.25

F32 = jnp.float32
BF16 = jnp.bfloat16


def nn(a, b):
    return lax.dot_general(a, b, (((1,), (0,)), ((), ())), preferred_element_type=F32)


def nt(a, b):
    return lax.dot_general(a, b, (((1,), (1,)), ((), ())), preferred_element_type=F32)


def tn(a, b):
    return lax.dot_general(a, b, (((0,), (0,)), ((), ())), preferred_element_type=F32)


def block_mean(head_width):
    row = lax.broadcasted_iota(jnp.int32, (GROUP, GROUP), 0) // head_width
    col = lax.broadcasted_iota(jnp.int32, (GROUP, GROUP), 1) // head_width
    return jnp.where(row == col, 1.0 / head_width, 0.0).astype(BF16)


def params():
    return pltpu.CompilerParams(vmem_limit_bytes=36 * 1024 * 1024)


def half_cols(which, width):
    half = width // 2
    core = lax.axis_index("lev") % 2
    return pl.ds(pl.multiple_of((core ^ which) * half, half), half)


def in_hbm(array):
    return pltpu.with_memory_space_constraint(array, pltpu.HBM)


def call(kernel, name, out_shape, *operands):
    return pl.pallas_call(
        kernel, out_shape=out_shape, compiler_params=params(), name=name
    )(*operands)


def pack_kernel(tok_ref, cot_ref, gain_ref, tok_out, *cot_outs):
    batch, rows, parts, chunk, width = tok_ref.shape
    for b in range(batch):
        for q in range(parts):
            for r in range(rows):
                tok_out[b * parts + q, r * chunk : (r + 1) * chunk, :] = tok_ref[b, r, q]
    for s in range(2):
        cols = half_cols(s, width)
        gain = gain_ref[:, cols]
        for b in range(batch):
            for q in range(parts):
                for r in range(rows):
                    piece = cot_ref[b, r, q, :, cols].astype(F32)
                    cot_outs[s][b * parts + q, r * chunk : (r + 1) * chunk, :] = (
                        piece * gain
                    ).astype(BF16)


def pack(tokens, cot, gain):
    batch, rows, parts, chunk, width = tokens.shape
    shape = (batch * parts, rows * chunk)
    return call(
        pack_kernel,
        "pack",
        [jax.ShapeDtypeStruct(shape + (width,), BF16)]
        + [jax.ShapeDtypeStruct(shape + (width // 2,), BF16)] * 2,
        tokens,
        cot,
        gain,
    )


def output_kernel(tok_ref, gain_ref, own_ref, other_ref, out_ref):
    batch, rows, parts, chunk, width = tok_ref.shape
    for s, ref in enumerate((own_ref, other_ref)):
        cols = half_cols(s, width)
        gain = gain_ref[:, cols]
        for b in range(batch):
            for q in range(parts):
                for r in range(rows):
                    mixed = ref[b * parts + q, r * chunk : (r + 1) * chunk, :].astype(F32)
                    out_ref[b, r, q, :, cols] = (
                        tok_ref[b, r, q, :, cols].astype(F32) + gain * mixed
                    ).astype(BF16)


def make_output(tokens, gain, mixed):
    return call(
        output_kernel,
        "make_output",
        jax.ShapeDtypeStruct(tokens.shape, BF16),
        tokens,
        gain,
        *mixed,
    )


def gradient_kernel(cot_ref, back_ref, out_ref):
    batch, rows, parts, chunk, width = cot_ref.shape
    for b in range(batch):
        for q in range(parts):
            for r in range(rows):
                back = back_ref[b * parts + q, r * chunk : (r + 1) * chunk, :].astype(F32)
                out_ref[b, r, q] = (cot_ref[b, r, q].astype(F32) + back).astype(BF16)


def make_gradient(cot, back):
    return call(
        gradient_kernel, "make_gradient", jax.ShapeDtypeStruct(cot.shape, BF16), cot, back
    )


def forward_kernel(
    samples, lat_count, chunk, owners,
    tok_ref, mask_ref, wq_ref, wk_ref, wv_ref, wm_ref,
    qn_ref, kn_ref, v_ref, rq_ref, rk_ref, p_ref, att_ref, own_ref, other_ref,
    normed_ref, acc_ref, keep_ref,
):
    step = pl.program_id(0)
    count, width = normed_ref.shape
    head_width = width // HEADS

    @pl.when(step == 0)
    def _():
        x = tok_ref[...].astype(F32)
        rx = lax.rsqrt(jnp.mean(x * x, axis=-1, keepdims=True) + epsilon)
        normed_ref[...] = (x * rx).astype(BF16)
        acc_ref[...] = jnp.zeros_like(acc_ref)
        spread = (
            lax.broadcasted_iota(jnp.int32, (lat_count, count), 0)
            == lax.broadcasted_iota(jnp.int32, (lat_count, count), 1) // chunk
        ).astype(F32)
        per_sample = nn(mask_ref[...].astype(F32), spread)
        mine = lax.axis_index("lat") // (owners // samples)
        pick = lax.broadcasted_iota(jnp.int32, (samples, count), 0) == mine
        valid = jnp.sum(jnp.where(pick, per_sample, 0.0), axis=0, keepdims=True)
        same = (
            lax.broadcasted_iota(jnp.int32, (count, count), 0) % chunk
            == lax.broadcasted_iota(jnp.int32, (count, count), 1) % chunk
        )
        keep_ref[...] = jnp.where(same, valid, 0.0)

    normed = normed_ref[...]
    mean_mat = block_mean(head_width)
    q = nn(normed, wq_ref[...])
    k = nn(normed, wk_ref[...])
    v = nn(normed, wv_ref[...]).astype(BF16)
    rq = lax.rsqrt(nn((q * q).astype(BF16), mean_mat) + epsilon)
    rk = lax.rsqrt(nn((k * k).astype(BF16), mean_mat) + epsilon)
    qn = (q * rq).astype(BF16)
    kn = (k * rk).astype(BF16)
    qn_ref[...] = qn
    kn_ref[...] = kn
    v_ref[...] = v
    rq_ref[...] = rq
    rk_ref[...] = rk
    keep = keep_ref[...]
    lane = lax.broadcasted_iota(jnp.int32, (count, 128), 1) // head_width
    per_tile = 128 // head_width
    tiles = []
    for t in range(GROUP // 128):
        cols = slice(t * 128, (t + 1) * 128)
        q_t, k_t, v_t = qn[:, cols], kn[:, cols], v[:, cols]
        total = None
        for h in range(per_tile):
            q_h = jnp.where(lane == h, q_t * score_scale, jnp.zeros_like(q_t))
            e = jnp.exp(nt(q_h, k_t)) * keep
            p = (e * (1.0 / jnp.sum(e, axis=-1, keepdims=True))).astype(BF16)
            p_ref[t * per_tile + h] = p
            o = nn(p, v_t)
            total = o if total is None else jnp.where(lane == h, o, total)
        tiles.append(total)
    att = jnp.concatenate(tiles, axis=1).astype(BF16)
    features = att_ref.shape[-1]
    for f in range(GROUP // features):
        att_ref[f] = att[:, f * features : (f + 1) * features]
    acc_ref[...] += nn(att, wm_ref[...])

    @pl.when(step == pl.num_programs(0) - 1)
    def _():
        for s, ref in enumerate((own_ref, other_ref)):
            ref[...] = acc_ref[:, half_cols(s, width)].astype(BF16)


def forward(tok_col, key_mask, w_qkv, w_mix, chunk, owners):
    count, width = tok_col.shape
    samples, lat_count = key_mask.shape
    steps = width // GROUP
    per_step = GROUP // (width // HEADS)
    features = width // owners
    same = lambda shape: pl.BlockSpec(shape, lambda i: (0, 0))
    cols = pl.BlockSpec((count, GROUP), lambda i: (0, i))
    weight = lambda which: pl.BlockSpec((width, GROUP), lambda i: (0, i + which * steps))
    return pl.pallas_call(
        functools.partial(forward_kernel, samples, lat_count, chunk, owners),
        out_shape=(
            [pltpu.HBM((count, width), BF16)] * 3
            + [pltpu.HBM((count, width), F32)] * 2
            + [pltpu.HBM((HEADS, count, count), BF16)]
            + [jax.ShapeDtypeStruct((owners, count, features), BF16)]
            + [jax.ShapeDtypeStruct((count, width // 2), BF16)] * 2
        ),
        grid=(steps,),
        in_specs=[
            same((count, width)),
            same((samples, lat_count)),
            weight(0),
            weight(1),
            weight(2),
            pl.BlockSpec((GROUP, width), lambda i: (i, 0)),
        ],
        out_specs=(
            [cols] * 5
            + [pl.BlockSpec((per_step, count, count), lambda i: (i, 0, 0))]
            + [pl.BlockSpec((GROUP // features, count, features), lambda i: (i, 0, 0))]
            + [same((count, width // 2))] * 2
        ),
        scratch_shapes=[
            pltpu.VMEM((count, width), BF16),
            pltpu.VMEM((count, width), F32),
            pltpu.VMEM((count, count), F32),
        ],
        compiler_params=params(),
        cost_estimate=pl.CostEstimate(
            flops=2 * count * width * (4 * width + 2 * count * 4),
            bytes_accessed=20 * count * width + 8 * width * width,
            transcendentals=HEADS * count * count,
        ),
        name="forward",
    )(tok_col, key_mask, *[in_hbm(w_qkv)] * 3, in_hbm(w_mix))


def backward_kernel(
    tok_ref, own_ref, other_ref, wm_ref, wq_ref, wk_ref, wv_ref,
    qn_ref, kn_ref, v_ref, rq_ref, rk_ref, p_ref,
    out_ref, acc_ref,
):
    step = pl.program_id(0)
    count, width = acc_ref.shape
    head_width = width // HEADS
    d_att = nt(own_ref[...], wm_ref[:, half_cols(0, width)])
    d_att += nt(other_ref[...], wm_ref[:, half_cols(1, width)])
    d_att = d_att.astype(BF16)
    qn, kn, v = qn_ref[...], kn_ref[...], v_ref[...]
    lane = lax.broadcasted_iota(jnp.int32, (count, 128), 1) // head_width
    per_tile = 128 // head_width
    dq_tiles, dk_tiles, dv_tiles = [], [], []
    for t in range(GROUP // 128):
        cols = slice(t * 128, (t + 1) * 128)
        q_t, k_t, v_t, d_t = qn[:, cols], kn[:, cols], v[:, cols], d_att[:, cols]
        dq = dk = dv = None
        for h in range(per_tile):
            d_h = jnp.where(lane == h, d_t, jnp.zeros_like(d_t))
            d_p = nt(d_h, v_t)
            p_b = p_ref[t * per_tile + h]
            p = p_b.astype(F32)
            pd = p * d_p
            d_s = ((pd - p * jnp.sum(pd, axis=-1, keepdims=True)) * score_scale).astype(BF16)
            dq_h, dk_h, dv_h = nn(d_s, k_t), tn(d_s, q_t), tn(p_b, d_t)
            if dq is None:
                dq, dk, dv = dq_h, dk_h, dv_h
            else:
                dq = jnp.where(lane == h, dq_h, dq)
                dk = jnp.where(lane == h, dk_h, dk)
                dv = jnp.where(lane == h, dv_h, dv)
        dq_tiles.append(dq)
        dk_tiles.append(dk)
        dv_tiles.append(dv)
    mean_mat = block_mean(head_width)
    dq = jnp.concatenate(dq_tiles, axis=1)
    dk = jnp.concatenate(dk_tiles, axis=1)
    dv = jnp.concatenate(dv_tiles, axis=1).astype(BF16)

    def through_norm(upstream, unit, factor):
        unit = unit.astype(F32)
        inner = nn((upstream * unit).astype(BF16), mean_mat)
        return (factor * (upstream - unit * inner)).astype(BF16)

    gq = through_norm(dq, qn, rq_ref[...])
    gk = through_norm(dk, kn, rk_ref[...])
    total = nt(gq, wq_ref[...]) + nt(gk, wk_ref[...]) + nt(dv, wv_ref[...])

    @pl.when(step == 0)
    def _():
        acc_ref[...] = total

    @pl.when(step > 0)
    def _():
        acc_ref[...] += total

    @pl.when(step == pl.num_programs(0) - 1)
    def _():
        x = tok_ref[...].astype(F32)
        rx = lax.rsqrt(jnp.mean(x * x, axis=-1, keepdims=True) + epsilon)
        d = acc_ref[...]
        inner = jnp.mean(d * x, axis=-1, keepdims=True)
        out_ref[...] = (rx * d - x * (rx * rx * rx * inner)).astype(BF16)


def backward(tok_col, flow, w_mix, w_qkv, saved):
    count, width = tok_col.shape
    steps = width // GROUP
    per_step = GROUP // (width // HEADS)
    same = lambda shape: pl.BlockSpec(shape, lambda i: (0, 0))
    cols = pl.BlockSpec((count, GROUP), lambda i: (0, i))
    weight = lambda which: pl.BlockSpec((width, GROUP), lambda i: (0, i + which * steps))
    return pl.pallas_call(
        backward_kernel,
        out_shape=jax.ShapeDtypeStruct((count, width), BF16),
        grid=(steps,),
        in_specs=[
            same((count, width)),
            same((count, width // 2)),
            same((count, width // 2)),
            pl.BlockSpec((GROUP, width), lambda i: (i, 0)),
            weight(0),
            weight(1),
            weight(2),
            *([cols] * 5),
            pl.BlockSpec((per_step, count, count), lambda i: (i, 0, 0)),
        ],
        out_specs=same((count, width)),
        scratch_shapes=[pltpu.VMEM((count, width), F32)],
        compiler_params=params(),
        cost_estimate=pl.CostEstimate(
            flops=2 * count * width * (4 * width + 4 * count * 4),
            bytes_accessed=20 * count * width + 8 * width * width,
            transcendentals=0,
        ),
        name="backward",
    )(tok_col, *flow, in_hbm(w_mix), *[in_hbm(w_qkv)] * 3, *map(in_hbm, saved))


def mix_gradient_kernel(factor, own_ref, other_ref, *refs):
    *flow_refs, own_out, other_out, flow_scr = refs
    bands, owners, cells, share = flow_refs[0].shape
    count = bands * cells
    features = own_ref.shape[-1]
    chip = lax.axis_index("lev") // 2
    for k, ref in enumerate(flow_refs):
        cols = pl.ds(pl.multiple_of((chip ^ k) * share, share), share)
        for j in range(owners):
            for p in range(bands):
                at = j * count + p * cells
                flow_scr[at : at + cells, cols] = ref[p, j]
    flow = flow_scr[...]
    own = own_ref[...].reshape(owners * count, features)
    other = other_ref[...].reshape(owners * count, features)
    own_out[...] = tn(own, flow) * factor
    other_out[...] = (tn(other, flow) * factor).astype(BF16)


def mix_gradient(own, other, flow_parts, factor):
    owners, count, features = own.shape
    half = flow_parts[0].shape[-1] * len(flow_parts)
    return pl.pallas_call(
        functools.partial(mix_gradient_kernel, factor),
        out_shape=[
            jax.ShapeDtypeStruct((features, half), F32),
            jax.ShapeDtypeStruct((features, half), BF16),
        ],
        scratch_shapes=[pltpu.VMEM((owners * count, half), BF16)],
        compiler_params=params(),
        cost_estimate=pl.CostEstimate(
            flops=4 * owners * count * features * half,
            bytes_accessed=2 * owners * count * (2 * features + half),
            transcendentals=0,
        ),
        name="mix_gradient",
    )(own, other, *flow_parts)


def place_kernel(own_ref, other_ref, out_ref):
    width = out_ref.shape[-1]
    out_ref[:, half_cols(0, width)] = own_ref[...]
    out_ref[:, half_cols(1, width)] = other_ref[...].astype(F32)


def place(own, other):
    rows, half = own.shape
    return call(place_kernel, "place", jax.ShapeDtypeStruct((rows, 2 * half), F32), own, other)


def swap(block):
    return lax.all_to_all(block, "lat", split_axis=0, concat_axis=0, tiled=True)


def from_level(block, offset):
    return lax.ppermute(block, "lev", [(i, i ^ offset) for i in range(lax.axis_size("lev"))])


def add_kernel(own_ref, received_ref, *rest):
    rest[-1][...] = (own_ref[...].astype(F32) + received_ref[...].astype(F32)).astype(BF16)


def add(own, received, after=()):
    whole = pl.BlockSpec(memory_space=pltpu.VMEM)
    return pl.pallas_call(
        add_kernel,
        out_shape=jax.ShapeDtypeStruct(own.shape, BF16),
        in_specs=[whole, whole] + [pl.BlockSpec(memory_space=pl.ANY)] * len(after),
        out_specs=whole,
        compiler_params=params(),
        name="add",
    )(own, received, *after)


def pair_total(own, other):
    return add(own, from_level(other, 1))


def level_total(total, after):
    offset = 2
    while offset < lax.axis_size("lev"):
        total = add(total, from_level(total, offset), after)
        offset *= 2
    return total


def slice_kernel(in_ref, out_ref):
    share = out_ref.shape[-1]
    at = pl.multiple_of(lax.axis_index("lev") // 2 * share, share)
    out_ref[...] = in_ref[:, :, pl.ds(at, share)]


def gather_flow(flow_band):
    chips = lax.axis_size("lev") // 2
    owners, cells, half = flow_band.shape
    shape = jax.ShapeDtypeStruct((owners, cells, half // chips), BF16)
    mine = lax.all_gather(call(slice_kernel, "slice", shape, flow_band), "lat", axis=0)
    return [mine] + [from_level(mine, 2 * k) for k in range(1, chips)]


def on_device(tokens, key_mask, w_qkv, w_mix, level_scale, cotangent):
    batch, _, rows, lon, width = tokens.shape
    owners = lax.axis_size("lat")
    parts = owners // batch
    chunk = lon // parts
    cells = rows * chunk
    count = batch * rows * lon
    half = width // 2
    tok_band = tokens.reshape(batch, rows, parts, chunk, width)
    cot_band = cotangent.reshape(batch, rows, parts, chunk, width)
    w_mix = w_mix.reshape(width, width)

    tok_send, cot_own, cot_other = pack(tok_band, cot_band, level_scale)
    tok_col = swap(tok_send).reshape(count, width)
    flow_band = level_total(pair_total(cot_own, cot_other), (tok_col,))
    flow_own = swap(flow_band).reshape(count, half)
    flow = (flow_own, from_level(flow_own, 1))
    flow_parts = gather_flow(flow_band)

    *saved, attended, mix_own, mix_other = forward(
        tok_col, key_mask, w_qkv, w_mix, chunk, owners
    )
    attended = swap(attended)
    mix_pair = pair_total(mix_own, mix_other)
    back_col = backward(tok_col, flow, w_mix, w_qkv, saved)
    mix_half = level_total(mix_pair, (back_col,))
    back = swap(back_col.reshape(owners, cells, width))
    mix_band = swap(mix_half.reshape(owners, cells, half))
    output = make_output(tok_band, level_scale, (mix_band, from_level(mix_band, 1)))
    d_tokens = make_gradient(cot_band, back)

    factor = 1.0 / math.sqrt(count * owners)
    grad_own, grad_other = mix_gradient(attended, from_level(attended, 1), flow_parts, factor)
    mix_grad = place(grad_own, from_level(grad_other, 1))
    return (
        output.reshape(tokens.shape),
        d_tokens.reshape(tokens.shape),
        mix_grad.reshape(1, width // owners, width),
    )


def solution(mesh):
    return jax.shard_map(
        on_device,
        mesh=mesh,
        in_specs=(
            P(None, "lev", "lat", None, None),
            P(),
            P(),
            P("lev", None, None),
            P("lev", None),
            P(None, "lev", "lat", None, None),
        ),
        out_specs=(
            P(None, "lev", "lat", None, None),
            P(None, "lev", "lat", None, None),
            P("lev", "lat", None),
        ),
        check_vma=False,
    )
```

```python
import functools
import math

import jax
import jax.numpy as jnp
from jax import lax
from jax.experimental import pallas as pl
from jax.experimental.pallas import tpu as pltpu
from jax.sharding import PartitionSpec as P

HEADS = 16
GROUP = 256

epsilon = 1e-06
score_scale = 0.25

F32 = jnp.float32
BF16 = jnp.bfloat16


def nn(a, b):
    return lax.dot_general(a, b, (((1,), (0,)), ((), ())), preferred_element_type=F32)


def nt(a, b):
    return lax.dot_general(a, b, (((1,), (1,)), ((), ())), preferred_element_type=F32)


def tn(a, b):
    return lax.dot_general(a, b, (((0,), (0,)), ((), ())), preferred_element_type=F32)


def block_mean(head_width):
    row = lax.broadcasted_iota(jnp.int32, (GROUP, GROUP), 0) // head_width
    col = lax.broadcasted_iota(jnp.int32, (GROUP, GROUP), 1) // head_width
    return jnp.where(row == col, 1.0 / head_width, 0.0).astype(BF16)


def params():
    return pltpu.CompilerParams(vmem_limit_bytes=36 * 1024 * 1024)


def half_cols(which, width):
    half = width // 2
    core = lax.axis_index("lev") % 2
    return pl.ds(pl.multiple_of((core ^ which) * half, half), half)


def in_hbm(array):
    return pltpu.with_memory_space_constraint(array, pltpu.HBM)


def call(kernel, name, out_shape, *operands):
    return pl.pallas_call(
        kernel, out_shape=out_shape, compiler_params=params(), name=name
    )(*operands)


def pack_kernel(tok_ref, cot_ref, gain_ref, tok_out, *cot_outs):
    batch, rows, parts, chunk, width = tok_ref.shape
    for b in range(batch):
        for q in range(parts):
            for r in range(rows):
                tok_out[b * parts + q, r * chunk : (r + 1) * chunk, :] = tok_ref[b, r, q]
    for s in range(2):
        cols = half_cols(s, width)
        gain = gain_ref[:, cols]
        for b in range(batch):
            for q in range(parts):
                for r in range(rows):
                    piece = cot_ref[b, r, q, :, cols].astype(F32)
                    cot_outs[s][b * parts + q, r * chunk : (r + 1) * chunk, :] = (
                        piece * gain
                    ).astype(BF16)


def pack(tokens, cot, gain):
    batch, rows, parts, chunk, width = tokens.shape
    shape = (batch * parts, rows * chunk)
    return call(
        pack_kernel,
        "pack",
        [jax.ShapeDtypeStruct(shape + (width,), BF16)]
        + [jax.ShapeDtypeStruct(shape + (width // 2,), BF16)] * 2,
        in_hbm(tokens),
        in_hbm(cot),
        in_hbm(gain),
    )


def output_kernel(tok_ref, gain_ref, own_ref, other_ref, out_ref):
    batch, rows, parts, chunk, width = tok_ref.shape
    for s, ref in enumerate((own_ref, other_ref)):
        cols = half_cols(s, width)
        gain = gain_ref[:, cols]
        for t in range(batch * parts):
            owner = lax.axis_index("lat") ^ t
            b, q = owner // parts, owner % parts
            for r in range(rows):
                mixed = ref[t, r * chunk : (r + 1) * chunk, :].astype(F32)
                out_ref[b, r, q, :, cols] = (
                    tok_ref[b, r, q, :, cols].astype(F32) + gain * mixed
                ).astype(BF16)


def make_output(tokens, gain, mixed):
    return call(
        output_kernel,
        "make_output",
        jax.ShapeDtypeStruct(tokens.shape, BF16),
        tokens,
        gain,
        *mixed,
    )


def gradient_kernel(cot_ref, back_ref, out_ref):
    batch, rows, parts, chunk, width = cot_ref.shape
    for b in range(batch):
        for q in range(parts):
            for r in range(rows):
                back = back_ref[b * parts + q, r * chunk : (r + 1) * chunk, :].astype(F32)
                out_ref[b, r, q] = (cot_ref[b, r, q].astype(F32) + back).astype(BF16)


def make_gradient(cot, back):
    return call(
        gradient_kernel, "make_gradient", jax.ShapeDtypeStruct(cot.shape, BF16), cot, back
    )


def forward_kernel(
    samples, lat_count, chunk, owners,
    tok_ref, mask_ref, wq_ref, wk_ref, wv_ref, wm_ref,
    qn_ref, kn_ref, v_ref, rq_ref, rk_ref, p_ref, att_ref, own_ref, other_ref,
    normed_ref, acc_ref, keep_ref,
):
    step = pl.program_id(0)
    count, width = normed_ref.shape
    head_width = width // HEADS

    @pl.when(step == 0)
    def _():
        x = tok_ref[...].astype(F32)
        rx = lax.rsqrt(jnp.mean(x * x, axis=-1, keepdims=True) + epsilon)
        normed_ref[...] = (x * rx).astype(BF16)
        acc_ref[...] = jnp.zeros_like(acc_ref)
        spread = (
            lax.broadcasted_iota(jnp.int32, (lat_count, count), 0)
            == lax.broadcasted_iota(jnp.int32, (lat_count, count), 1) // chunk
        ).astype(F32)
        per_sample = nn(mask_ref[...].astype(F32), spread)
        mine = lax.axis_index("lat") // (owners // samples)
        pick = lax.broadcasted_iota(jnp.int32, (samples, count), 0) == mine
        valid = jnp.sum(jnp.where(pick, per_sample, 0.0), axis=0, keepdims=True)
        same = (
            lax.broadcasted_iota(jnp.int32, (count, count), 0) % chunk
            == lax.broadcasted_iota(jnp.int32, (count, count), 1) % chunk
        )
        keep_ref[...] = jnp.where(same, valid, 0.0)

    normed = normed_ref[...]
    mean_mat = block_mean(head_width)
    q = nn(normed, wq_ref[...])
    k = nn(normed, wk_ref[...])
    v = nn(normed, wv_ref[...]).astype(BF16)
    rq = lax.rsqrt(nn((q * q).astype(BF16), mean_mat) + epsilon)
    rk = lax.rsqrt(nn((k * k).astype(BF16), mean_mat) + epsilon)
    qn = (q * rq).astype(BF16)
    kn = (k * rk).astype(BF16)
    qn_ref[...] = qn
    kn_ref[...] = kn
    v_ref[...] = v
    rq_ref[...] = rq.astype(BF16)
    rk_ref[...] = rk.astype(BF16)
    keep = keep_ref[...]
    lane = lax.broadcasted_iota(jnp.int32, (count, 128), 1) // head_width
    per_tile = 128 // head_width
    tiles = []
    for t in range(GROUP // 128):
        cols = slice(t * 128, (t + 1) * 128)
        q_t, k_t, v_t = qn[:, cols], kn[:, cols], v[:, cols]
        total = None
        for h in range(per_tile):
            q_h = jnp.where(lane == h, q_t * score_scale, jnp.zeros_like(q_t))
            e = jnp.exp(nt(q_h, k_t)) * keep
            p = (e * (1.0 / jnp.sum(e, axis=-1, keepdims=True))).astype(BF16)
            p_ref[t * per_tile + h] = p
            o = nn(p, v_t)
            total = o if total is None else jnp.where(lane == h, o, total)
        tiles.append(total)
    att = jnp.concatenate(tiles, axis=1).astype(BF16)
    features = att_ref.shape[-1]
    for f in range(GROUP // features):
        att_ref[f] = att[:, f * features : (f + 1) * features]
    acc_ref[...] += nn(att, wm_ref[...])

    @pl.when(step == pl.num_programs(0) - 1)
    def _():
        for s, ref in enumerate((own_ref, other_ref)):
            ref[...] = acc_ref[:, half_cols(s, width)].astype(BF16)


def forward(tok_col, key_mask, w_qkv, w_mix, chunk, owners):
    count, width = tok_col.shape
    samples, lat_count = key_mask.shape
    steps = width // GROUP
    per_step = GROUP // (width // HEADS)
    features = width // owners
    same = lambda shape: pl.BlockSpec(shape, lambda i: (0, 0))
    cols = pl.BlockSpec((count, GROUP), lambda i: (0, i))
    weight = lambda which: pl.BlockSpec((width, GROUP), lambda i: (0, i + which * steps))
    return pl.pallas_call(
        functools.partial(forward_kernel, samples, lat_count, chunk, owners),
        out_shape=(
            [pltpu.HBM((count, width), BF16)] * 5
            + [pltpu.HBM((HEADS, count, count), BF16)]
            + [jax.ShapeDtypeStruct((owners, count, features), BF16)]
            + [jax.ShapeDtypeStruct((count, width // 2), BF16)] * 2
        ),
        grid=(steps,),
        in_specs=[
            same((count, width)),
            same((samples, lat_count)),
            weight(0),
            weight(1),
            weight(2),
            pl.BlockSpec((GROUP, width), lambda i: (i, 0)),
        ],
        out_specs=(
            [cols] * 5
            + [pl.BlockSpec((per_step, count, count), lambda i: (i, 0, 0))]
            + [pl.BlockSpec((GROUP // features, count, features), lambda i: (i, 0, 0))]
            + [same((count, width // 2))] * 2
        ),
        scratch_shapes=[
            pltpu.VMEM((count, width), BF16),
            pltpu.VMEM((count, width), F32),
            pltpu.VMEM((count, count), F32),
        ],
        compiler_params=params(),
        cost_estimate=pl.CostEstimate(
            flops=2 * count * width * (4 * width + 2 * count * 4),
            bytes_accessed=20 * count * width + 8 * width * width,
            transcendentals=HEADS * count * count,
        ),
        name="forward",
    )(tok_col, key_mask, *[in_hbm(w_qkv)] * 3, in_hbm(w_mix))


def backward_kernel(
    tok_ref, own_ref, other_ref, wm_ref, wq_ref, wk_ref, wv_ref,
    qn_ref, kn_ref, v_ref, rq_ref, rk_ref, p_ref,
    out_ref, acc_ref,
):
    step = pl.program_id(0)
    count, width = acc_ref.shape
    head_width = width // HEADS
    d_att = nt(own_ref[...], wm_ref[:, half_cols(0, width)])
    d_att += nt(other_ref[...], wm_ref[:, half_cols(1, width)])
    d_att = d_att.astype(BF16)
    qn, kn, v = qn_ref[...], kn_ref[...], v_ref[...]
    lane = lax.broadcasted_iota(jnp.int32, (count, 128), 1) // head_width
    per_tile = 128 // head_width
    dq_tiles, dk_tiles, dv_tiles = [], [], []
    for t in range(GROUP // 128):
        cols = slice(t * 128, (t + 1) * 128)
        q_t, k_t, v_t, d_t = qn[:, cols], kn[:, cols], v[:, cols], d_att[:, cols]
        dq = dk = dv = None
        for h in range(per_tile):
            d_h = jnp.where(lane == h, d_t, jnp.zeros_like(d_t))
            d_p = nt(d_h, v_t)
            p_b = p_ref[t * per_tile + h]
            p = p_b.astype(F32)
            pd = p * d_p
            d_s = ((pd - p * jnp.sum(pd, axis=-1, keepdims=True)) * score_scale).astype(BF16)
            dq_h, dk_h, dv_h = nn(d_s, k_t), tn(d_s, q_t), tn(p_b, d_t)
            if dq is None:
                dq, dk, dv = dq_h, dk_h, dv_h
            else:
                dq = jnp.where(lane == h, dq_h, dq)
                dk = jnp.where(lane == h, dk_h, dk)
                dv = jnp.where(lane == h, dv_h, dv)
        dq_tiles.append(dq)
        dk_tiles.append(dk)
        dv_tiles.append(dv)
    mean_mat = block_mean(head_width)
    dq = jnp.concatenate(dq_tiles, axis=1)
    dk = jnp.concatenate(dk_tiles, axis=1)
    dv = jnp.concatenate(dv_tiles, axis=1).astype(BF16)

    def through_norm(upstream, unit, factor):
        unit = unit.astype(F32)
        inner = nn((upstream * unit).astype(BF16), mean_mat)
        return (factor.astype(F32) * (upstream - unit * inner)).astype(BF16)

    gq = through_norm(dq, qn, rq_ref[...])
    gk = through_norm(dk, kn, rk_ref[...])
    total = nt(gq, wq_ref[...]) + nt(gk, wk_ref[...]) + nt(dv, wv_ref[...])

    @pl.when(step == 0)
    def _():
        acc_ref[...] = total

    @pl.when(step > 0)
    def _():
        acc_ref[...] += total

    @pl.when(step == pl.num_programs(0) - 1)
    def _():
        x = tok_ref[...].astype(F32)
        rx = lax.rsqrt(jnp.mean(x * x, axis=-1, keepdims=True) + epsilon)
        d = acc_ref[...]
        inner = jnp.mean(d * x, axis=-1, keepdims=True)
        out_ref[...] = (rx * d - x * (rx * rx * rx * inner)).astype(BF16)


def backward(tok_col, flow, w_mix, w_qkv, saved):
    count, width = tok_col.shape
    steps = width // GROUP
    per_step = GROUP // (width // HEADS)
    same = lambda shape: pl.BlockSpec(shape, lambda i: (0, 0))
    cols = pl.BlockSpec((count, GROUP), lambda i: (0, i))
    weight = lambda which: pl.BlockSpec((width, GROUP), lambda i: (0, i + which * steps))
    return pl.pallas_call(
        backward_kernel,
        out_shape=jax.ShapeDtypeStruct((count, width), BF16),
        grid=(steps,),
        in_specs=[
            same((count, width)),
            same((count, width // 2)),
            same((count, width // 2)),
            pl.BlockSpec((GROUP, width), lambda i: (i, 0)),
            weight(0),
            weight(1),
            weight(2),
            *([cols] * 5),
            pl.BlockSpec((per_step, count, count), lambda i: (i, 0, 0)),
        ],
        out_specs=same((count, width)),
        scratch_shapes=[pltpu.VMEM((count, width), F32)],
        compiler_params=params(),
        cost_estimate=pl.CostEstimate(
            flops=2 * count * width * (4 * width + 4 * count * 4),
            bytes_accessed=20 * count * width + 8 * width * width,
            transcendentals=0,
        ),
        name="backward",
    )(tok_col, *flow, in_hbm(w_mix), *[in_hbm(w_qkv)] * 3, *map(in_hbm, saved))


def mix_gradient_kernel(factor, own_ref, other_ref, *refs):
    *flow_refs, own_out, other_out, flow_scr = refs
    bands, owners, cells, share = flow_refs[0].shape
    count = bands * cells
    features = own_ref.shape[-1]
    for k, ref in enumerate(flow_refs):
        cols = slice(k * share, (k + 1) * share)
        for j in range(owners):
            for p in range(bands):
                at = j * count + p * cells
                flow_scr[at : at + cells, cols] = ref[p, j]
    flow = flow_scr[...]
    own = own_ref[...].reshape(owners * count, features)
    other = other_ref[...].reshape(owners * count, features)
    own_out[...] = tn(own, flow) * factor
    other_out[...] = (tn(other, flow) * factor).astype(BF16)


def mix_gradient(own, other, flow_parts, factor):
    owners, count, features = own.shape
    half = flow_parts[0].shape[-1] * len(flow_parts)
    return pl.pallas_call(
        functools.partial(mix_gradient_kernel, factor),
        out_shape=[
            jax.ShapeDtypeStruct((features, half), F32),
            jax.ShapeDtypeStruct((features, half), BF16),
        ],
        scratch_shapes=[pltpu.VMEM((owners * count, half), BF16)],
        compiler_params=params(),
        cost_estimate=pl.CostEstimate(
            flops=4 * owners * count * features * half,
            bytes_accessed=2 * owners * count * (2 * features + half),
            transcendentals=0,
        ),
        name="mix_gradient",
    )(own, other, *flow_parts)


def place_kernel(own_ref, other_ref, out_ref):
    width = out_ref.shape[-1]
    out_ref[:, half_cols(0, width)] = own_ref[...]
    out_ref[:, half_cols(1, width)] = other_ref[...].astype(F32)


def place(own, other):
    rows, half = own.shape
    return call(place_kernel, "place", jax.ShapeDtypeStruct((rows, 2 * half), F32), own, other)


def swap(block):
    return lax.all_to_all(block, "lat", split_axis=0, concat_axis=0, tiled=True)


def from_level(block, offset):
    return lax.ppermute(block, "lev", [(i, i ^ offset) for i in range(lax.axis_size("lev"))])


def add_kernel(own_ref, received_ref, out_ref):
    out_ref[...] = (own_ref[...].astype(F32) + received_ref[...].astype(F32)).astype(BF16)


def add(own, received):
    return call(add_kernel, "add", jax.ShapeDtypeStruct(own.shape, BF16), own, received)


def pair_total(own, other):
    return add(own, from_level(other, 1))


def before_last(total):
    offset = 2
    while 2 * offset < lax.axis_size("lev"):
        total = add(total, from_level(total, offset))
        offset *= 2
    return total, from_level(total, offset)


def add_flow_kernel(own_ref, received_ref, _, out_ref, *part_refs):
    total = (own_ref[...].astype(F32) + received_ref[...].astype(F32)).astype(BF16)
    out_ref[...] = total
    share = part_refs[0].shape[-1]
    for k, ref in enumerate(part_refs):
        ref[...] = total[:, :, k * share : (k + 1) * share]


def add_flow(own, received, after):
    owners, cells, half = own.shape
    whole = pl.BlockSpec(memory_space=pltpu.VMEM)
    part = jax.ShapeDtypeStruct((owners, cells, half // 2), BF16)
    return pl.pallas_call(
        add_flow_kernel,
        out_shape=[jax.ShapeDtypeStruct(own.shape, BF16), part, part],
        in_specs=[whole, whole, pl.BlockSpec(memory_space=pl.ANY)],
        out_specs=[whole] * 3,
        compiler_params=params(),
        name="add_flow",
    )(own, received, after)


def add_mixed_kernel(own_ref, received_ref, _, *out_refs):
    for t, out_ref in enumerate(out_refs):
        band = lax.axis_index("lat") ^ t
        out_ref[...] = (own_ref[band].astype(F32) + received_ref[band].astype(F32)).astype(BF16)


def add_mixed(own, received, after):
    owners, cells, half = own.shape
    whole = pl.BlockSpec(memory_space=pltpu.VMEM)
    return pl.pallas_call(
        add_mixed_kernel,
        out_shape=[jax.ShapeDtypeStruct((cells, half), BF16)] * owners,
        in_specs=[whole, whole, pl.BlockSpec(memory_space=pl.ANY)],
        out_specs=[whole] * owners,
        compiler_params=params(),
        name="add_mixed",
    )(own, received, after)


def join_kernel(*refs):
    for t, ref in enumerate(refs[:-1]):
        refs[-1][t] = ref[...]


def to_bands(parts):
    owners = len(parts)
    cells, half = parts[0].shape
    received = [parts[0]] + [
        lax.ppermute(parts[t], "lat", [(i, i ^ t) for i in range(owners)])
        for t in range(1, owners)
    ]
    return call(
        join_kernel, "join", jax.ShapeDtypeStruct((owners, cells, half), BF16), *received
    )


def on_device(tokens, key_mask, w_qkv, w_mix, level_scale, cotangent):
    batch, _, rows, lon, width = tokens.shape
    owners = lax.axis_size("lat")
    parts = owners // batch
    chunk = lon // parts
    cells = rows * chunk
    count = batch * rows * lon
    half = width // 2
    tok_band = tokens.reshape(batch, rows, parts, chunk, width)
    cot_band = cotangent.reshape(batch, rows, parts, chunk, width)
    w_mix = w_mix.reshape(width, width)

    tok_send, cot_own, cot_other = pack(tok_band, cot_band, level_scale)
    tok_col = swap(tok_send).reshape(count, width)
    flow_band, *flow_parts = add_flow(*before_last(pair_total(cot_own, cot_other)), tok_col)
    flow_own = swap(flow_band).reshape(count, half)
    flow = (flow_own, from_level(flow_own, 1))
    flow_parts = [lax.all_gather(part, "lat", axis=0) for part in flow_parts]

    *saved, attended, mix_own, mix_other = forward(
        tok_col, key_mask, w_qkv, w_mix, chunk, owners
    )
    attended = swap(attended)
    mix_terms = before_last(pair_total(mix_own, mix_other))
    back_col = backward(tok_col, flow, w_mix, w_qkv, saved)
    back = swap(back_col.reshape(owners, cells, width))
    mix_terms = [term.reshape(owners, cells, half) for term in mix_terms]
    mix_band = to_bands(add_mixed(*mix_terms, back_col))
    output = make_output(tok_band, level_scale, (mix_band, from_level(mix_band, 1)))
    d_tokens = make_gradient(cot_band, back)

    factor = 1.0 / math.sqrt(count * owners)
    grad_own, grad_other = mix_gradient(attended, from_level(attended, 1), flow_parts, factor)
    mix_grad = place(grad_own, from_level(grad_other, 1))
    return (
        output.reshape(tokens.shape),
        d_tokens.reshape(tokens.shape),
        mix_grad.reshape(1, width // owners, width),
    )


def solution(mesh):
    return jax.shard_map(
        on_device,
        mesh=mesh,
        in_specs=(
            P(None, "lev", "lat", None, None),
            P(),
            P(),
            P("lev", None, None),
            P("lev", None),
            P(None, "lev", "lat", None, None),
        ),
        out_specs=(
            P(None, "lev", "lat", None, None),
            P(None, "lev", "lat", None, None),
            P("lev", "lat", None),
        ),
        check_vma=False,
    )
```

```python
import functools
import math

import jax
import jax.numpy as jnp
from jax import lax
from jax.experimental import pallas as pl
from jax.experimental.pallas import tpu as pltpu
from jax.sharding import PartitionSpec as P

HEADS = 16
GROUP = 256

epsilon = 1e-06
score_scale = 0.25

F32 = jnp.float32
BF16 = jnp.bfloat16


def nn(a, b):
    return lax.dot_general(a, b, (((1,), (0,)), ((), ())), preferred_element_type=F32)


def nt(a, b):
    return lax.dot_general(a, b, (((1,), (1,)), ((), ())), preferred_element_type=F32)


def tn(a, b):
    return lax.dot_general(a, b, (((0,), (0,)), ((), ())), preferred_element_type=F32)


def block_mean(head_width):
    row = lax.broadcasted_iota(jnp.int32, (GROUP, GROUP), 0) // head_width
    col = lax.broadcasted_iota(jnp.int32, (GROUP, GROUP), 1) // head_width
    return jnp.where(row == col, 1.0 / head_width, 0.0).astype(BF16)


def params():
    return pltpu.CompilerParams(vmem_limit_bytes=36 * 1024 * 1024)


def half_cols(which, width):
    half = width // 2
    core = lax.axis_index("lev") % 2
    return pl.ds(pl.multiple_of((core ^ which) * half, half), half)


def in_hbm(array):
    return pltpu.with_memory_space_constraint(array, pltpu.HBM)


def call(kernel, name, out_shape, *operands):
    return pl.pallas_call(
        kernel, out_shape=out_shape, compiler_params=params(), name=name
    )(*operands)


def pack_kernel(tok_ref, cot_ref, gain_ref, tok_out, *cot_outs):
    batch, rows, parts, chunk, width = tok_ref.shape
    for b in range(batch):
        for q in range(parts):
            for r in range(rows):
                tok_out[b * parts + q, r * chunk : (r + 1) * chunk, :] = tok_ref[b, r, q]
    for s in range(2):
        cols = half_cols(s, width)
        gain = gain_ref[:, cols]
        for b in range(batch):
            for q in range(parts):
                for r in range(rows):
                    piece = cot_ref[b, r, q, :, cols].astype(F32)
                    cot_outs[s][b * parts + q, r * chunk : (r + 1) * chunk, :] = (
                        piece * gain
                    ).astype(BF16)


def pack(tokens, cot, gain):
    batch, rows, parts, chunk, width = tokens.shape
    shape = (batch * parts, rows * chunk)
    return call(
        pack_kernel,
        "pack",
        [jax.ShapeDtypeStruct(shape + (width,), BF16)]
        + [jax.ShapeDtypeStruct(shape + (width // 2,), BF16)] * 2,
        in_hbm(tokens),
        in_hbm(cot),
        in_hbm(gain),
    )


def output_kernel(tok_ref, gain_ref, own_ref, other_ref, out_ref):
    batch, rows, parts, chunk, width = tok_ref.shape
    for s, ref in enumerate((own_ref, other_ref)):
        cols = half_cols(s, width)
        gain = gain_ref[:, cols]
        for t in range(batch * parts):
            b, q = t // parts, t % parts
            for r in range(rows):
                mixed = ref[t, r * chunk : (r + 1) * chunk, :].astype(F32)
                out_ref[b, r, q, :, cols] = (
                    tok_ref[b, r, q, :, cols].astype(F32) + gain * mixed
                ).astype(BF16)


def make_output(tokens, gain, mixed):
    return call(
        output_kernel,
        "make_output",
        jax.ShapeDtypeStruct(tokens.shape, BF16),
        tokens,
        gain,
        *mixed,
    )


def gradient_kernel(cot_ref, back_ref, out_ref):
    batch, rows, parts, chunk, width = cot_ref.shape
    for b in range(batch):
        for q in range(parts):
            for r in range(rows):
                back = back_ref[b * parts + q, r * chunk : (r + 1) * chunk, :width].astype(F32)
                out_ref[b, r, q] = (cot_ref[b, r, q].astype(F32) + back).astype(BF16)


def make_gradient(cot, back):
    return call(
        gradient_kernel, "make_gradient", jax.ShapeDtypeStruct(cot.shape, BF16), cot, back
    )


def by_head(tile, lane):
    zero = jnp.zeros_like(tile)
    return jnp.concatenate([jnp.where(lane == 0, tile, zero), jnp.where(lane == 1, tile, zero)], axis=0)


def one_head(stacked, lane):
    count = lane.shape[0]
    return jnp.where(lane == 0, stacked[:count], stacked[count:])


def side_by_side(stacked):
    count = stacked.shape[0] // 2
    return jnp.concatenate([stacked[:count], stacked[count:]], axis=1)


def forward_kernel(
    samples, lat_count, chunk, owners,
    tok_ref, mask_ref, wq_ref, wk_ref, wv_ref, wm_ref,
    qn_ref, kn_ref, v_ref, rq_ref, rk_ref, ri_ref, p_ref, att_ref, own_ref, other_ref,
    normed_ref, acc_ref, keep_ref,
):
    step = pl.program_id(0)
    count, width = normed_ref.shape
    head_width = width // HEADS

    @pl.when(step == 0)
    def _():
        x = tok_ref[...].astype(F32)
        rx = lax.rsqrt(jnp.mean(x * x, axis=-1, keepdims=True) + epsilon)
        normed_ref[...] = (x * rx).astype(BF16)
        acc_ref[...] = jnp.zeros_like(acc_ref)
        spread = (
            lax.broadcasted_iota(jnp.int32, (lat_count, count), 0)
            == lax.broadcasted_iota(jnp.int32, (lat_count, count), 1) // chunk
        ).astype(F32)
        per_sample = nn(mask_ref[...].astype(F32), spread)
        mine = lax.axis_index("lat") // (owners // samples)
        pick = lax.broadcasted_iota(jnp.int32, (samples, count), 0) == mine
        valid = jnp.sum(jnp.where(pick, per_sample, 0.0), axis=0, keepdims=True)
        same = (
            lax.broadcasted_iota(jnp.int32, (count, count), 0) % chunk
            == lax.broadcasted_iota(jnp.int32, (count, count), 1) % chunk
        )
        keep_ref[...] = jnp.where(same, valid, 0.0)

    normed = normed_ref[...]
    mean_mat = block_mean(head_width)
    q = nn(normed, wq_ref[...])
    k = nn(normed, wk_ref[...])
    v = nn(normed, wv_ref[...]).astype(BF16)
    rq = lax.rsqrt(nn((q * q).astype(BF16), mean_mat) + epsilon)
    rk = lax.rsqrt(nn((k * k).astype(BF16), mean_mat) + epsilon)
    qn = (q * rq).astype(BF16)
    kn = (k * rk).astype(BF16)
    qn_ref[...] = qn
    kn_ref[...] = kn
    v_ref[...] = v
    rq_ref[...] = rq.astype(BF16)
    rk_ref[...] = rk.astype(BF16)
    keep = keep_ref[...]
    keep = jnp.concatenate([keep, keep], axis=0)
    lane = lax.broadcasted_iota(jnp.int32, (count, 128), 1) // head_width
    ones = jnp.ones((count, 128), BF16)
    tiles = []
    for t in range(GROUP // 128):
        cols = slice(t * 128, (t + 1) * 128)
        v_ones = jnp.concatenate([v[:, cols], ones], axis=1)
        e = jnp.exp(nt(by_head(qn[:, cols] * score_scale, lane), kn[:, cols])) * keep
        e = e.astype(BF16)
        p_ref[t] = e
        o = nn(e, v_ones)
        inverse = 1.0 / o[:, 128:]
        tiles.append(one_head(o[:, :128] * inverse, lane))
        ri_ref[:, cols] = one_head(inverse, lane)
    att = jnp.concatenate(tiles, axis=1).astype(BF16)
    features = att_ref.shape[-1]
    for f in range(GROUP // features):
        att_ref[f] = att[:, f * features : (f + 1) * features]
    acc_ref[...] += nn(att, wm_ref[...])

    @pl.when(step == pl.num_programs(0) - 1)
    def _():
        for s, ref in enumerate((own_ref, other_ref)):
            ref[...] = acc_ref[:, half_cols(s, width)].astype(BF16)


def forward(tok_col, key_mask, w_qkv, w_mix, chunk, owners):
    count, width = tok_col.shape
    samples, lat_count = key_mask.shape
    steps = width // GROUP
    features = width // owners
    same = lambda shape: pl.BlockSpec(shape, lambda i: (0, 0))
    cols = pl.BlockSpec((count, GROUP), lambda i: (0, i))
    weight = lambda which: pl.BlockSpec((width, GROUP), lambda i: (0, i + which * steps))
    return pl.pallas_call(
        functools.partial(forward_kernel, samples, lat_count, chunk, owners),
        out_shape=(
            [pltpu.HBM((count, width), BF16)] * 5
            + [pltpu.HBM((count, width), F32)]
            + [pltpu.HBM((width // 128, 2 * count, count), BF16)]
            + [jax.ShapeDtypeStruct((owners, count, features), BF16)]
            + [jax.ShapeDtypeStruct((count, width // 2), BF16)] * 2
        ),
        grid=(steps,),
        in_specs=[
            same((count, width)),
            same((samples, lat_count)),
            weight(0),
            weight(1),
            weight(2),
            pl.BlockSpec((GROUP, width), lambda i: (i, 0)),
        ],
        out_specs=(
            [cols] * 6
            + [pl.BlockSpec((GROUP // 128, 2 * count, count), lambda i: (i, 0, 0))]
            + [pl.BlockSpec((GROUP // features, count, features), lambda i: (i, 0, 0))]
            + [same((count, width // 2))] * 2
        ),
        scratch_shapes=[
            pltpu.VMEM((count, width), BF16),
            pltpu.VMEM((count, width), F32),
            pltpu.VMEM((count, count), F32),
        ],
        compiler_params=params(),
        cost_estimate=pl.CostEstimate(
            flops=2 * count * width * (4 * width + 2 * count * 4),
            bytes_accessed=20 * count * width + 8 * width * width,
            transcendentals=HEADS * count * count,
        ),
        name="forward",
    )(tok_col, key_mask, *[in_hbm(w_qkv)] * 3, in_hbm(w_mix))


def backward_kernel(
    tok_ref, own_ref, other_ref, wm_ref, wq_ref, wk_ref, wv_ref,
    qn_ref, kn_ref, v_ref, rq_ref, rk_ref, ri_ref, p_ref, _,
    out_ref, acc_ref,
):
    step = pl.program_id(0)
    count, width = acc_ref.shape
    head_width = width // HEADS
    d_att = nt(own_ref[...], wm_ref[:, half_cols(0, width)])
    d_att += nt(other_ref[...], wm_ref[:, half_cols(1, width)])
    inverse = ri_ref[...]
    d_att = (d_att * inverse).astype(BF16)
    qn, kn, v = qn_ref[...], kn_ref[...], v_ref[...]
    lane = lax.broadcasted_iota(jnp.int32, (count, 128), 1) // head_width
    dq_tiles, dk_tiles, dv_tiles = [], [], []
    for t in range(GROUP // 128):
        cols = slice(t * 128, (t + 1) * 128)
        d_t = d_att[:, cols]
        d_p = nt(by_head(d_t, lane), v[:, cols])
        e = p_ref[t]
        e_wide = e.astype(F32)
        first = t * 128
        second = first + head_width
        row_inverse = jnp.concatenate(
            [inverse[:, first : first + 1], inverse[:, second : second + 1]], axis=0
        )
        weighted = e_wide * d_p
        inner = jnp.sum(weighted, axis=-1, keepdims=True) * row_inverse
        d_s = (weighted - e_wide * inner).astype(BF16)
        dq_tiles.append(one_head(nn(d_s, kn[:, cols]), lane) * score_scale)
        dk_tiles.append(one_head(tn(side_by_side(d_s), qn[:, cols]), lane) * score_scale)
        dv_tiles.append(one_head(tn(side_by_side(e), d_t), lane))
    mean_mat = block_mean(head_width)
    dq = jnp.concatenate(dq_tiles, axis=1)
    dk = jnp.concatenate(dk_tiles, axis=1)
    dv = jnp.concatenate(dv_tiles, axis=1).astype(BF16)

    def through_norm(upstream, unit, factor):
        unit = unit.astype(F32)
        inner = nn((upstream * unit).astype(BF16), mean_mat)
        return (factor.astype(F32) * (upstream - unit * inner)).astype(BF16)

    gq = through_norm(dq, qn, rq_ref[...])
    gk = through_norm(dk, kn, rk_ref[...])
    total = nt(gq, wq_ref[...]) + nt(gk, wk_ref[...]) + nt(dv, wv_ref[...])

    @pl.when(step == 0)
    def _():
        acc_ref[...] = total

    @pl.when(step > 0)
    def _():
        acc_ref[...] += total

    @pl.when(step == pl.num_programs(0) - 1)
    def _():
        x = tok_ref[...].astype(F32)
        rx = lax.rsqrt(jnp.mean(x * x, axis=-1, keepdims=True) + epsilon)
        d = acc_ref[...]
        inner = jnp.mean(d * x, axis=-1, keepdims=True)
        out_ref[...] = (rx * d - x * (rx * rx * rx * inner)).astype(BF16)


def backward(tok_col, flow, w_mix, w_qkv, saved, after):
    count, width = tok_col.shape
    steps = width // GROUP
    same = lambda shape: pl.BlockSpec(shape, lambda i: (0, 0))
    cols = pl.BlockSpec((count, GROUP), lambda i: (0, i))
    weight = lambda which: pl.BlockSpec((width, GROUP), lambda i: (0, i + which * steps))
    return pl.pallas_call(
        backward_kernel,
        out_shape=jax.ShapeDtypeStruct((count, width), BF16),
        grid=(steps,),
        in_specs=[
            same((count, width)),
            same((count, width // 2)),
            same((count, width // 2)),
            pl.BlockSpec((GROUP, width), lambda i: (i, 0)),
            weight(0),
            weight(1),
            weight(2),
            *([cols] * 6),
            pl.BlockSpec((GROUP // 128, 2 * count, count), lambda i: (i, 0, 0)),
            pl.BlockSpec(memory_space=pl.ANY),
        ],
        out_specs=same((count, width)),
        scratch_shapes=[pltpu.VMEM((count, width), F32)],
        compiler_params=params(),
        cost_estimate=pl.CostEstimate(
            flops=2 * count * width * (4 * width + 4 * count * 4),
            bytes_accessed=20 * count * width + 8 * width * width,
            transcendentals=0,
        ),
        name="backward",
    )(tok_col, *flow, in_hbm(w_mix), *[in_hbm(w_qkv)] * 3, *map(in_hbm, saved), after)


def mix_gradient_kernel(factor, own_ref, other_ref, flow_ref, own_out, other_out, flow_scr):
    bands, owners, cells, half = flow_ref.shape
    count = bands * cells
    features = own_ref.shape[-1]
    for j in range(owners):
        for p in range(bands):
            at = j * count + p * cells
            flow_scr[at : at + cells, :] = flow_ref[p, j]
    flow = flow_scr[...]
    own = own_ref[...].reshape(owners * count, features)
    other = other_ref[...].reshape(owners * count, features)
    own_out[...] = tn(own, flow) * factor
    other_out[...] = (tn(other, flow) * factor).astype(BF16)


def mix_gradient(own, other, flow_all, factor):
    owners, count, features = own.shape
    half = flow_all.shape[-1]
    return pl.pallas_call(
        functools.partial(mix_gradient_kernel, factor),
        out_shape=[
            jax.ShapeDtypeStruct((features, half), F32),
            jax.ShapeDtypeStruct((features, half), BF16),
        ],
        scratch_shapes=[pltpu.VMEM((owners * count, half), BF16)],
        compiler_params=params(),
        cost_estimate=pl.CostEstimate(
            flops=4 * owners * count * features * half,
            bytes_accessed=2 * owners * count * (2 * features + half),
            transcendentals=0,
        ),
        name="mix_gradient",
    )(own, other, flow_all)


def place_kernel(own_ref, other_ref, out_ref):
    width = out_ref.shape[-1]
    out_ref[:, half_cols(0, width)] = own_ref[...]
    out_ref[:, half_cols(1, width)] = other_ref[...].astype(F32)


def place(own, other):
    rows, half = own.shape
    return call(place_kernel, "place", jax.ShapeDtypeStruct((rows, 2 * half), F32), own, other)


def swap(block):
    return lax.all_to_all(block, "lat", split_axis=0, concat_axis=0, tiled=True)


def from_level(block, offset):
    return lax.ppermute(block, "lev", [(i, i ^ offset) for i in range(lax.axis_size("lev"))])


def add_kernel(own_ref, received_ref, out_ref):
    out_ref[...] = (own_ref[...].astype(F32) + received_ref[...].astype(F32)).astype(BF16)


def add(own, received):
    return call(add_kernel, "add", jax.ShapeDtypeStruct(own.shape, BF16), own, received)


def pair_total(own, other):
    return add(own, from_level(other, 1))


def before_last(total):
    offset = 2
    while 2 * offset < lax.axis_size("lev"):
        total = add(total, from_level(total, offset))
        offset *= 2
    return total, from_level(total, offset)


def add_flow_kernel(own_ref, received_ref, _, out_ref):
    add_kernel(own_ref, received_ref, out_ref)


def add_flow(own, received, after):
    whole = pl.BlockSpec(memory_space=pltpu.VMEM)
    return pl.pallas_call(
        add_flow_kernel,
        out_shape=jax.ShapeDtypeStruct(own.shape, BF16),
        in_specs=[whole, whole, pl.BlockSpec(memory_space=pl.ANY)],
        out_specs=whole,
        compiler_params=params(),
        name="add_flow",
    )(own, received, after)


def add_mixed_kernel(own_ref, received_ref, back_ref, out_ref):
    width = back_ref.shape[-1]
    out_ref[:, :width] = back_ref[...]
    out_ref[:, width:] = (own_ref[...].astype(F32) + received_ref[...].astype(F32)).astype(BF16)


def add_mixed(own, received, back):
    count, width = back.shape
    shape = jax.ShapeDtypeStruct((count, width + own.shape[-1]), BF16)
    return call(add_mixed_kernel, "add_mixed", shape, own, received, back)


def cut_kernel(in_ref, out_ref):
    out_ref[...] = in_ref[:, :, in_ref.shape[-1] - out_ref.shape[-1] :]


def cut_mixed(received):
    owners, cells, wide = received.shape
    shape = jax.ShapeDtypeStruct((owners, cells, wide // 3), BF16)
    return call(cut_kernel, "cut_mixed", shape, received)


def on_device(tokens, key_mask, w_qkv, w_mix, level_scale, cotangent):
    batch, _, rows, lon, width = tokens.shape
    owners = lax.axis_size("lat")
    parts = owners // batch
    chunk = lon // parts
    cells = rows * chunk
    count = batch * rows * lon
    half = width // 2
    tok_band = tokens.reshape(batch, rows, parts, chunk, width)
    cot_band = cotangent.reshape(batch, rows, parts, chunk, width)
    w_mix = w_mix.reshape(width, width)

    tok_send, cot_own, cot_other = pack(tok_band, cot_band, level_scale)
    tok_col = swap(tok_send).reshape(count, width)
    flow_band = add_flow(*before_last(pair_total(cot_own, cot_other)), tok_col)
    flow_own = swap(flow_band).reshape(count, half)
    flow = (flow_own, from_level(flow_own, 1))
    flow_all = lax.all_gather(flow_band, "lat", axis=0)

    *saved, attended, mix_own, mix_other = forward(
        tok_col, key_mask, w_qkv, w_mix, chunk, owners
    )
    attended = swap(attended)
    mix_terms = before_last(pair_total(mix_own, mix_other))
    back_col = backward(tok_col, flow, w_mix, w_qkv, saved, mix_terms[0])
    back = swap(add_mixed(*mix_terms, back_col).reshape(owners, cells, width + half))
    d_tokens = make_gradient(cot_band, back)
    mix_band = cut_mixed(back)
    output = make_output(tok_band, level_scale, (mix_band, from_level(mix_band, 1)))

    factor = 1.0 / math.sqrt(count * owners)
    grad_own, grad_other = mix_gradient(attended, from_level(attended, 1), flow_all, factor)
    mix_grad = place(grad_own, from_level(grad_other, 1))
    return (
        output.reshape(tokens.shape),
        d_tokens.reshape(tokens.shape),
        mix_grad.reshape(1, width // owners, width),
    )


def solution(mesh):
    return jax.shard_map(
        on_device,
        mesh=mesh,
        in_specs=(
            P(None, "lev", "lat", None, None),
            P(),
            P(),
            P("lev", None, None),
            P("lev", None),
            P(None, "lev", "lat", None, None),
        ),
        out_specs=(
            P(None, "lev", "lat", None, None),
            P(None, "lev", "lat", None, None),
            P("lev", "lat", None),
        ),
        check_vma=False,
    )
```

```python
import functools
import math

import jax
import jax.numpy as jnp
from jax import lax
from jax.experimental import pallas as pl
from jax.experimental.pallas import tpu as pltpu
from jax.sharding import PartitionSpec as P

HEADS = 16
GROUP = 256

epsilon = 1e-06
score_scale = 0.25

F32 = jnp.float32
BF16 = jnp.bfloat16


def nn(a, b):
    return lax.dot_general(a, b, (((1,), (0,)), ((), ())), preferred_element_type=F32)


def nt(a, b):
    return lax.dot_general(a, b, (((1,), (1,)), ((), ())), preferred_element_type=F32)


def tn(a, b):
    return lax.dot_general(a, b, (((0,), (0,)), ((), ())), preferred_element_type=F32)


def block_mean(head_width):
    row = lax.broadcasted_iota(jnp.int32, (GROUP, GROUP), 0) // head_width
    col = lax.broadcasted_iota(jnp.int32, (GROUP, GROUP), 1) // head_width
    return jnp.where(row == col, 1.0 / head_width, 0.0).astype(BF16)


def params():
    return pltpu.CompilerParams(vmem_limit_bytes=36 * 1024 * 1024)


def half_cols(which, width):
    half = width // 2
    core = lax.axis_index("lev") % 2
    return pl.ds(pl.multiple_of((core ^ which) * half, half), half)


def in_hbm(array):
    return pltpu.with_memory_space_constraint(array, pltpu.HBM)


def call(kernel, name, out_shape, *operands):
    return pl.pallas_call(
        kernel, out_shape=out_shape, compiler_params=params(), name=name
    )(*operands)


def pack_kernel(tok_ref, cot_ref, gain_ref, tok_out, *cot_outs):
    batch, rows, parts, chunk, width = tok_ref.shape
    for b in range(batch):
        for q in range(parts):
            for r in range(rows):
                tok_out[b * parts + q, r * chunk : (r + 1) * chunk, :] = tok_ref[b, r, q]
    for s in range(2):
        cols = half_cols(s, width)
        gain = gain_ref[:, cols]
        for b in range(batch):
            for q in range(parts):
                for r in range(rows):
                    piece = cot_ref[b, r, q, :, cols].astype(F32)
                    cot_outs[s][b * parts + q, r * chunk : (r + 1) * chunk, :] = (
                        piece * gain
                    ).astype(BF16)


def pack(tokens, cot, gain):
    batch, rows, parts, chunk, width = tokens.shape
    shape = (batch * parts, rows * chunk)
    return call(
        pack_kernel,
        "pack",
        [jax.ShapeDtypeStruct(shape + (width,), BF16)]
        + [jax.ShapeDtypeStruct(shape + (width // 2,), BF16)] * 2,
        in_hbm(tokens),
        in_hbm(cot),
        in_hbm(gain),
    )


def output_kernel(tok_ref, gain_ref, own_ref, other_ref, out_ref):
    batch, rows, parts, chunk, width = tok_ref.shape
    for s, ref in enumerate((own_ref, other_ref)):
        cols = half_cols(s, width)
        gain = gain_ref[:, cols]
        for t in range(batch * parts):
            b, q = t // parts, t % parts
            for r in range(rows):
                mixed = ref[t, r * chunk : (r + 1) * chunk, :].astype(F32)
                out_ref[b, r, q, :, cols] = (
                    tok_ref[b, r, q, :, cols].astype(F32) + gain * mixed
                ).astype(BF16)


def make_output(tokens, gain, mixed):
    return call(
        output_kernel,
        "make_output",
        jax.ShapeDtypeStruct(tokens.shape, BF16),
        tokens,
        gain,
        *mixed,
    )


def gradient_kernel(cot_ref, back_ref, out_ref):
    batch, rows, parts, chunk, width = cot_ref.shape
    for b in range(batch):
        for q in range(parts):
            for r in range(rows):
                back = back_ref[b * parts + q, r * chunk : (r + 1) * chunk, :width].astype(F32)
                out_ref[b, r, q] = (cot_ref[b, r, q].astype(F32) + back).astype(BF16)


def make_gradient(cot, back):
    return call(
        gradient_kernel, "make_gradient", jax.ShapeDtypeStruct(cot.shape, BF16), cot, back
    )


def by_head(tile, lane):
    zero = jnp.zeros_like(tile)
    return jnp.concatenate([jnp.where(lane == 0, tile, zero), jnp.where(lane == 1, tile, zero)], axis=0)


def one_head(stacked, lane):
    count = lane.shape[0]
    return jnp.where(lane == 0, stacked[:count], stacked[count:])


def side_by_side(stacked):
    count = stacked.shape[0] // 2
    return jnp.concatenate([stacked[:count], stacked[count:]], axis=1)


def forward_kernel(
    samples, lat_count, chunk, owners,
    tok_ref, mask_ref, wq_ref, wk_ref, wv_ref, wm_ref,
    qn_ref, kn_ref, v_ref, rq_ref, rk_ref, ri_ref, p_ref, att_ref, own_ref, other_ref,
    normed_ref, acc_ref, keep_ref,
):
    step = pl.program_id(0)
    count, width = normed_ref.shape
    head_width = width // HEADS

    @pl.when(step == 0)
    def _():
        x = tok_ref[...].astype(F32)
        rx = lax.rsqrt(jnp.mean(x * x, axis=-1, keepdims=True) + epsilon)
        normed_ref[...] = (x * rx).astype(BF16)
        acc_ref[...] = jnp.zeros_like(acc_ref)
        spread = (
            lax.broadcasted_iota(jnp.int32, (lat_count, count), 0)
            == lax.broadcasted_iota(jnp.int32, (lat_count, count), 1) // chunk
        ).astype(F32)
        per_sample = nn(mask_ref[...].astype(F32), spread)
        mine = lax.axis_index("lat") // (owners // samples)
        pick = lax.broadcasted_iota(jnp.int32, (samples, count), 0) == mine
        valid = jnp.sum(jnp.where(pick, per_sample, 0.0), axis=0, keepdims=True)
        same = (
            lax.broadcasted_iota(jnp.int32, (count, count), 0) % chunk
            == lax.broadcasted_iota(jnp.int32, (count, count), 1) % chunk
        )
        keep_ref[...] = jnp.where(same, valid, 0.0)

    normed = normed_ref[...]
    mean_mat = block_mean(head_width)
    q = nn(normed, wq_ref[...])
    k = nn(normed, wk_ref[...])
    v = nn(normed, wv_ref[...]).astype(BF16)
    rq = lax.rsqrt(nn((q * q).astype(BF16), mean_mat) + epsilon)
    rk = lax.rsqrt(nn((k * k).astype(BF16), mean_mat) + epsilon)
    qn = (q * rq).astype(BF16)
    kn = (k * rk).astype(BF16)
    qn_ref[...] = qn
    kn_ref[...] = kn
    v_ref[...] = v
    rq_ref[...] = rq.astype(BF16)
    rk_ref[...] = rk.astype(BF16)
    keep = keep_ref[...]
    keep = jnp.concatenate([keep, keep], axis=0)
    lane = lax.broadcasted_iota(jnp.int32, (count, 128), 1) // head_width
    ones = jnp.ones((count, 128), BF16)
    tiles = []
    for t in range(GROUP // 128):
        cols = slice(t * 128, (t + 1) * 128)
        v_ones = jnp.concatenate([v[:, cols], ones], axis=1)
        e = jnp.exp(nt(by_head(qn[:, cols] * score_scale, lane), kn[:, cols])) * keep
        e = e.astype(BF16)
        p_ref[t] = e
        o = nn(e, v_ones)
        inverse = 1.0 / o[:, 128:]
        tiles.append(one_head(o[:, :128] * inverse, lane))
        ri_ref[:, cols] = one_head(inverse, lane)
    att = jnp.concatenate(tiles, axis=1).astype(BF16)
    features = att_ref.shape[-1]
    for f in range(GROUP // features):
        att_ref[f] = att[:, f * features : (f + 1) * features]
    acc_ref[...] += nn(att, wm_ref[...])

    @pl.when(step == pl.num_programs(0) - 1)
    def _():
        for s, ref in enumerate((own_ref, other_ref)):
            ref[...] = acc_ref[:, half_cols(s, width)].astype(BF16)


def forward(tok_col, key_mask, w_qkv, w_mix, chunk, owners):
    count, width = tok_col.shape
    samples, lat_count = key_mask.shape
    steps = width // GROUP
    features = width // owners
    same = lambda shape: pl.BlockSpec(shape, lambda i: (0, 0))
    cols = pl.BlockSpec((count, GROUP), lambda i: (0, i))
    weight = lambda which: pl.BlockSpec((width, GROUP), lambda i: (0, i + which * steps))
    return pl.pallas_call(
        functools.partial(forward_kernel, samples, lat_count, chunk, owners),
        out_shape=(
            [pltpu.HBM((count, width), BF16)] * 5
            + [pltpu.HBM((count, width), F32)]
            + [pltpu.HBM((width // 128, 2 * count, count), BF16)]
            + [jax.ShapeDtypeStruct((owners, count, features), BF16)]
            + [jax.ShapeDtypeStruct((count, width // 2), BF16)] * 2
        ),
        grid=(steps,),
        in_specs=[
            same((count, width)),
            same((samples, lat_count)),
            weight(0),
            weight(1),
            weight(2),
            pl.BlockSpec((GROUP, width), lambda i: (i, 0)),
        ],
        out_specs=(
            [cols] * 6
            + [pl.BlockSpec((GROUP // 128, 2 * count, count), lambda i: (i, 0, 0))]
            + [pl.BlockSpec((GROUP // features, count, features), lambda i: (i, 0, 0))]
            + [same((count, width // 2))] * 2
        ),
        scratch_shapes=[
            pltpu.VMEM((count, width), BF16),
            pltpu.VMEM((count, width), F32),
            pltpu.VMEM((count, count), F32),
        ],
        compiler_params=params(),
        cost_estimate=pl.CostEstimate(
            flops=2 * count * width * (4 * width + 2 * count * 4),
            bytes_accessed=20 * count * width + 8 * width * width,
            transcendentals=HEADS * count * count,
        ),
        name="forward",
    )(tok_col, key_mask, *[in_hbm(w_qkv)] * 3, in_hbm(w_mix))


def backward_kernel(
    tok_ref, own_ref, other_ref, wm_ref, wq_ref, wk_ref, wv_ref,
    qn_ref, kn_ref, v_ref, rq_ref, rk_ref, ri_ref, p_ref, _,
    out_ref, acc_ref,
):
    step = pl.program_id(0)
    count, width = acc_ref.shape
    head_width = width // HEADS
    d_att = nt(own_ref[...], wm_ref[:, half_cols(0, width)])
    d_att += nt(other_ref[...], wm_ref[:, half_cols(1, width)])
    inverse = ri_ref[...]
    d_att = (d_att * inverse).astype(BF16)
    qn, kn, v = qn_ref[...], kn_ref[...], v_ref[...]
    lane = lax.broadcasted_iota(jnp.int32, (count, 128), 1) // head_width
    dq_tiles, dk_tiles, dv_tiles = [], [], []
    for t in range(GROUP // 128):
        cols = slice(t * 128, (t + 1) * 128)
        d_t = d_att[:, cols]
        d_p = nt(by_head(d_t, lane), v[:, cols])
        e = p_ref[t]
        e_wide = e.astype(F32)
        first = t * 128
        second = first + head_width
        row_inverse = jnp.concatenate(
            [inverse[:, first : first + 1], inverse[:, second : second + 1]], axis=0
        )
        weighted = e_wide * d_p
        inner = jnp.sum(weighted, axis=-1, keepdims=True) * row_inverse
        d_s = (weighted - e_wide * inner).astype(BF16)
        dq_tiles.append(one_head(nn(d_s, kn[:, cols]), lane) * score_scale)
        dk_tiles.append(one_head(tn(side_by_side(d_s), qn[:, cols]), lane) * score_scale)
        dv_tiles.append(one_head(tn(side_by_side(e), d_t), lane))
    mean_mat = block_mean(head_width)
    dq = jnp.concatenate(dq_tiles, axis=1)
    dk = jnp.concatenate(dk_tiles, axis=1)
    dv = jnp.concatenate(dv_tiles, axis=1).astype(BF16)

    def through_norm(upstream, unit, factor):
        unit = unit.astype(F32)
        inner = nn((upstream * unit).astype(BF16), mean_mat)
        return (factor.astype(F32) * (upstream - unit * inner)).astype(BF16)

    gq = through_norm(dq, qn, rq_ref[...])
    gk = through_norm(dk, kn, rk_ref[...])
    total = nt(gq, wq_ref[...]) + nt(gk, wk_ref[...]) + nt(dv, wv_ref[...])

    @pl.when(step == 0)
    def _():
        acc_ref[...] = total

    @pl.when(step > 0)
    def _():
        acc_ref[...] += total

    @pl.when(step == pl.num_programs(0) - 1)
    def _():
        x = tok_ref[...].astype(F32)
        rx = lax.rsqrt(jnp.mean(x * x, axis=-1, keepdims=True) + epsilon)
        d = acc_ref[...]
        inner = jnp.mean(d * x, axis=-1, keepdims=True)
        out_ref[...] = (rx * d - x * (rx * rx * rx * inner)).astype(BF16)


def backward(tok_col, flow, w_mix, w_qkv, saved, after):
    count, width = tok_col.shape
    steps = width // GROUP
    same = lambda shape: pl.BlockSpec(shape, lambda i: (0, 0))
    cols = pl.BlockSpec((count, GROUP), lambda i: (0, i))
    weight = lambda which: pl.BlockSpec((width, GROUP), lambda i: (0, i + which * steps))
    return pl.pallas_call(
        backward_kernel,
        out_shape=jax.ShapeDtypeStruct((count, width), BF16),
        grid=(steps,),
        in_specs=[
            same((count, width)),
            same((count, width // 2)),
            same((count, width // 2)),
            pl.BlockSpec((GROUP, width), lambda i: (i, 0)),
            weight(0),
            weight(1),
            weight(2),
            *([cols] * 6),
            pl.BlockSpec((GROUP // 128, 2 * count, count), lambda i: (i, 0, 0)),
            pl.BlockSpec(memory_space=pl.ANY),
        ],
        out_specs=same((count, width)),
        scratch_shapes=[pltpu.VMEM((count, width), F32)],
        compiler_params=params(),
        cost_estimate=pl.CostEstimate(
            flops=2 * count * width * (4 * width + 4 * count * 4),
            bytes_accessed=20 * count * width + 8 * width * width,
            transcendentals=0,
        ),
        name="backward",
    )(tok_col, *flow, in_hbm(w_mix), *[in_hbm(w_qkv)] * 3, *map(in_hbm, saved), after)


def mix_gradient_kernel(factor, own_flow_ref, other_flow_ref, *refs):
    att_refs, out_refs = refs[: len(refs) // 2], refs[len(refs) // 2 :]
    width = out_refs[0].shape[-1]
    for att_ref, out_ref in zip(att_refs, out_refs):
        att = att_ref[...]
        for s, flow_ref in enumerate((own_flow_ref, other_flow_ref)):
            term = tn(att, flow_ref[...]) * factor
            out_ref[:, half_cols(s, width)] = term.astype(out_ref.dtype)


def mix_gradient(attended, flow, factor):
    rows, features = attended[0].shape
    width = 2 * flow[0].shape[-1]
    out = [jax.ShapeDtypeStruct((features, width), F32)]
    out += [jax.ShapeDtypeStruct((features, width), BF16)] * (len(attended) - 1)
    return pl.pallas_call(
        functools.partial(mix_gradient_kernel, factor),
        out_shape=out,
        compiler_params=params(),
        cost_estimate=pl.CostEstimate(
            flops=2 * rows * features * width * len(attended),
            bytes_accessed=2 * rows * (features * len(attended) + width),
            transcendentals=0,
        ),
        name="mix_gradient",
    )(*flow, *attended)


def chip_rows(array, axis, chip):
    rows = array.shape[axis] // (lax.axis_size("lev") // 2)
    return lax.dynamic_slice_in_dim(array, chip * rows, rows, axis)


def swap(block):
    return lax.all_to_all(block, "lat", split_axis=0, concat_axis=0, tiled=True)


def from_level(block, offset):
    return lax.ppermute(block, "lev", [(i, i ^ offset) for i in range(lax.axis_size("lev"))])


def add_kernel(own_ref, received_ref, out_ref):
    out_ref[...] = (own_ref[...].astype(F32) + received_ref[...].astype(F32)).astype(BF16)


def add(own, received):
    return call(add_kernel, "add", jax.ShapeDtypeStruct(own.shape, BF16), own, received)


def pair_total(own, other):
    return add(own, from_level(other, 1))


def before_last(total):
    offset = 2
    while 2 * offset < lax.axis_size("lev"):
        total = add(total, from_level(total, offset))
        offset *= 2
    return total, from_level(total, offset)


def add_flow_kernel(own_ref, received_ref, _, out_ref):
    add_kernel(own_ref, received_ref, out_ref)


def add_flow(own, received, after):
    whole = pl.BlockSpec(memory_space=pltpu.VMEM)
    return pl.pallas_call(
        add_flow_kernel,
        out_shape=jax.ShapeDtypeStruct(own.shape, BF16),
        in_specs=[whole, whole, pl.BlockSpec(memory_space=pl.ANY)],
        out_specs=whole,
        compiler_params=params(),
        name="add_flow",
    )(own, received, after)


def add_mixed_kernel(own_ref, received_ref, back_ref, out_ref):
    width = back_ref.shape[-1]
    out_ref[:, :width] = back_ref[...]
    out_ref[:, width:] = (own_ref[...].astype(F32) + received_ref[...].astype(F32)).astype(BF16)


def add_mixed(own, received, back):
    count, width = back.shape
    shape = jax.ShapeDtypeStruct((count, width + own.shape[-1]), BF16)
    return call(add_mixed_kernel, "add_mixed", shape, own, received, back)


def cut_kernel(in_ref, _, out_ref):
    out_ref[...] = in_ref[:, :, in_ref.shape[-1] - out_ref.shape[-1] :]


def cut_mixed(received, after):
    owners, cells, wide = received.shape
    whole = pl.BlockSpec(memory_space=pltpu.VMEM)
    return pl.pallas_call(
        cut_kernel,
        out_shape=jax.ShapeDtypeStruct((owners, cells, wide // 3), BF16),
        in_specs=[whole, pl.BlockSpec(memory_space=pl.ANY)],
        out_specs=whole,
        compiler_params=params(),
        name="cut_mixed",
    )(received, after)


def on_device(tokens, key_mask, w_qkv, w_mix, level_scale, cotangent):
    batch, _, rows, lon, width = tokens.shape
    owners = lax.axis_size("lat")
    parts = owners // batch
    chunk = lon // parts
    cells = rows * chunk
    count = batch * rows * lon
    half = width // 2
    tok_band = tokens.reshape(batch, rows, parts, chunk, width)
    cot_band = cotangent.reshape(batch, rows, parts, chunk, width)
    w_mix = w_mix.reshape(width, width)

    tok_send, cot_own, cot_other = pack(tok_band, cot_band, level_scale)
    tok_col = swap(tok_send).reshape(count, width)
    flow_band = add_flow(*before_last(pair_total(cot_own, cot_other)), tok_col)
    flow_own = swap(flow_band).reshape(count, half)
    flow = (flow_own, from_level(flow_own, 1))
    chip = lax.axis_index("lev") // 2
    chips = lax.axis_size("lev") // 2
    flow_rows = lax.all_gather(chip_rows(flow_band, 1, chip), "lat", axis=0)

    *saved, attended, mix_own, mix_other = forward(
        tok_col, key_mask, w_qkv, w_mix, chunk, owners
    )
    attended = swap(attended)
    mix_terms = before_last(pair_total(mix_own, mix_other))
    back_col = backward(tok_col, flow, w_mix, w_qkv, saved, mix_terms[0])
    back = swap(add_mixed(*mix_terms, back_col).reshape(owners, cells, width + half))
    d_tokens = make_gradient(cot_band, back)

    factor = 1.0 / math.sqrt(count * owners)
    flow_rows = jnp.swapaxes(flow_rows, 0, 1).reshape(-1, half)
    features = width // owners
    attended = attended.reshape(owners, owners, cells, features)
    attended = [chip_rows(attended, 2, chip ^ k).reshape(-1, features) for k in range(chips)]
    attended[1:] = [from_level(attended[k], 2 * k) for k in range(1, chips)]
    grads = mix_gradient(attended, (flow_rows, from_level(flow_rows, 1)), factor)
    mix_grad = grads[0]
    for k in range(1, chips):
        mix_grad += from_level(grads[k], 2 * k).astype(F32)

    mix_band = cut_mixed(back, grads[0])
    output = make_output(tok_band, level_scale, (mix_band, from_level(mix_band, 1)))
    return (
        output.reshape(tokens.shape),
        d_tokens.reshape(tokens.shape),
        mix_grad.reshape(1, width // owners, width),
    )


def solution(mesh):
    return jax.shard_map(
        on_device,
        mesh=mesh,
        in_specs=(
            P(None, "lev", "lat", None, None),
            P(),
            P(),
            P("lev", None, None),
            P("lev", None),
            P(None, "lev", "lat", None, None),
        ),
        out_specs=(
            P(None, "lev", "lat", None, None),
            P(None, "lev", "lat", None, None),
            P("lev", "lat", None),
        ),
        check_vma=False,
    )
```

```python
import functools
import math

import jax
import jax.numpy as jnp
from jax import lax
from jax.experimental import pallas as pl
from jax.experimental.pallas import tpu as pltpu
from jax.sharding import PartitionSpec as P

HEADS = 16
GROUP = 256

epsilon = 1e-06
score_scale = 0.25

F32 = jnp.float32
BF16 = jnp.bfloat16


def nn(a, b):
    return lax.dot_general(a, b, (((1,), (0,)), ((), ())), preferred_element_type=F32)


def nt(a, b):
    return lax.dot_general(a, b, (((1,), (1,)), ((), ())), preferred_element_type=F32)


def tn(a, b):
    return lax.dot_general(a, b, (((0,), (0,)), ((), ())), preferred_element_type=F32)


def block_mean(head_width):
    row = lax.broadcasted_iota(jnp.int32, (GROUP, GROUP), 0) // head_width
    col = lax.broadcasted_iota(jnp.int32, (GROUP, GROUP), 1) // head_width
    return jnp.where(row == col, 1.0 / head_width, 0.0).astype(BF16)


def params():
    return pltpu.CompilerParams(vmem_limit_bytes=36 * 1024 * 1024)


def half_cols(which, width):
    half = width // 2
    core = lax.axis_index("lev") % 2
    return pl.ds(pl.multiple_of((core ^ which) * half, half), half)


def in_hbm(array):
    return pltpu.with_memory_space_constraint(array, pltpu.HBM)


def call(kernel, name, out_shape, *operands):
    return pl.pallas_call(
        kernel, out_shape=out_shape, compiler_params=params(), name=name
    )(*operands)


def pack_kernel(tok_ref, cot_ref, gain_ref, tok_out, *cot_outs):
    batch, rows, parts, chunk, width = tok_ref.shape
    for b in range(batch):
        for q in range(parts):
            for r in range(rows):
                tok_out[b * parts + q, r * chunk : (r + 1) * chunk, :] = tok_ref[b, r, q]
    for s in range(2):
        cols = half_cols(s, width)
        gain = gain_ref[:, cols]
        for b in range(batch):
            for q in range(parts):
                for r in range(rows):
                    piece = cot_ref[b, r, q, :, cols].astype(F32)
                    cot_outs[s][b * parts + q, r * chunk : (r + 1) * chunk, :] = (
                        piece * gain
                    ).astype(BF16)


def pack(tokens, cot, gain):
    batch, rows, parts, chunk, width = tokens.shape
    shape = (batch * parts, rows * chunk)
    return call(
        pack_kernel,
        "pack",
        [jax.ShapeDtypeStruct(shape + (width,), BF16)]
        + [jax.ShapeDtypeStruct(shape + (width // 2,), BF16)] * 2,
        in_hbm(tokens),
        in_hbm(cot),
        in_hbm(gain),
    )


def output_kernel(tok_ref, gain_ref, own_ref, other_ref, out_ref):
    batch, rows, parts, chunk, width = tok_ref.shape
    for s, ref in enumerate((own_ref, other_ref)):
        cols = half_cols(s, width)
        gain = gain_ref[:, cols]
        for t in range(batch * parts):
            b, q = t // parts, t % parts
            for r in range(rows):
                mixed = ref[t, r * chunk : (r + 1) * chunk, :].astype(F32)
                out_ref[b, r, q, :, cols] = (
                    tok_ref[b, r, q, :, cols].astype(F32) + gain * mixed
                ).astype(BF16)


def make_output(tokens, gain, mixed):
    return call(
        output_kernel,
        "make_output",
        jax.ShapeDtypeStruct(tokens.shape, BF16),
        tokens,
        gain,
        *mixed,
    )


def gradient_kernel(cot_ref, back_ref, out_ref):
    batch, rows, parts, chunk, width = cot_ref.shape
    for b in range(batch):
        for q in range(parts):
            for r in range(rows):
                back = back_ref[b * parts + q, r * chunk : (r + 1) * chunk, :width].astype(F32)
                out_ref[b, r, q] = (cot_ref[b, r, q].astype(F32) + back).astype(BF16)


def make_gradient(cot, back):
    return call(
        gradient_kernel, "make_gradient", jax.ShapeDtypeStruct(cot.shape, BF16), cot, back
    )


def by_head(tile, lane):
    zero = jnp.zeros_like(tile)
    return jnp.concatenate([jnp.where(lane == 0, tile, zero), jnp.where(lane == 1, tile, zero)], axis=0)


def one_head(stacked, lane):
    count = lane.shape[0]
    return jnp.where(lane == 0, stacked[:count], stacked[count:])


def side_by_side(stacked):
    count = stacked.shape[0] // 2
    return jnp.concatenate([stacked[:count], stacked[count:]], axis=1)


def forward_kernel(
    samples, lat_count, chunk, owners,
    tok_ref, mask_ref, wq_ref, wk_ref, wv_ref, wm_ref,
    qn_ref, kn_ref, v_ref, rq_ref, rk_ref, ri_ref, p_ref, att_ref, own_ref, other_ref,
    normed_ref, acc_ref, keep_ref,
):
    step = pl.program_id(0)
    count, width = normed_ref.shape
    head_width = width // HEADS

    @pl.when(step == 0)
    def _():
        x = tok_ref[...].astype(F32)
        rx = lax.rsqrt(jnp.mean(x * x, axis=-1, keepdims=True) + epsilon)
        normed_ref[...] = (x * rx).astype(BF16)
        acc_ref[...] = jnp.zeros_like(acc_ref)
        spread = (
            lax.broadcasted_iota(jnp.int32, (lat_count, count), 0)
            == lax.broadcasted_iota(jnp.int32, (lat_count, count), 1) // chunk
        ).astype(F32)
        per_sample = nn(mask_ref[...].astype(F32), spread)
        mine = lax.axis_index("lat") // (owners // samples)
        pick = lax.broadcasted_iota(jnp.int32, (samples, count), 0) == mine
        valid = jnp.sum(jnp.where(pick, per_sample, 0.0), axis=0, keepdims=True)
        same = (
            lax.broadcasted_iota(jnp.int32, (count, count), 0) % chunk
            == lax.broadcasted_iota(jnp.int32, (count, count), 1) % chunk
        )
        keep_ref[...] = jnp.where(same, valid, 0.0)

    normed = normed_ref[...]
    mean_mat = block_mean(head_width)
    q = nn(normed, wq_ref[...])
    k = nn(normed, wk_ref[...])
    v = nn(normed, wv_ref[...]).astype(BF16)
    rq = lax.rsqrt(nn((q * q).astype(BF16), mean_mat) + epsilon)
    rk = lax.rsqrt(nn((k * k).astype(BF16), mean_mat) + epsilon)
    qn = (q * rq).astype(BF16)
    kn = (k * rk).astype(BF16)
    qn_ref[...] = qn
    kn_ref[...] = kn
    v_ref[...] = v
    rq_ref[...] = rq.astype(BF16)
    rk_ref[...] = rk.astype(BF16)
    keep = keep_ref[...]
    keep = jnp.concatenate([keep, keep], axis=0)
    lane = lax.broadcasted_iota(jnp.int32, (count, 128), 1) // head_width
    ones = jnp.ones((count, 128), BF16)
    tiles = []
    for t in range(GROUP // 128):
        cols = slice(t * 128, (t + 1) * 128)
        v_ones = jnp.concatenate([v[:, cols], ones], axis=1)
        e = jnp.exp(nt(by_head(qn[:, cols] * score_scale, lane), kn[:, cols])) * keep
        e = e.astype(BF16)
        p_ref[t] = e
        o = nn(e, v_ones)
        inverse = 1.0 / o[:, 128:]
        tiles.append(one_head(o[:, :128] * inverse, lane))
        ri_ref[:, cols] = one_head(inverse, lane)
    att = jnp.concatenate(tiles, axis=1).astype(BF16)
    features = att_ref.shape[-1]
    for f in range(GROUP // features):
        att_ref[f] = att[:, f * features : (f + 1) * features]
    acc_ref[...] += nn(att, wm_ref[...])

    @pl.when(step == pl.num_programs(0) - 1)
    def _():
        for s, ref in enumerate((own_ref, other_ref)):
            ref[...] = acc_ref[:, half_cols(s, width)].astype(BF16)


def forward(tok_col, key_mask, w_qkv, w_mix, chunk, owners):
    count, width = tok_col.shape
    samples, lat_count = key_mask.shape
    steps = width // GROUP
    features = width // owners
    same = lambda shape: pl.BlockSpec(shape, lambda i: (0, 0))
    cols = pl.BlockSpec((count, GROUP), lambda i: (0, i))
    weight = lambda which: pl.BlockSpec((width, GROUP), lambda i: (0, i + which * steps))
    return pl.pallas_call(
        functools.partial(forward_kernel, samples, lat_count, chunk, owners),
        out_shape=(
            [pltpu.HBM((count, width), BF16)] * 5
            + [pltpu.HBM((count, width), F32)]
            + [pltpu.HBM((width // 128, 2 * count, count), BF16)]
            + [jax.ShapeDtypeStruct((owners, count, features), BF16)]
            + [jax.ShapeDtypeStruct((count, width // 2), BF16)] * 2
        ),
        grid=(steps,),
        in_specs=[
            same((count, width)),
            same((samples, lat_count)),
            weight(0),
            weight(1),
            weight(2),
            pl.BlockSpec((GROUP, width), lambda i: (i, 0)),
        ],
        out_specs=(
            [cols] * 6
            + [pl.BlockSpec((GROUP // 128, 2 * count, count), lambda i: (i, 0, 0))]
            + [pl.BlockSpec((GROUP // features, count, features), lambda i: (i, 0, 0))]
            + [same((count, width // 2))] * 2
        ),
        scratch_shapes=[
            pltpu.VMEM((count, width), BF16),
            pltpu.VMEM((count, width), F32),
            pltpu.VMEM((count, count), F32),
        ],
        compiler_params=params(),
        cost_estimate=pl.CostEstimate(
            flops=2 * count * width * (4 * width + 2 * count * 4),
            bytes_accessed=20 * count * width + 8 * width * width,
            transcendentals=HEADS * count * count,
        ),
        name="forward",
    )(tok_col, key_mask, *[in_hbm(w_qkv)] * 3, in_hbm(w_mix))


def backward_kernel(
    tok_ref, own_ref, other_ref, wm_ref, wq_ref, wk_ref, wv_ref,
    qn_ref, kn_ref, v_ref, rq_ref, rk_ref, ri_ref, p_ref, _,
    out_ref, acc_ref,
):
    step = pl.program_id(0)
    count, width = acc_ref.shape
    head_width = width // HEADS
    d_att = nt(own_ref[...], wm_ref[:, half_cols(0, width)])
    d_att += nt(other_ref[...], wm_ref[:, half_cols(1, width)])
    inverse = ri_ref[...]
    d_att = (d_att * inverse).astype(BF16)
    qn, kn, v = qn_ref[...], kn_ref[...], v_ref[...]
    lane = lax.broadcasted_iota(jnp.int32, (count, 128), 1) // head_width
    dq_tiles, dk_tiles, dv_tiles = [], [], []
    for t in range(GROUP // 128):
        cols = slice(t * 128, (t + 1) * 128)
        d_t = d_att[:, cols]
        d_p = nt(by_head(d_t, lane), v[:, cols])
        e = p_ref[t]
        e_wide = e.astype(F32)
        first = t * 128
        second = first + head_width
        row_inverse = jnp.concatenate(
            [inverse[:, first : first + 1], inverse[:, second : second + 1]], axis=0
        )
        weighted = e_wide * d_p
        inner = jnp.sum(weighted, axis=-1, keepdims=True) * row_inverse
        d_s = (weighted - e_wide * inner).astype(BF16)
        dq_tiles.append(one_head(nn(d_s, kn[:, cols]), lane) * score_scale)
        dk_tiles.append(one_head(tn(side_by_side(d_s), qn[:, cols]), lane) * score_scale)
        dv_tiles.append(one_head(tn(side_by_side(e), d_t), lane))
    mean_mat = block_mean(head_width)
    dq = jnp.concatenate(dq_tiles, axis=1)
    dk = jnp.concatenate(dk_tiles, axis=1)
    dv = jnp.concatenate(dv_tiles, axis=1).astype(BF16)

    def through_norm(upstream, unit, factor):
        unit = unit.astype(F32)
        inner = nn((upstream * unit).astype(BF16), mean_mat)
        return (factor.astype(F32) * (upstream - unit * inner)).astype(BF16)

    gq = through_norm(dq, qn, rq_ref[...])
    gk = through_norm(dk, kn, rk_ref[...])
    total = nt(gq, wq_ref[...]) + nt(gk, wk_ref[...]) + nt(dv, wv_ref[...])

    @pl.when(step == 0)
    def _():
        acc_ref[...] = total

    @pl.when(step > 0)
    def _():
        acc_ref[...] += total

    @pl.when(step == pl.num_programs(0) - 1)
    def _():
        x = tok_ref[...].astype(F32)
        rx = lax.rsqrt(jnp.mean(x * x, axis=-1, keepdims=True) + epsilon)
        d = acc_ref[...]
        inner = jnp.mean(d * x, axis=-1, keepdims=True)
        out_ref[...] = (rx * d - x * (rx * rx * rx * inner)).astype(BF16)


def backward(tok_col, flow, w_mix, w_qkv, saved, after):
    count, width = tok_col.shape
    steps = width // GROUP
    same = lambda shape: pl.BlockSpec(shape, lambda i: (0, 0))
    cols = pl.BlockSpec((count, GROUP), lambda i: (0, i))
    weight = lambda which: pl.BlockSpec((width, GROUP), lambda i: (0, i + which * steps))
    return pl.pallas_call(
        backward_kernel,
        out_shape=jax.ShapeDtypeStruct((count, width), BF16),
        grid=(steps,),
        in_specs=[
            same((count, width)),
            same((count, width // 2)),
            same((count, width // 2)),
            pl.BlockSpec((GROUP, width), lambda i: (i, 0)),
            weight(0),
            weight(1),
            weight(2),
            *([cols] * 6),
            pl.BlockSpec((GROUP // 128, 2 * count, count), lambda i: (i, 0, 0)),
            pl.BlockSpec(memory_space=pl.ANY),
        ],
        out_specs=same((count, width)),
        scratch_shapes=[pltpu.VMEM((count, width), F32)],
        compiler_params=params(),
        cost_estimate=pl.CostEstimate(
            flops=2 * count * width * (4 * width + 4 * count * 4),
            bytes_accessed=20 * count * width + 8 * width * width,
            transcendentals=0,
        ),
        name="backward",
    )(tok_col, *flow, in_hbm(w_mix), *[in_hbm(w_qkv)] * 3, *map(in_hbm, saved), after)


def mix_gradient_kernel(factor, own_flow_ref, other_flow_ref, *refs):
    att_refs, out_refs = refs[: len(refs) // 2], refs[len(refs) // 2 :]
    width = out_refs[0].shape[-1]
    for att_ref, out_ref in zip(att_refs, out_refs):
        att = att_ref[...]
        for s, flow_ref in enumerate((own_flow_ref, other_flow_ref)):
            term = tn(att, flow_ref[...]) * factor
            out_ref[:, half_cols(s, width)] = term.astype(out_ref.dtype)


def mix_gradient(attended, flow, factor):
    rows, features = attended[0].shape
    width = 2 * flow[0].shape[-1]
    out = [jax.ShapeDtypeStruct((features, width), F32)]
    out += [jax.ShapeDtypeStruct((features, width), BF16)] * (len(attended) - 1)
    return pl.pallas_call(
        functools.partial(mix_gradient_kernel, factor),
        out_shape=out,
        compiler_params=params(),
        cost_estimate=pl.CostEstimate(
            flops=2 * rows * features * width * len(attended),
            bytes_accessed=2 * rows * (features * len(attended) + width),
            transcendentals=0,
        ),
        name="mix_gradient",
    )(*flow, *attended)


def chip_rows(array, axis, chip):
    rows = array.shape[axis] // (lax.axis_size("lev") // 2)
    return lax.dynamic_slice_in_dim(array, chip * rows, rows, axis)


def swap(block):
    return lax.all_to_all(block, "lat", split_axis=0, concat_axis=0, tiled=True)


def from_level(block, offset):
    return lax.ppermute(block, "lev", [(i, i ^ offset) for i in range(lax.axis_size("lev"))])


def add_kernel(own_ref, received_ref, out_ref):
    out_ref[...] = (own_ref[...].astype(F32) + received_ref[...].astype(F32)).astype(BF16)


def add(own, received):
    return call(add_kernel, "add", jax.ShapeDtypeStruct(own.shape, BF16), own, received)


def pair_total(own, other):
    return add(own, from_level(other, 1))


def before_last(total):
    offset = 2
    while 2 * offset < lax.axis_size("lev"):
        total = add(total, from_level(total, offset))
        offset *= 2
    return total, from_level(total, offset)


def add_flow_kernel(own_ref, received_ref, _, out_ref, *rows_refs):
    add_kernel(own_ref, received_ref, out_ref)
    for ref in rows_refs:
        rows = ref.shape[1]
        at = pl.ds(pl.multiple_of(lax.axis_index("lev") // 2 * rows, rows), rows)
        total = own_ref[:, at, :].astype(F32) + received_ref[:, at, :].astype(F32)
        ref[...] = total.astype(BF16)


def add_flow(own, received, after):
    owners, cells, half = own.shape
    chips = lax.axis_size("lev") // 2
    rows = cells // chips
    whole = pl.BlockSpec(memory_space=pltpu.VMEM)
    shapes = [jax.ShapeDtypeStruct(own.shape, BF16)]
    if rows % 16 == 0:
        shapes.append(jax.ShapeDtypeStruct((owners, rows, half), BF16))
    outs = pl.pallas_call(
        add_flow_kernel,
        out_shape=shapes,
        in_specs=[whole, whole, pl.BlockSpec(memory_space=pl.ANY)],
        out_specs=[whole] * len(shapes),
        compiler_params=params(),
        name="add_flow",
    )(own, received, after)
    if len(outs) == 2:
        return outs
    return outs[0], chip_rows(outs[0], 1, lax.axis_index("lev") // 2)


def join_kernel(first_ref, second_ref, _, out_ref):
    count = first_ref.shape[0]
    out_ref[:count] = first_ref[...]
    out_ref[count:] = second_ref[...]


def join(first, second, after):
    whole = pl.BlockSpec(memory_space=pltpu.VMEM)
    return pl.pallas_call(
        join_kernel,
        out_shape=jax.ShapeDtypeStruct((2 * first.shape[0],) + first.shape[1:], BF16),
        in_specs=[whole, whole, pl.BlockSpec(memory_space=pl.ANY)],
        out_specs=whole,
        compiler_params=params(),
        name="join",
    )(first, second, after)


def from_owner(block, offset):
    return lax.ppermute(block, "lat", [(i, i ^ offset) for i in range(lax.axis_size("lat"))])


def arrange_kernel(first_ref, second_ref, out_ref):
    owners = out_ref.shape[1]
    bits = owners.bit_length() - 1
    half = owners // 2
    for u in range(owners):
        band = lax.axis_index("lat") ^ int(format(u, f"0{bits}b")[::-1], 2)
        ref = first_ref if u < half else second_ref
        out_ref[:, band] = ref[u % half]


def arrange(first, second):
    _, owners, rows, half = first.shape
    shape = jax.ShapeDtypeStruct((owners, owners, rows, half), BF16)
    return call(arrange_kernel, "arrange", shape, first, second)


def add_mixed_kernel(own_ref, received_ref, back_ref, out_ref):
    width = back_ref.shape[-1]
    out_ref[:, :width] = back_ref[...]
    out_ref[:, width:] = (own_ref[...].astype(F32) + received_ref[...].astype(F32)).astype(BF16)


def add_mixed(own, received, back):
    count, width = back.shape
    shape = jax.ShapeDtypeStruct((count, width + own.shape[-1]), BF16)
    return call(add_mixed_kernel, "add_mixed", shape, own, received, back)


def cut_kernel(in_ref, _, out_ref):
    out_ref[...] = in_ref[:, :, in_ref.shape[-1] - out_ref.shape[-1] :]


def cut_mixed(received, after):
    owners, cells, wide = received.shape
    whole = pl.BlockSpec(memory_space=pltpu.VMEM)
    return pl.pallas_call(
        cut_kernel,
        out_shape=jax.ShapeDtypeStruct((owners, cells, wide // 3), BF16),
        in_specs=[whole, pl.BlockSpec(memory_space=pl.ANY)],
        out_specs=whole,
        compiler_params=params(),
        name="cut_mixed",
    )(received, after)


def on_device(tokens, key_mask, w_qkv, w_mix, level_scale, cotangent):
    batch, _, rows, lon, width = tokens.shape
    owners = lax.axis_size("lat")
    parts = owners // batch
    chunk = lon // parts
    cells = rows * chunk
    count = batch * rows * lon
    half = width // 2
    tok_band = tokens.reshape(batch, rows, parts, chunk, width)
    cot_band = cotangent.reshape(batch, rows, parts, chunk, width)
    w_mix = w_mix.reshape(width, width)

    tok_send, cot_own, cot_other = pack(tok_band, cot_band, level_scale)
    tok_col = swap(tok_send).reshape(count, width)
    flow_band, flow_rows = add_flow(*before_last(pair_total(cot_own, cot_other)), tok_col)
    flow_rows = flow_rows[None]
    offset = owners // 2
    received = from_owner(flow_rows, offset)
    flow_own = swap(flow_band).reshape(count, half)
    flow = (flow_own, from_level(flow_own, 1))
    chip = lax.axis_index("lev") // 2
    chips = lax.axis_size("lev") // 2

    *saved, attended, mix_own, mix_other = forward(
        tok_col, key_mask, w_qkv, w_mix, chunk, owners
    )
    attended = swap(attended)
    mix_terms = before_last(pair_total(mix_own, mix_other))
    while offset > 2:
        flow_rows = join(flow_rows, received, mix_terms[0])
        offset //= 2
        received = from_owner(flow_rows, offset)
    back_col = backward(tok_col, flow, w_mix, w_qkv, saved, flow_rows)
    flow_rows = join(flow_rows, received, back_col)
    received = from_owner(flow_rows, 1)
    back = swap(add_mixed(*mix_terms, back_col).reshape(owners, cells, width + half))
    d_tokens = make_gradient(cot_band, back)

    factor = 1.0 / math.sqrt(count * owners)
    features = width // owners
    attended = attended.reshape(owners, owners, cells, features)
    attended = [chip_rows(attended, 2, chip ^ k).reshape(-1, features) for k in range(chips)]
    attended[1:] = [from_level(attended[k], 2 * k) for k in range(1, chips)]
    flow_rows = arrange(flow_rows, received).reshape(-1, half)
    grads = mix_gradient(attended, (flow_rows, from_level(flow_rows, 1)), factor)
    mix_grad = grads[0]
    for k in range(1, chips):
        mix_grad += from_level(grads[k], 2 * k).astype(F32)

    mix_band = cut_mixed(back, mix_grad)
    output = make_output(tok_band, level_scale, (mix_band, from_level(mix_band, 1)))
    return (
        output.reshape(tokens.shape),
        d_tokens.reshape(tokens.shape),
        mix_grad.reshape(1, width // owners, width),
    )


def solution(mesh):
    return jax.shard_map(
        on_device,
        mesh=mesh,
        in_specs=(
            P(None, "lev", "lat", None, None),
            P(),
            P(),
            P("lev", None, None),
            P("lev", None),
            P(None, "lev", "lat", None, None),
        ),
        out_specs=(
            P(None, "lev", "lat", None, None),
            P(None, "lev", "lat", None, None),
            P("lev", "lat", None),
        ),
        check_vma=False,
    )
```

```python
import functools
import math

import jax
import jax.numpy as jnp
from jax import lax
from jax.experimental import pallas as pl
from jax.experimental.pallas import tpu as pltpu
from jax.sharding import PartitionSpec as P

HEADS = 16
GROUP = 256

epsilon = 1e-06
score_scale = 0.25

F32 = jnp.float32
BF16 = jnp.bfloat16


def nn(a, b):
    return lax.dot_general(a, b, (((1,), (0,)), ((), ())), preferred_element_type=F32)


def nt(a, b):
    return lax.dot_general(a, b, (((1,), (1,)), ((), ())), preferred_element_type=F32)


def tn(a, b):
    return lax.dot_general(a, b, (((0,), (0,)), ((), ())), preferred_element_type=F32)


def block_mean(head_width):
    row = lax.broadcasted_iota(jnp.int32, (GROUP, GROUP), 0) // head_width
    col = lax.broadcasted_iota(jnp.int32, (GROUP, GROUP), 1) // head_width
    return jnp.where(row == col, 1.0 / head_width, 0.0).astype(BF16)


def params():
    return pltpu.CompilerParams(vmem_limit_bytes=36 * 1024 * 1024)


def half_cols(which, width):
    half = width // 2
    core = lax.axis_index("lev") % 2
    return pl.ds(pl.multiple_of((core ^ which) * half, half), half)


def in_hbm(array):
    return pltpu.with_memory_space_constraint(array, pltpu.HBM)


def call(kernel, name, out_shape, *operands):
    return pl.pallas_call(
        kernel, out_shape=out_shape, compiler_params=params(), name=name
    )(*operands)


def pack_kernel(tok_ref, cot_ref, gain_ref, tok_out, *cot_outs):
    batch, rows, parts, chunk, width = tok_ref.shape
    for b in range(batch):
        for q in range(parts):
            for r in range(rows):
                tok_out[b * parts + q, r * chunk : (r + 1) * chunk, :] = tok_ref[b, r, q]
    for s in range(2):
        cols = half_cols(s, width)
        gain = gain_ref[:, cols]
        for b in range(batch):
            for q in range(parts):
                for r in range(rows):
                    piece = cot_ref[b, r, q, :, cols].astype(F32)
                    cot_outs[s][b * parts + q, r * chunk : (r + 1) * chunk, :] = (
                        piece * gain
                    ).astype(BF16)


def pack(tokens, cot, gain):
    batch, rows, parts, chunk, width = tokens.shape
    shape = (batch * parts, rows * chunk)
    return call(
        pack_kernel,
        "pack",
        [jax.ShapeDtypeStruct(shape + (width,), BF16)]
        + [jax.ShapeDtypeStruct(shape + (width // 2,), BF16)] * 2,
        in_hbm(tokens),
        in_hbm(cot),
        in_hbm(gain),
    )


def output_kernel(tok_ref, gain_ref, own_ref, other_ref, out_ref):
    batch, rows, parts, chunk, width = tok_ref.shape
    for s, ref in enumerate((own_ref, other_ref)):
        cols = half_cols(s, width)
        gain = gain_ref[:, cols]
        for t in range(batch * parts):
            b, q = t // parts, t % parts
            for r in range(rows):
                mixed = ref[t, r * chunk : (r + 1) * chunk, :].astype(F32)
                out_ref[b, r, q, :, cols] = (
                    tok_ref[b, r, q, :, cols].astype(F32) + gain * mixed
                ).astype(BF16)


def make_output(tokens, gain, mixed):
    return call(
        output_kernel,
        "make_output",
        jax.ShapeDtypeStruct(tokens.shape, BF16),
        tokens,
        gain,
        *mixed,
    )


def gradient_kernel(cot_ref, back_ref, out_ref):
    batch, rows, parts, chunk, width = cot_ref.shape
    for b in range(batch):
        for q in range(parts):
            for r in range(rows):
                back = back_ref[b * parts + q, r * chunk : (r + 1) * chunk, :width].astype(F32)
                out_ref[b, r, q] = (cot_ref[b, r, q].astype(F32) + back).astype(BF16)


def make_gradient(cot, back):
    return call(
        gradient_kernel, "make_gradient", jax.ShapeDtypeStruct(cot.shape, BF16), cot, back
    )


def by_head(tile, lane):
    zero = jnp.zeros_like(tile)
    return jnp.concatenate([jnp.where(lane == 0, tile, zero), jnp.where(lane == 1, tile, zero)], axis=0)


def one_head(stacked, lane):
    count = lane.shape[0]
    return jnp.where(lane == 0, stacked[:count], stacked[count:])


def side_by_side(stacked):
    count = stacked.shape[0] // 2
    return jnp.concatenate([stacked[:count], stacked[count:]], axis=1)


def forward_kernel(
    samples, lat_count, chunk, owners,
    tok_ref, mask_ref, wq_ref, wk_ref, wv_ref, wm_ref, _,
    qn_ref, kn_ref, v_ref, rq_ref, rk_ref, ri_ref, p_ref, att_ref, own_ref, other_ref,
    normed_ref, acc_ref, keep_ref,
):
    step = pl.program_id(0)
    count, width = normed_ref.shape
    head_width = width // HEADS

    @pl.when(step == 0)
    def _():
        x = tok_ref[...].astype(F32)
        rx = lax.rsqrt(jnp.mean(x * x, axis=-1, keepdims=True) + epsilon)
        normed_ref[...] = (x * rx).astype(BF16)
        acc_ref[...] = jnp.zeros_like(acc_ref)
        spread = (
            lax.broadcasted_iota(jnp.int32, (lat_count, count), 0)
            == lax.broadcasted_iota(jnp.int32, (lat_count, count), 1) // chunk
        ).astype(F32)
        per_sample = nn(mask_ref[...].astype(F32), spread)
        mine = lax.axis_index("lat") // (owners // samples)
        pick = lax.broadcasted_iota(jnp.int32, (samples, count), 0) == mine
        valid = jnp.sum(jnp.where(pick, per_sample, 0.0), axis=0, keepdims=True)
        same = (
            lax.broadcasted_iota(jnp.int32, (count, count), 0) % chunk
            == lax.broadcasted_iota(jnp.int32, (count, count), 1) % chunk
        )
        keep_ref[...] = jnp.where(same, valid, 0.0)

    normed = normed_ref[...]
    mean_mat = block_mean(head_width)
    q = nn(normed, wq_ref[...])
    k = nn(normed, wk_ref[...])
    v = nn(normed, wv_ref[...]).astype(BF16)
    rq = lax.rsqrt(nn((q * q).astype(BF16), mean_mat) + epsilon)
    rk = lax.rsqrt(nn((k * k).astype(BF16), mean_mat) + epsilon)
    qn = (q * rq).astype(BF16)
    kn = (k * rk).astype(BF16)
    qn_ref[...] = qn
    kn_ref[...] = kn
    v_ref[...] = v
    rq_ref[...] = rq.astype(BF16)
    rk_ref[...] = rk.astype(BF16)
    keep = keep_ref[...]
    keep = jnp.concatenate([keep, keep], axis=0)
    lane = lax.broadcasted_iota(jnp.int32, (count, 128), 1) // head_width
    ones = jnp.ones((count, 128), BF16)
    tiles = []
    for t in range(GROUP // 128):
        cols = slice(t * 128, (t + 1) * 128)
        v_ones = jnp.concatenate([v[:, cols], ones], axis=1)
        e = jnp.exp(nt(by_head(qn[:, cols] * score_scale, lane), kn[:, cols])) * keep
        e = e.astype(BF16)
        p_ref[t] = e
        o = nn(e, v_ones)
        inverse = 1.0 / o[:, 128:]
        tiles.append(one_head(o[:, :128] * inverse, lane))
        ri_ref[:, cols] = one_head(inverse, lane)
    att = jnp.concatenate(tiles, axis=1).astype(BF16)
    features = att_ref.shape[-1]
    for f in range(GROUP // features):
        att_ref[f] = att[:, f * features : (f + 1) * features]
    acc_ref[...] += nn(att, wm_ref[...])

    @pl.when(step == pl.num_programs(0) - 1)
    def _():
        for s, ref in enumerate((own_ref, other_ref)):
            ref[...] = acc_ref[:, half_cols(s, width)].astype(BF16)


def forward(tok_col, key_mask, w_qkv, w_mix, chunk, owners, after):
    count, width = tok_col.shape
    samples, lat_count = key_mask.shape
    steps = width // GROUP
    features = width // owners
    same = lambda shape: pl.BlockSpec(shape, lambda i: (0, 0))
    cols = pl.BlockSpec((count, GROUP), lambda i: (0, i))
    weight = lambda which: pl.BlockSpec((width, GROUP), lambda i: (0, i + which * steps))
    return pl.pallas_call(
        functools.partial(forward_kernel, samples, lat_count, chunk, owners),
        out_shape=(
            [pltpu.HBM((count, width), BF16)] * 5
            + [pltpu.HBM((count, width), F32)]
            + [pltpu.HBM((width // 128, 2 * count, count), BF16)]
            + [jax.ShapeDtypeStruct((owners, count, features), BF16)]
            + [jax.ShapeDtypeStruct((count, width // 2), BF16)] * 2
        ),
        grid=(steps,),
        in_specs=[
            same((count, width)),
            same((samples, lat_count)),
            weight(0),
            weight(1),
            weight(2),
            pl.BlockSpec((GROUP, width), lambda i: (i, 0)),
            pl.BlockSpec(memory_space=pl.ANY),
        ],
        out_specs=(
            [cols] * 6
            + [pl.BlockSpec((GROUP // 128, 2 * count, count), lambda i: (i, 0, 0))]
            + [pl.BlockSpec((GROUP // features, count, features), lambda i: (i, 0, 0))]
            + [same((count, width // 2))] * 2
        ),
        scratch_shapes=[
            pltpu.VMEM((count, width), BF16),
            pltpu.VMEM((count, width), F32),
            pltpu.VMEM((count, count), F32),
        ],
        compiler_params=params(),
        cost_estimate=pl.CostEstimate(
            flops=2 * count * width * (4 * width + 2 * count * 4),
            bytes_accessed=20 * count * width + 8 * width * width,
            transcendentals=HEADS * count * count,
        ),
        name="forward",
    )(tok_col, key_mask, *[in_hbm(w_qkv)] * 3, in_hbm(w_mix), after)


def backward_kernel(
    tok_ref, own_ref, other_ref, wm_ref, wq_ref, wk_ref, wv_ref,
    qn_ref, kn_ref, v_ref, rq_ref, rk_ref, ri_ref, p_ref, *rest,
):
    out_ref, acc_ref = rest[-2:]
    step = pl.program_id(0)
    count, width = acc_ref.shape
    head_width = width // HEADS
    d_att = nt(own_ref[...], wm_ref[:, half_cols(0, width)])
    d_att += nt(other_ref[...], wm_ref[:, half_cols(1, width)])
    inverse = ri_ref[...]
    d_att = (d_att * inverse).astype(BF16)
    qn, kn, v = qn_ref[...], kn_ref[...], v_ref[...]
    lane = lax.broadcasted_iota(jnp.int32, (count, 128), 1) // head_width
    dq_tiles, dk_tiles, dv_tiles = [], [], []
    for t in range(GROUP // 128):
        cols = slice(t * 128, (t + 1) * 128)
        d_t = d_att[:, cols]
        d_p = nt(by_head(d_t, lane), v[:, cols])
        e = p_ref[t]
        e_wide = e.astype(F32)
        first = t * 128
        second = first + head_width
        row_inverse = jnp.concatenate(
            [inverse[:, first : first + 1], inverse[:, second : second + 1]], axis=0
        )
        weighted = e_wide * d_p
        inner = jnp.sum(weighted, axis=-1, keepdims=True) * row_inverse
        d_s = (weighted - e_wide * inner).astype(BF16)
        dq_tiles.append(one_head(nn(d_s, kn[:, cols]), lane) * score_scale)
        dk_tiles.append(one_head(tn(side_by_side(d_s), qn[:, cols]), lane) * score_scale)
        dv_tiles.append(one_head(tn(side_by_side(e), d_t), lane))
    mean_mat = block_mean(head_width)
    dq = jnp.concatenate(dq_tiles, axis=1)
    dk = jnp.concatenate(dk_tiles, axis=1)
    dv = jnp.concatenate(dv_tiles, axis=1).astype(BF16)

    def through_norm(upstream, unit, factor):
        unit = unit.astype(F32)
        inner = nn((upstream * unit).astype(BF16), mean_mat)
        return (factor.astype(F32) * (upstream - unit * inner)).astype(BF16)

    gq = through_norm(dq, qn, rq_ref[...])
    gk = through_norm(dk, kn, rk_ref[...])
    total = nt(gq, wq_ref[...]) + nt(gk, wk_ref[...]) + nt(dv, wv_ref[...])

    @pl.when(step == 0)
    def _():
        acc_ref[...] = total

    @pl.when(step > 0)
    def _():
        acc_ref[...] += total

    @pl.when(step == pl.num_programs(0) - 1)
    def _():
        x = tok_ref[...].astype(F32)
        rx = lax.rsqrt(jnp.mean(x * x, axis=-1, keepdims=True) + epsilon)
        d = acc_ref[...]
        inner = jnp.mean(d * x, axis=-1, keepdims=True)
        out_ref[...] = (rx * d - x * (rx * rx * rx * inner)).astype(BF16)


def backward(tok_col, flow, w_mix, w_qkv, saved, *after):
    count, width = tok_col.shape
    steps = width // GROUP
    same = lambda shape: pl.BlockSpec(shape, lambda i: (0, 0))
    cols = pl.BlockSpec((count, GROUP), lambda i: (0, i))
    weight = lambda which: pl.BlockSpec((width, GROUP), lambda i: (0, i + which * steps))
    return pl.pallas_call(
        backward_kernel,
        out_shape=jax.ShapeDtypeStruct((count, width), BF16),
        grid=(steps,),
        in_specs=[
            same((count, width)),
            same((count, width // 2)),
            same((count, width // 2)),
            pl.BlockSpec((GROUP, width), lambda i: (i, 0)),
            weight(0),
            weight(1),
            weight(2),
            *([cols] * 6),
            pl.BlockSpec((GROUP // 128, 2 * count, count), lambda i: (i, 0, 0)),
        ]
        + [pl.BlockSpec(memory_space=pl.ANY)] * len(after),
        out_specs=same((count, width)),
        scratch_shapes=[pltpu.VMEM((count, width), F32)],
        compiler_params=params(),
        cost_estimate=pl.CostEstimate(
            flops=2 * count * width * (4 * width + 4 * count * 4),
            bytes_accessed=20 * count * width + 8 * width * width,
            transcendentals=0,
        ),
        name="backward",
    )(tok_col, *flow, in_hbm(w_mix), *[in_hbm(w_qkv)] * 3, *map(in_hbm, saved), *after)


def mix_gradient_kernel(factor, own_flow_ref, other_flow_ref, *refs):
    att_refs, out_refs = refs[: len(refs) // 2], refs[len(refs) // 2 :]
    width = out_refs[0].shape[-1]
    for att_ref, out_ref in zip(att_refs, out_refs):
        att = att_ref[...]
        for s, flow_ref in enumerate((own_flow_ref, other_flow_ref)):
            term = tn(att, flow_ref[...]) * factor
            out_ref[:, half_cols(s, width)] = term.astype(out_ref.dtype)


def mix_gradient(attended, flow, factor):
    rows, features = attended[0].shape
    width = 2 * flow[0].shape[-1]
    out = [jax.ShapeDtypeStruct((features, width), F32)]
    out += [jax.ShapeDtypeStruct((features, width), BF16)] * (len(attended) - 1)
    return pl.pallas_call(
        functools.partial(mix_gradient_kernel, factor),
        out_shape=out,
        compiler_params=params(),
        cost_estimate=pl.CostEstimate(
            flops=2 * rows * features * width * len(attended),
            bytes_accessed=2 * rows * (features * len(attended) + width),
            transcendentals=0,
        ),
        name="mix_gradient",
    )(*flow, *attended)


def chip_rows(array, axis, chip):
    rows = array.shape[axis] // (lax.axis_size("lev") // 2)
    return lax.dynamic_slice_in_dim(array, (chip * rows).astype(jnp.uint32), rows, axis)


def swap(block):
    return lax.all_to_all(block, "lat", split_axis=0, concat_axis=0, tiled=True)


def from_level(block, offset):
    return lax.ppermute(block, "lev", [(i, i ^ offset) for i in range(lax.axis_size("lev"))])


def add_kernel(own_ref, received_ref, out_ref):
    out_ref[...] = (own_ref[...].astype(F32) + received_ref[...].astype(F32)).astype(BF16)


def add(own, received):
    return call(add_kernel, "add", jax.ShapeDtypeStruct(own.shape, BF16), own, received)


def pair_total(own, other):
    return add(own, from_level(other, 1))


def before_last(total):
    offset = 2
    while 2 * offset < lax.axis_size("lev"):
        total = add(total, from_level(total, offset))
        offset *= 2
    return total, from_level(total, offset)


def add_flow_kernel(own_ref, received_ref, _, out_ref, *rows_refs):
    add_kernel(own_ref, received_ref, out_ref)
    for ref in rows_refs:
        rows = ref.shape[1]
        at = pl.ds(pl.multiple_of(lax.axis_index("lev") // 2 * rows, rows), rows)
        total = own_ref[:, at, :].astype(F32) + received_ref[:, at, :].astype(F32)
        ref[...] = total.astype(BF16)


def add_flow(own, received, after):
    owners, cells, half = own.shape
    chips = lax.axis_size("lev") // 2
    rows = cells // chips
    whole = pl.BlockSpec(memory_space=pltpu.VMEM)
    shapes = [jax.ShapeDtypeStruct(own.shape, BF16)]
    if rows % 16 == 0:
        shapes.append(jax.ShapeDtypeStruct((owners, rows, half), BF16))
    outs = pl.pallas_call(
        add_flow_kernel,
        out_shape=shapes,
        in_specs=[whole, whole, pl.BlockSpec(memory_space=pl.ANY)],
        out_specs=[whole] * len(shapes),
        compiler_params=params(),
        name="add_flow",
    )(own, received, after)
    if len(outs) == 2:
        return outs
    return outs[0], chip_rows(outs[0], 1, lax.axis_index("lev") // 2)


def join_kernel(first_ref, second_ref, out_ref):
    count = first_ref.shape[0]
    out_ref[:count] = first_ref[...]
    out_ref[count:] = second_ref[...]


def join(first, second):
    shape = jax.ShapeDtypeStruct((2 * first.shape[0],) + first.shape[1:], BF16)
    return call(join_kernel, "join", shape, first, second)


def from_owner(block, offset):
    return lax.ppermute(block, "lat", [(i, i ^ offset) for i in range(lax.axis_size("lat"))])


def arrange_kernel(first_ref, second_ref, _, out_ref):
    owners = out_ref.shape[1]
    bits = owners.bit_length() - 1
    half = owners // 2
    for u in range(owners):
        band = lax.axis_index("lat") ^ int(format(u, f"0{bits}b")[::-1], 2)
        ref = first_ref if u < half else second_ref
        out_ref[:, band] = ref[u % half]


def arrange(first, second, after):
    _, owners, rows, half = first.shape
    whole = pl.BlockSpec(memory_space=pltpu.VMEM)
    return pl.pallas_call(
        arrange_kernel,
        out_shape=jax.ShapeDtypeStruct((owners, owners, rows, half), BF16),
        in_specs=[whole, whole, pl.BlockSpec(memory_space=pl.ANY)],
        out_specs=whole,
        compiler_params=params(),
        name="arrange",
    )(first, second, after)


def add_mixed_kernel(own_ref, received_ref, back_ref, out_ref):
    width = back_ref.shape[-1]
    out_ref[:, :width] = back_ref[...]
    out_ref[:, width:] = (own_ref[...].astype(F32) + received_ref[...].astype(F32)).astype(BF16)


def add_mixed(own, received, back):
    count, width = back.shape
    shape = jax.ShapeDtypeStruct((count, width + own.shape[-1]), BF16)
    return call(add_mixed_kernel, "add_mixed", shape, own, received, back)


def cut_kernel(in_ref, _, out_ref):
    out_ref[...] = in_ref[:, :, in_ref.shape[-1] - out_ref.shape[-1] :]


def cut_mixed(received, after):
    owners, cells, wide = received.shape
    whole = pl.BlockSpec(memory_space=pltpu.VMEM)
    return pl.pallas_call(
        cut_kernel,
        out_shape=jax.ShapeDtypeStruct((owners, cells, wide // 3), BF16),
        in_specs=[whole, pl.BlockSpec(memory_space=pl.ANY)],
        out_specs=whole,
        compiler_params=params(),
        name="cut_mixed",
    )(received, after)


def on_device(tokens, key_mask, w_qkv, w_mix, level_scale, cotangent):
    batch, _, rows, lon, width = tokens.shape
    owners = lax.axis_size("lat")
    parts = owners // batch
    chunk = lon // parts
    cells = rows * chunk
    count = batch * rows * lon
    half = width // 2
    tok_band = tokens.reshape(batch, rows, parts, chunk, width)
    cot_band = cotangent.reshape(batch, rows, parts, chunk, width)
    w_mix = w_mix.reshape(width, width)

    tok_send, cot_own, cot_other = pack(tok_band, cot_band, level_scale)
    tok_col = swap(tok_send).reshape(count, width)
    flow_band, flow_rows = add_flow(*before_last(pair_total(cot_own, cot_other)), tok_col)
    flow_rows = flow_rows[None]
    offset = owners // 2
    flow_rows = join(flow_rows, from_owner(flow_rows, offset))
    flow_own = swap(flow_band).reshape(count, half)
    flow = (flow_own, from_level(flow_own, 1))
    chip = lax.shift_right_logical(lax.axis_index("lev"), 1)
    chips = lax.axis_size("lev") // 2

    *saved, attended, mix_own, mix_other = forward(
        tok_col, key_mask, w_qkv, w_mix, chunk, owners, flow_rows
    )
    attended = swap(attended)
    mix_terms = before_last(pair_total(mix_own, mix_other))
    while offset > 2:
        offset //= 2
        flow_rows = join(flow_rows, from_owner(flow_rows, offset))
    received = from_owner(flow_rows, 1)
    back_col = backward(tok_col, flow, w_mix, w_qkv, saved, mix_terms[0], flow_rows)
    sent = add_mixed(*mix_terms, back_col)
    back = swap(sent.reshape(owners, cells, width + half))
    d_tokens = make_gradient(cot_band, back)

    factor = 1.0 / math.sqrt(count * owners)
    features = width // owners
    attended = attended.reshape(owners, owners, cells, features)
    attended = [chip_rows(attended, 2, chip ^ k).reshape(-1, features) for k in range(chips)]
    attended[1:] = [from_level(attended[k], 2 * k) for k in range(1, chips)]
    flow_rows = arrange(flow_rows, received, sent).reshape(-1, half)
    grads = mix_gradient(attended, (flow_rows, from_level(flow_rows, 1)), factor)
    mix_grad = grads[0]
    for k in range(1, chips):
        mix_grad += from_level(grads[k], 2 * k).astype(F32)

    mix_band = cut_mixed(back, mix_grad)
    output = make_output(tok_band, level_scale, (mix_band, from_level(mix_band, 1)))
    return (
        output.reshape(tokens.shape),
        d_tokens.reshape(tokens.shape),
        mix_grad.reshape(1, width // owners, width),
    )


def solution(mesh):
    return jax.shard_map(
        on_device,
        mesh=mesh,
        in_specs=(
            P(None, "lev", "lat", None, None),
            P(),
            P(),
            P("lev", None, None),
            P("lev", None),
            P(None, "lev", "lat", None, None),
        ),
        out_specs=(
            P(None, "lev", "lat", None, None),
            P(None, "lev", "lat", None, None),
            P("lev", "lat", None),
        ),
        check_vma=False,
    )
```

```python
import functools
import math

import jax
import jax.numpy as jnp
from jax import lax
from jax.experimental import pallas as pl
from jax.experimental.pallas import tpu as pltpu
from jax.sharding import PartitionSpec as P

HEADS = 16
GROUP = 256

epsilon = 1e-06
score_scale = 0.25

F32 = jnp.float32
BF16 = jnp.bfloat16


def nn(a, b):
    return lax.dot_general(a, b, (((1,), (0,)), ((), ())), preferred_element_type=F32)


def nt(a, b):
    return lax.dot_general(a, b, (((1,), (1,)), ((), ())), preferred_element_type=F32)


def tn(a, b):
    return lax.dot_general(a, b, (((0,), (0,)), ((), ())), preferred_element_type=F32)


def block_mean(head_width):
    row = lax.broadcasted_iota(jnp.int32, (GROUP, GROUP), 0) // head_width
    col = lax.broadcasted_iota(jnp.int32, (GROUP, GROUP), 1) // head_width
    return jnp.where(row == col, 1.0 / head_width, 0.0).astype(BF16)


def params():
    return pltpu.CompilerParams(vmem_limit_bytes=36 * 1024 * 1024)


def half_cols(which, width):
    half = width // 2
    core = lax.axis_index("lev") % 2
    return pl.ds(pl.multiple_of((core ^ which) * half, half), half)


def in_hbm(array):
    return pltpu.with_memory_space_constraint(array, pltpu.HBM)


def call(kernel, name, out_shape, *operands):
    return pl.pallas_call(
        kernel, out_shape=out_shape, compiler_params=params(), name=name
    )(*operands)


def pack_kernel(tok_ref, cot_ref, gain_ref, tok_out, *cot_outs):
    batch, rows, parts, chunk, width = tok_ref.shape
    for b in range(batch):
        for q in range(parts):
            for r in range(rows):
                tok_out[b * parts + q, r * chunk : (r + 1) * chunk, :] = tok_ref[b, r, q]
    for s in range(2):
        cols = half_cols(s, width)
        gain = gain_ref[:, cols]
        for b in range(batch):
            for q in range(parts):
                for r in range(rows):
                    piece = cot_ref[b, r, q, :, cols].astype(F32)
                    cot_outs[s][b * parts + q, r * chunk : (r + 1) * chunk, :] = (
                        piece * gain
                    ).astype(BF16)


def pack(tokens, cot, gain):
    batch, rows, parts, chunk, width = tokens.shape
    shape = (batch * parts, rows * chunk)
    return call(
        pack_kernel,
        "pack",
        [jax.ShapeDtypeStruct(shape + (width,), BF16)]
        + [jax.ShapeDtypeStruct(shape + (width // 2,), BF16)] * 2,
        in_hbm(tokens),
        in_hbm(cot),
        in_hbm(gain),
    )


def output_kernel(tok_ref, gain_ref, own_ref, other_ref, out_ref):
    batch, rows, parts, chunk, width = tok_ref.shape
    for s, ref in enumerate((own_ref, other_ref)):
        cols = half_cols(s, width)
        gain = gain_ref[:, cols]
        for t in range(batch * parts):
            b, q = t // parts, t % parts
            for r in range(rows):
                mixed = ref[t, r * chunk : (r + 1) * chunk, :].astype(F32)
                out_ref[b, r, q, :, cols] = (
                    tok_ref[b, r, q, :, cols].astype(F32) + gain * mixed
                ).astype(BF16)


def make_output(tokens, gain, mixed):
    return call(
        output_kernel,
        "make_output",
        jax.ShapeDtypeStruct(tokens.shape, BF16),
        tokens,
        gain,
        *mixed,
    )


def gradient_kernel(cot_ref, back_ref, out_ref):
    batch, rows, parts, chunk, width = cot_ref.shape
    for b in range(batch):
        for q in range(parts):
            for r in range(rows):
                back = back_ref[b * parts + q, r * chunk : (r + 1) * chunk, :width].astype(F32)
                out_ref[b, r, q] = (cot_ref[b, r, q].astype(F32) + back).astype(BF16)


def make_gradient(cot, back):
    return call(
        gradient_kernel, "make_gradient", jax.ShapeDtypeStruct(cot.shape, BF16), cot, back
    )


def by_head(tile, lane):
    zero = jnp.zeros_like(tile)
    return jnp.concatenate([jnp.where(lane == 0, tile, zero), jnp.where(lane == 1, tile, zero)], axis=0)


def one_head(stacked, lane):
    count = lane.shape[0]
    return jnp.where(lane == 0, stacked[:count], stacked[count:])


def side_by_side(stacked):
    count = stacked.shape[0] // 2
    return jnp.concatenate([stacked[:count], stacked[count:]], axis=1)


def forward_kernel(
    samples, lat_count, chunk, owners,
    tok_ref, mask_ref, wq_ref, wk_ref, wv_ref, wm_ref,
    qn_ref, kn_ref, v_ref, rq_ref, rk_ref, ri_ref, p_ref, att_ref, own_ref, other_ref,
    normed_ref, acc_ref, keep_ref,
):
    step = pl.program_id(0)
    count, width = normed_ref.shape
    head_width = width // HEADS

    @pl.when(step == 0)
    def _():
        x = tok_ref[...].astype(F32)
        rx = lax.rsqrt(jnp.mean(x * x, axis=-1, keepdims=True) + epsilon)
        normed_ref[...] = (x * rx).astype(BF16)
        acc_ref[...] = jnp.zeros_like(acc_ref)
        spread = (
            lax.broadcasted_iota(jnp.int32, (lat_count, count), 0)
            == lax.broadcasted_iota(jnp.int32, (lat_count, count), 1) // chunk
        ).astype(F32)
        per_sample = nn(mask_ref[...].astype(F32), spread)
        mine = lax.axis_index("lat") // (owners // samples)
        pick = lax.broadcasted_iota(jnp.int32, (samples, count), 0) == mine
        valid = jnp.sum(jnp.where(pick, per_sample, 0.0), axis=0, keepdims=True)
        same = (
            lax.broadcasted_iota(jnp.int32, (count, count), 0) % chunk
            == lax.broadcasted_iota(jnp.int32, (count, count), 1) % chunk
        )
        keep_ref[...] = jnp.where(same, valid, 0.0)

    normed = normed_ref[...]
    mean_mat = block_mean(head_width)
    q = nn(normed, wq_ref[...])
    k = nn(normed, wk_ref[...])
    v = nn(normed, wv_ref[...]).astype(BF16)
    rq = lax.rsqrt(nn((q * q).astype(BF16), mean_mat) + epsilon)
    rk = lax.rsqrt(nn((k * k).astype(BF16), mean_mat) + epsilon)
    qn = (q * rq).astype(BF16)
    kn = (k * rk).astype(BF16)
    qn_ref[...] = qn
    kn_ref[...] = kn
    v_ref[...] = v
    rq_ref[...] = rq.astype(BF16)
    rk_ref[...] = rk.astype(BF16)
    keep = keep_ref[...]
    keep = jnp.concatenate([keep, keep], axis=0)
    lane = lax.broadcasted_iota(jnp.int32, (count, 128), 1) // head_width
    ones = jnp.ones((count, 128), BF16)
    tiles = []
    for t in range(GROUP // 128):
        cols = slice(t * 128, (t + 1) * 128)
        v_ones = jnp.concatenate([v[:, cols], ones], axis=1)
        e = jnp.exp(nt(by_head(qn[:, cols] * score_scale, lane), kn[:, cols])) * keep
        e = e.astype(BF16)
        p_ref[t] = e
        o = nn(e, v_ones)
        inverse = 1.0 / o[:, 128:]
        tiles.append(one_head(o[:, :128] * inverse, lane))
        ri_ref[:, cols] = one_head(inverse, lane)
    att = jnp.concatenate(tiles, axis=1).astype(BF16)
    features = att_ref.shape[-1]
    for f in range(GROUP // features):
        att_ref[f] = att[:, f * features : (f + 1) * features]
    acc_ref[...] += nn(att, wm_ref[...])

    @pl.when(step == pl.num_programs(0) - 1)
    def _():
        for s, ref in enumerate((own_ref, other_ref)):
            ref[...] = acc_ref[:, half_cols(s, width)].astype(BF16)


def forward(tok_col, key_mask, w_qkv, w_mix, chunk, owners):
    count, width = tok_col.shape
    samples, lat_count = key_mask.shape
    steps = width // GROUP
    features = width // owners
    same = lambda shape: pl.BlockSpec(shape, lambda i: (0, 0))
    cols = pl.BlockSpec((count, GROUP), lambda i: (0, i))
    weight = lambda which: pl.BlockSpec((width, GROUP), lambda i: (0, i + which * steps))
    return pl.pallas_call(
        functools.partial(forward_kernel, samples, lat_count, chunk, owners),
        out_shape=(
            [pltpu.HBM((count, width), BF16)] * 5
            + [pltpu.HBM((count, width), F32)]
            + [pltpu.HBM((width // 128, 2 * count, count), BF16)]
            + [jax.ShapeDtypeStruct((owners, count, features), BF16)]
            + [jax.ShapeDtypeStruct((count, width // 2), BF16)] * 2
        ),
        grid=(steps,),
        in_specs=[
            same((count, width)),
            same((samples, lat_count)),
            weight(0),
            weight(1),
            weight(2),
            pl.BlockSpec((GROUP, width), lambda i: (i, 0)),
        ],
        out_specs=(
            [cols] * 6
            + [pl.BlockSpec((GROUP // 128, 2 * count, count), lambda i: (i, 0, 0))]
            + [pl.BlockSpec((GROUP // features, count, features), lambda i: (i, 0, 0))]
            + [same((count, width // 2))] * 2
        ),
        scratch_shapes=[
            pltpu.VMEM((count, width), BF16),
            pltpu.VMEM((count, width), F32),
            pltpu.VMEM((count, count), F32),
        ],
        compiler_params=params(),
        cost_estimate=pl.CostEstimate(
            flops=2 * count * width * width,
            bytes_accessed=2 * count * width,
            transcendentals=0,
        ),
        name="forward",
    )(tok_col, key_mask, *[in_hbm(w_qkv)] * 3, in_hbm(w_mix))


def backward_kernel(
    tok_ref, own_ref, other_ref, wm_ref, wq_ref, wk_ref, wv_ref,
    qn_ref, kn_ref, v_ref, rq_ref, rk_ref, ri_ref, p_ref, *rest,
):
    out_ref, acc_ref = rest[-2:]
    step = pl.program_id(0)
    count, width = acc_ref.shape
    head_width = width // HEADS
    d_att = nt(own_ref[...], wm_ref[:, half_cols(0, width)])
    d_att += nt(other_ref[...], wm_ref[:, half_cols(1, width)])
    inverse = ri_ref[...]
    d_att = (d_att * inverse).astype(BF16)
    qn, kn, v = qn_ref[...], kn_ref[...], v_ref[...]
    lane = lax.broadcasted_iota(jnp.int32, (count, 128), 1) // head_width
    dq_tiles, dk_tiles, dv_tiles = [], [], []
    for t in range(GROUP // 128):
        cols = slice(t * 128, (t + 1) * 128)
        d_t = d_att[:, cols]
        d_p = nt(by_head(d_t, lane), v[:, cols])
        e = p_ref[t]
        e_wide = e.astype(F32)
        first = t * 128
        second = first + head_width
        row_inverse = jnp.concatenate(
            [inverse[:, first : first + 1], inverse[:, second : second + 1]], axis=0
        )
        weighted = e_wide * d_p
        inner = jnp.sum(weighted, axis=-1, keepdims=True) * row_inverse
        d_s = (weighted - e_wide * inner).astype(BF16)
        dq_tiles.append(one_head(nn(d_s, kn[:, cols]), lane) * score_scale)
        dk_tiles.append(one_head(tn(side_by_side(d_s), qn[:, cols]), lane) * score_scale)
        dv_tiles.append(one_head(tn(side_by_side(e), d_t), lane))
    mean_mat = block_mean(head_width)
    dq = jnp.concatenate(dq_tiles, axis=1)
    dk = jnp.concatenate(dk_tiles, axis=1)
    dv = jnp.concatenate(dv_tiles, axis=1).astype(BF16)

    def through_norm(upstream, unit, factor):
        unit = unit.astype(F32)
        inner = nn((upstream * unit).astype(BF16), mean_mat)
        return (factor.astype(F32) * (upstream - unit * inner)).astype(BF16)

    gq = through_norm(dq, qn, rq_ref[...])
    gk = through_norm(dk, kn, rk_ref[...])
    total = nt(gq, wq_ref[...]) + nt(gk, wk_ref[...]) + nt(dv, wv_ref[...])

    @pl.when(step == 0)
    def _():
        acc_ref[...] = total

    @pl.when(step > 0)
    def _():
        acc_ref[...] += total

    @pl.when(step == pl.num_programs(0) - 1)
    def _():
        x = tok_ref[...].astype(F32)
        rx = lax.rsqrt(jnp.mean(x * x, axis=-1, keepdims=True) + epsilon)
        d = acc_ref[...]
        inner = jnp.mean(d * x, axis=-1, keepdims=True)
        out_ref[...] = (rx * d - x * (rx * rx * rx * inner)).astype(BF16)


def backward(tok_col, flow, w_mix, w_qkv, saved, *after):
    count, width = tok_col.shape
    steps = width // GROUP
    same = lambda shape: pl.BlockSpec(shape, lambda i: (0, 0))
    cols = pl.BlockSpec((count, GROUP), lambda i: (0, i))
    weight = lambda which: pl.BlockSpec((width, GROUP), lambda i: (0, i + which * steps))
    return pl.pallas_call(
        backward_kernel,
        out_shape=jax.ShapeDtypeStruct((count, width), BF16),
        grid=(steps,),
        in_specs=[
            same((count, width)),
            same((count, width // 2)),
            same((count, width // 2)),
            pl.BlockSpec((GROUP, width), lambda i: (i, 0)),
            weight(0),
            weight(1),
            weight(2),
            *([cols] * 6),
            pl.BlockSpec((GROUP // 128, 2 * count, count), lambda i: (i, 0, 0)),
        ]
        + [pl.BlockSpec(memory_space=pl.ANY)] * len(after),
        out_specs=same((count, width)),
        scratch_shapes=[pltpu.VMEM((count, width), F32)],
        compiler_params=params(),
        cost_estimate=pl.CostEstimate(
            flops=2 * count * width * (4 * width + 4 * count * 4),
            bytes_accessed=20 * count * width + 8 * width * width,
            transcendentals=0,
        ),
        name="backward",
    )(tok_col, *flow, in_hbm(w_mix), *[in_hbm(w_qkv)] * 3, *map(in_hbm, saved), *after)


def mix_gradient_kernel(factor, own_flow_ref, other_flow_ref, *refs):
    att_refs, out_refs = refs[: len(refs) // 2], refs[len(refs) // 2 :]
    width = out_refs[0].shape[-1]
    for att_ref, out_ref in zip(att_refs, out_refs):
        att = att_ref[...]
        for s, flow_ref in enumerate((own_flow_ref, other_flow_ref)):
            term = tn(att, flow_ref[...]) * factor
            out_ref[:, half_cols(s, width)] = term.astype(out_ref.dtype)


def mix_gradient(attended, flow, factor):
    rows, features = attended[0].shape
    width = 2 * flow[0].shape[-1]
    out = [jax.ShapeDtypeStruct((features, width), F32)]
    out += [jax.ShapeDtypeStruct((features, width), BF16)] * (len(attended) - 1)
    return pl.pallas_call(
        functools.partial(mix_gradient_kernel, factor),
        out_shape=out,
        compiler_params=params(),
        cost_estimate=pl.CostEstimate(
            flops=2 * rows * features * width * len(attended),
            bytes_accessed=2 * rows * (features * len(attended) + width),
            transcendentals=0,
        ),
        name="mix_gradient",
    )(*flow, *attended)


def chip_rows(array, axis, chip):
    rows = array.shape[axis] // (lax.axis_size("lev") // 2)
    return lax.dynamic_slice_in_dim(array, (chip * rows).astype(jnp.uint32), rows, axis)


def swap(block):
    return lax.all_to_all(block, "lat", split_axis=0, concat_axis=0, tiled=True)


def from_level(block, offset):
    return lax.ppermute(block, "lev", [(i, i ^ offset) for i in range(lax.axis_size("lev"))])


def add_kernel(own_ref, received_ref, out_ref):
    out_ref[...] = (own_ref[...].astype(F32) + received_ref[...].astype(F32)).astype(BF16)


def add(own, received):
    return call(add_kernel, "add", jax.ShapeDtypeStruct(own.shape, BF16), own, received)


def pair_total(own, other):
    return add(own, from_level(other, 1))


def before_last(total):
    offset = 2
    while 2 * offset < lax.axis_size("lev"):
        total = add(total, from_level(total, offset))
        offset *= 2
    return total, from_level(total, offset)


def add_flow_kernel(own_ref, received_ref, _, out_ref, *rows_refs):
    add_kernel(own_ref, received_ref, out_ref)
    for ref in rows_refs:
        rows = ref.shape[1]
        at = pl.ds(pl.multiple_of(lax.axis_index("lev") // 2 * rows, rows), rows)
        total = own_ref[:, at, :].astype(F32) + received_ref[:, at, :].astype(F32)
        ref[...] = total.astype(BF16)


def add_flow(own, received, after):
    owners, cells, half = own.shape
    chips = lax.axis_size("lev") // 2
    rows = cells // chips
    whole = pl.BlockSpec(memory_space=pltpu.VMEM)
    shapes = [jax.ShapeDtypeStruct(own.shape, BF16)]
    if rows % 16 == 0:
        shapes.append(jax.ShapeDtypeStruct((owners, rows, half), BF16))
    outs = pl.pallas_call(
        add_flow_kernel,
        out_shape=shapes,
        in_specs=[whole, whole, pl.BlockSpec(memory_space=pl.ANY)],
        out_specs=[whole] * len(shapes),
        compiler_params=params(),
        name="add_flow",
    )(own, received, after)
    if len(outs) == 2:
        return outs
    return outs[0], chip_rows(outs[0], 1, lax.axis_index("lev") // 2)


def join_kernel(*refs):
    *in_refs, out_ref = refs
    count = in_refs[0].shape[0]
    for k, ref in enumerate(in_refs):
        out_ref[k * count : (k + 1) * count] = ref[...]


def join(*parts):
    count = len(parts) * parts[0].shape[0]
    shape = jax.ShapeDtypeStruct((count,) + parts[0].shape[1:], BF16)
    return call(join_kernel, "join", shape, *parts)


def from_owner(block, offset):
    return lax.ppermute(block, "lat", [(i, i ^ offset) for i in range(lax.axis_size("lat"))])


def gathered_offset(u, owners):
    offset = u % 4 * (owners // 4)
    u //= 4
    bit = owners // 8
    while bit:
        offset += u % 2 * bit
        u //= 2
        bit //= 2
    return offset


def arrange_kernel(first_ref, second_ref, _, out_ref):
    owners = out_ref.shape[1]
    half = owners // 2
    for u in range(owners):
        band = lax.axis_index("lat") ^ gathered_offset(u, owners)
        ref = first_ref if u < half else second_ref
        out_ref[:, band] = ref[u % half]


def arrange(first, second, after):
    _, owners, rows, half = first.shape
    whole = pl.BlockSpec(memory_space=pltpu.VMEM)
    return pl.pallas_call(
        arrange_kernel,
        out_shape=jax.ShapeDtypeStruct((owners, owners, rows, half), BF16),
        in_specs=[whole, whole, pl.BlockSpec(memory_space=pl.ANY)],
        out_specs=whole,
        compiler_params=params(),
        name="arrange",
    )(first, second, after)


def add_mixed_kernel(own_ref, received_ref, back_ref, out_ref):
    width = back_ref.shape[-1]
    out_ref[:, :width] = back_ref[...]
    out_ref[:, width:] = (own_ref[...].astype(F32) + received_ref[...].astype(F32)).astype(BF16)


def add_mixed(own, received, back):
    count, width = back.shape
    shape = jax.ShapeDtypeStruct((count, width + own.shape[-1]), BF16)
    return call(add_mixed_kernel, "add_mixed", shape, own, received, back)


def cut_kernel(in_ref, _, out_ref):
    out_ref[...] = in_ref[:, :, in_ref.shape[-1] - out_ref.shape[-1] :]


def cut_mixed(received, after):
    owners, cells, wide = received.shape
    whole = pl.BlockSpec(memory_space=pltpu.VMEM)
    return pl.pallas_call(
        cut_kernel,
        out_shape=jax.ShapeDtypeStruct((owners, cells, wide // 3), BF16),
        in_specs=[whole, pl.BlockSpec(memory_space=pl.ANY)],
        out_specs=whole,
        compiler_params=params(),
        name="cut_mixed",
    )(received, after)


def on_device(tokens, key_mask, w_qkv, w_mix, level_scale, cotangent):
    batch, _, rows, lon, width = tokens.shape
    owners = lax.axis_size("lat")
    parts = owners // batch
    chunk = lon // parts
    cells = rows * chunk
    count = batch * rows * lon
    half = width // 2
    tok_band = tokens.reshape(batch, rows, parts, chunk, width)
    cot_band = cotangent.reshape(batch, rows, parts, chunk, width)
    w_mix = w_mix.reshape(width, width)

    tok_send, cot_own, cot_other = pack(tok_band, cot_band, level_scale)
    tok_col = swap(tok_send).reshape(count, width)
    flow_band, flow_rows = add_flow(*before_last(pair_total(cot_own, cot_other)), tok_col)
    flow_rows = flow_rows[None]
    flow_rows = [flow_rows] + [from_owner(flow_rows, k * owners // 4) for k in range(1, 4)]
    flow_own = swap(flow_band).reshape(count, half)
    flow = (flow_own, from_level(flow_own, 1))
    chip = lax.shift_right_logical(lax.axis_index("lev"), 1)
    chips = lax.axis_size("lev") // 2

    *saved, attended, mix_own, mix_other = forward(
        tok_col, key_mask, w_qkv, w_mix, chunk, owners
    )
    attended = swap(attended)
    mix_terms = before_last(pair_total(mix_own, mix_other))
    flow_rows = join(*flow_rows)
    offset = owners // 8
    while offset > 1:
        flow_rows = join(flow_rows, from_owner(flow_rows, offset))
        offset //= 2
    received = from_owner(flow_rows, offset)
    back_col = backward(tok_col, flow, w_mix, w_qkv, saved, mix_terms[0], flow_rows)
    sent = add_mixed(*mix_terms, back_col)
    back = swap(sent.reshape(owners, cells, width + half))
    d_tokens = make_gradient(cot_band, back)

    factor = 1.0 / math.sqrt(count * owners)
    features = width // owners
    attended = attended.reshape(owners, owners, cells, features)
    attended = [chip_rows(attended, 2, chip ^ k).reshape(-1, features) for k in range(chips)]
    attended[1:] = [from_level(attended[k], 2 * k) for k in range(1, chips)]
    flow_rows = arrange(flow_rows, received, sent).reshape(-1, half)
    grads = mix_gradient(attended, (flow_rows, from_level(flow_rows, 1)), factor)
    mix_grad = grads[0]
    for k in range(1, chips):
        mix_grad += from_level(grads[k], 2 * k).astype(F32)

    mix_band = cut_mixed(back, mix_grad)
    output = make_output(tok_band, level_scale, (mix_band, from_level(mix_band, 1)))
    return (
        output.reshape(tokens.shape),
        d_tokens.reshape(tokens.shape),
        mix_grad.reshape(1, width // owners, width),
    )


def solution(mesh):
    return jax.shard_map(
        on_device,
        mesh=mesh,
        in_specs=(
            P(None, "lev", "lat", None, None),
            P(),
            P(),
            P("lev", None, None),
            P("lev", None),
            P(None, "lev", "lat", None, None),
        ),
        out_specs=(
            P(None, "lev", "lat", None, None),
            P(None, "lev", "lat", None, None),
            P("lev", "lat", None),
        ),
        check_vma=False,
    )
```

```python
import functools
import math

import jax
import jax.numpy as jnp
from jax import lax
from jax.experimental import pallas as pl
from jax.experimental.pallas import tpu as pltpu
from jax.sharding import PartitionSpec as P

HEADS = 16
GROUP = 256

epsilon = 1e-06
score_scale = 0.25

F32 = jnp.float32
BF16 = jnp.bfloat16


def nn(a, b):
    return lax.dot_general(a, b, (((1,), (0,)), ((), ())), preferred_element_type=F32)


def nt(a, b):
    return lax.dot_general(a, b, (((1,), (1,)), ((), ())), preferred_element_type=F32)


def tn(a, b):
    return lax.dot_general(a, b, (((0,), (0,)), ((), ())), preferred_element_type=F32)


def block_mean(head_width):
    row = lax.broadcasted_iota(jnp.int32, (GROUP, GROUP), 0) // head_width
    col = lax.broadcasted_iota(jnp.int32, (GROUP, GROUP), 1) // head_width
    return jnp.where(row == col, 1.0 / head_width, 0.0).astype(BF16)


def params():
    return pltpu.CompilerParams(vmem_limit_bytes=36 * 1024 * 1024)


def half_cols(which, width):
    half = width // 2
    core = lax.axis_index("lev") % 2
    return pl.ds(pl.multiple_of((core ^ which) * half, half), half)


def in_hbm(array):
    return pltpu.with_memory_space_constraint(array, pltpu.HBM)


def call(kernel, name, out_shape, *operands):
    return pl.pallas_call(
        kernel, out_shape=out_shape, compiler_params=params(), name=name
    )(*operands)


def pack_kernel(tok_ref, cot_ref, gain_ref, tok_out, *cot_outs):
    batch, rows, parts, chunk, width = tok_ref.shape
    for b in range(batch):
        for q in range(parts):
            for r in range(rows):
                tok_out[b * parts + q, r * chunk : (r + 1) * chunk, :] = tok_ref[b, r, q]
    for s in range(2):
        cols = half_cols(s, width)
        gain = gain_ref[:, cols]
        for b in range(batch):
            for q in range(parts):
                for r in range(rows):
                    piece = cot_ref[b, r, q, :, cols].astype(F32)
                    cot_outs[s][b * parts + q, r * chunk : (r + 1) * chunk, :] = (
                        piece * gain
                    ).astype(BF16)


def pack(tokens, cot, gain):
    batch, rows, parts, chunk, width = tokens.shape
    shape = (batch * parts, rows * chunk)
    return call(
        pack_kernel,
        "pack",
        [jax.ShapeDtypeStruct(shape + (width,), BF16)]
        + [jax.ShapeDtypeStruct(shape + (width // 2,), BF16)] * 2,
        in_hbm(tokens),
        in_hbm(cot),
        in_hbm(gain),
    )


def output_kernel(tok_ref, gain_ref, own_ref, other_ref, out_ref):
    batch, rows, parts, chunk, width = tok_ref.shape
    for s, ref in enumerate((own_ref, other_ref)):
        cols = half_cols(s, width)
        gain = gain_ref[:, cols]
        for t in range(batch * parts):
            b, q = t // parts, t % parts
            for r in range(rows):
                mixed = ref[t, r * chunk : (r + 1) * chunk, :].astype(F32)
                out_ref[b, r, q, :, cols] = (
                    tok_ref[b, r, q, :, cols].astype(F32) + gain * mixed
                ).astype(BF16)


def make_output(tokens, gain, mixed):
    return call(
        output_kernel,
        "make_output",
        jax.ShapeDtypeStruct(tokens.shape, BF16),
        tokens,
        gain,
        *mixed,
    )


def gradient_kernel(cot_ref, back_ref, out_ref):
    batch, rows, parts, chunk, width = cot_ref.shape
    for b in range(batch):
        for q in range(parts):
            for r in range(rows):
                back = back_ref[b * parts + q, r * chunk : (r + 1) * chunk, :width].astype(F32)
                out_ref[b, r, q] = (cot_ref[b, r, q].astype(F32) + back).astype(BF16)


def make_gradient(cot, back):
    return call(
        gradient_kernel, "make_gradient", jax.ShapeDtypeStruct(cot.shape, BF16), cot, back
    )


def by_head(tile, lane):
    zero = jnp.zeros_like(tile)
    return jnp.concatenate([jnp.where(lane == 0, tile, zero), jnp.where(lane == 1, tile, zero)], axis=0)


def one_head(stacked, lane):
    count = lane.shape[0]
    return jnp.where(lane == 0, stacked[:count], stacked[count:])


def side_by_side(stacked):
    count = stacked.shape[0] // 2
    return jnp.concatenate([stacked[:count], stacked[count:]], axis=1)


def forward_kernel(
    samples, lat_count, chunk, owners,
    tok_ref, mask_ref, wq_ref, wk_ref, wv_ref, wm_ref, _,
    qn_ref, kn_ref, v_ref, rq_ref, rk_ref, ri_ref, p_ref, att_ref, own_ref, other_ref,
    normed_ref, acc_ref, keep_ref,
):
    step = pl.program_id(0)
    count, width = normed_ref.shape
    head_width = width // HEADS

    @pl.when(step == 0)
    def _():
        x = tok_ref[...].astype(F32)
        rx = lax.rsqrt(jnp.mean(x * x, axis=-1, keepdims=True) + epsilon)
        normed_ref[...] = (x * rx).astype(BF16)
        acc_ref[...] = jnp.zeros_like(acc_ref)
        spread = (
            lax.broadcasted_iota(jnp.int32, (lat_count, count), 0)
            == lax.broadcasted_iota(jnp.int32, (lat_count, count), 1) // chunk
        ).astype(F32)
        per_sample = nn(mask_ref[...].astype(F32), spread)
        mine = lax.axis_index("lat") // (owners // samples)
        pick = lax.broadcasted_iota(jnp.int32, (samples, count), 0) == mine
        valid = jnp.sum(jnp.where(pick, per_sample, 0.0), axis=0, keepdims=True)
        same = (
            lax.broadcasted_iota(jnp.int32, (count, count), 0) % chunk
            == lax.broadcasted_iota(jnp.int32, (count, count), 1) % chunk
        )
        keep_ref[...] = jnp.where(same, valid, 0.0)

    normed = normed_ref[...]
    mean_mat = block_mean(head_width)
    q = nn(normed, wq_ref[...])
    k = nn(normed, wk_ref[...])
    v = nn(normed, wv_ref[...]).astype(BF16)
    rq = lax.rsqrt(nn((q * q).astype(BF16), mean_mat) + epsilon)
    rk = lax.rsqrt(nn((k * k).astype(BF16), mean_mat) + epsilon)
    qn = (q * rq).astype(BF16)
    kn = (k * rk).astype(BF16)
    qn_ref[...] = qn
    kn_ref[...] = kn
    v_ref[...] = v
    rq_ref[...] = rq.astype(BF16)
    rk_ref[...] = rk.astype(BF16)
    keep = keep_ref[...]
    keep = jnp.concatenate([keep, keep], axis=0)
    lane = lax.broadcasted_iota(jnp.int32, (count, 128), 1) // head_width
    ones = jnp.ones((count, 128), BF16)
    tiles = []
    for t in range(GROUP // 128):
        cols = slice(t * 128, (t + 1) * 128)
        v_ones = jnp.concatenate([v[:, cols], ones], axis=1)
        e = jnp.exp(nt(by_head(qn[:, cols] * score_scale, lane), kn[:, cols])) * keep
        e = e.astype(BF16)
        p_ref[t] = e
        o = nn(e, v_ones)
        inverse = 1.0 / o[:, 128:]
        tiles.append(one_head(o[:, :128] * inverse, lane))
        ri_ref[:, cols] = one_head(inverse, lane)
    att = jnp.concatenate(tiles, axis=1).astype(BF16)
    features = att_ref.shape[-1]
    for f in range(GROUP // features):
        att_ref[f] = att[:, f * features : (f + 1) * features]
    acc_ref[...] += nn(att, wm_ref[...])

    @pl.when(step == pl.num_programs(0) - 1)
    def _():
        for s, ref in enumerate((own_ref, other_ref)):
            ref[...] = acc_ref[:, half_cols(s, width)].astype(BF16)


def forward(tok_col, key_mask, w_qkv, w_mix, chunk, owners, after):
    count, width = tok_col.shape
    samples, lat_count = key_mask.shape
    steps = width // GROUP
    features = width // owners
    same = lambda shape: pl.BlockSpec(shape, lambda i: (0, 0))
    cols = pl.BlockSpec((count, GROUP), lambda i: (0, i))
    weight = lambda which: pl.BlockSpec((width, GROUP), lambda i: (0, i + which * steps))
    return pl.pallas_call(
        functools.partial(forward_kernel, samples, lat_count, chunk, owners),
        out_shape=(
            [pltpu.HBM((count, width), BF16)] * 5
            + [pltpu.HBM((count, width), F32)]
            + [pltpu.HBM((width // 128, 2 * count, count), BF16)]
            + [jax.ShapeDtypeStruct((owners, count, features), BF16)]
            + [jax.ShapeDtypeStruct((count, width // 2), BF16)] * 2
        ),
        grid=(steps,),
        in_specs=[
            same((count, width)),
            same((samples, lat_count)),
            weight(0),
            weight(1),
            weight(2),
            pl.BlockSpec((GROUP, width), lambda i: (i, 0)),
            pl.BlockSpec(memory_space=pl.ANY),
        ],
        out_specs=(
            [cols] * 6
            + [pl.BlockSpec((GROUP // 128, 2 * count, count), lambda i: (i, 0, 0))]
            + [pl.BlockSpec((GROUP // features, count, features), lambda i: (i, 0, 0))]
            + [same((count, width // 2))] * 2
        ),
        scratch_shapes=[
            pltpu.VMEM((count, width), BF16),
            pltpu.VMEM((count, width), F32),
            pltpu.VMEM((count, count), F32),
        ],
        compiler_params=params(),
        cost_estimate=pl.CostEstimate(
            flops=2 * count * width * (4 * width + 2 * count * 4),
            bytes_accessed=20 * count * width + 8 * width * width,
            transcendentals=HEADS * count * count,
        ),
        name="forward",
    )(tok_col, key_mask, *[in_hbm(w_qkv)] * 3, in_hbm(w_mix), after)


def backward_kernel(
    tok_ref, own_ref, other_ref, wm_ref, wq_ref, wk_ref, wv_ref,
    qn_ref, kn_ref, v_ref, rq_ref, rk_ref, ri_ref, p_ref, *rest,
):
    out_ref, acc_ref = rest[-2:]
    step = pl.program_id(0)
    count, width = acc_ref.shape
    head_width = width // HEADS
    d_att = nt(own_ref[...], wm_ref[:, half_cols(0, width)])
    d_att += nt(other_ref[...], wm_ref[:, half_cols(1, width)])
    inverse = ri_ref[...]
    d_att = (d_att * inverse).astype(BF16)
    qn, kn, v = qn_ref[...], kn_ref[...], v_ref[...]
    lane = lax.broadcasted_iota(jnp.int32, (count, 128), 1) // head_width
    dq_tiles, dk_tiles, dv_tiles = [], [], []
    for t in range(GROUP // 128):
        cols = slice(t * 128, (t + 1) * 128)
        d_t = d_att[:, cols]
        d_p = nt(by_head(d_t, lane), v[:, cols])
        e = p_ref[t]
        e_wide = e.astype(F32)
        first = t * 128
        second = first + head_width
        row_inverse = jnp.concatenate(
            [inverse[:, first : first + 1], inverse[:, second : second + 1]], axis=0
        )
        weighted = e_wide * d_p
        inner = jnp.sum(weighted, axis=-1, keepdims=True) * row_inverse
        d_s = (weighted - e_wide * inner).astype(BF16)
        dq_tiles.append(one_head(nn(d_s, kn[:, cols]), lane) * score_scale)
        dk_tiles.append(one_head(tn(side_by_side(d_s), qn[:, cols]), lane) * score_scale)
        dv_tiles.append(one_head(tn(side_by_side(e), d_t), lane))
    mean_mat = block_mean(head_width)
    dq = jnp.concatenate(dq_tiles, axis=1)
    dk = jnp.concatenate(dk_tiles, axis=1)
    dv = jnp.concatenate(dv_tiles, axis=1).astype(BF16)

    def through_norm(upstream, unit, factor):
        unit = unit.astype(F32)
        inner = nn((upstream * unit).astype(BF16), mean_mat)
        return (factor.astype(F32) * (upstream - unit * inner)).astype(BF16)

    gq = through_norm(dq, qn, rq_ref[...])
    gk = through_norm(dk, kn, rk_ref[...])
    total = nt(gq, wq_ref[...]) + nt(gk, wk_ref[...]) + nt(dv, wv_ref[...])

    @pl.when(step == 0)
    def _():
        acc_ref[...] = total

    @pl.when(step > 0)
    def _():
        acc_ref[...] += total

    @pl.when(step == pl.num_programs(0) - 1)
    def _():
        x = tok_ref[...].astype(F32)
        rx = lax.rsqrt(jnp.mean(x * x, axis=-1, keepdims=True) + epsilon)
        d = acc_ref[...]
        inner = jnp.mean(d * x, axis=-1, keepdims=True)
        out_ref[...] = (rx * d - x * (rx * rx * rx * inner)).astype(BF16)


def backward(tok_col, flow, w_mix, w_qkv, saved, *after):
    count, width = tok_col.shape
    steps = width // GROUP
    same = lambda shape: pl.BlockSpec(shape, lambda i: (0, 0))
    cols = pl.BlockSpec((count, GROUP), lambda i: (0, i))
    weight = lambda which: pl.BlockSpec((width, GROUP), lambda i: (0, i + which * steps))
    return pl.pallas_call(
        backward_kernel,
        out_shape=jax.ShapeDtypeStruct((count, width), BF16),
        grid=(steps,),
        in_specs=[
            same((count, width)),
            same((count, width // 2)),
            same((count, width // 2)),
            pl.BlockSpec((GROUP, width), lambda i: (i, 0)),
            weight(0),
            weight(1),
            weight(2),
            *([cols] * 6),
            pl.BlockSpec((GROUP // 128, 2 * count, count), lambda i: (i, 0, 0)),
        ]
        + [pl.BlockSpec(memory_space=pl.ANY)] * len(after),
        out_specs=same((count, width)),
        scratch_shapes=[pltpu.VMEM((count, width), F32)],
        compiler_params=params(),
        cost_estimate=pl.CostEstimate(
            flops=2 * count * width * (4 * width + 4 * count * 4),
            bytes_accessed=20 * count * width + 8 * width * width,
            transcendentals=0,
        ),
        name="backward",
    )(tok_col, *flow, in_hbm(w_mix), *[in_hbm(w_qkv)] * 3, *map(in_hbm, saved), *after)


def mix_gradient_kernel(factor, own_flow_ref, other_flow_ref, *refs):
    att_refs, out_refs = refs[: len(refs) // 2], refs[len(refs) // 2 :]
    width = out_refs[0].shape[-1]
    for att_ref, out_ref in zip(att_refs, out_refs):
        att = att_ref[...]
        for s, flow_ref in enumerate((own_flow_ref, other_flow_ref)):
            term = tn(att, flow_ref[...]) * factor
            out_ref[:, half_cols(s, width)] = term.astype(out_ref.dtype)


def mix_gradient(attended, flow, factor):
    rows, features = attended[0].shape
    width = 2 * flow[0].shape[-1]
    out = [jax.ShapeDtypeStruct((features, width), F32)]
    out += [jax.ShapeDtypeStruct((features, width), BF16)] * (len(attended) - 1)
    return pl.pallas_call(
        functools.partial(mix_gradient_kernel, factor),
        out_shape=out,
        compiler_params=params(),
        cost_estimate=pl.CostEstimate(
            flops=2 * rows * features * width * len(attended),
            bytes_accessed=2 * rows * (features * len(attended) + width),
            transcendentals=0,
        ),
        name="mix_gradient",
    )(*flow, *attended)


def chip_rows(array, axis, chip):
    rows = array.shape[axis] // (lax.axis_size("lev") // 2)
    return lax.dynamic_slice_in_dim(array, (chip * rows).astype(jnp.uint32), rows, axis)


def swap(block):
    return lax.all_to_all(block, "lat", split_axis=0, concat_axis=0, tiled=True)


def from_level(block, offset):
    return lax.ppermute(block, "lev", [(i, i ^ offset) for i in range(lax.axis_size("lev"))])


def add_kernel(own_ref, received_ref, out_ref):
    out_ref[...] = (own_ref[...].astype(F32) + received_ref[...].astype(F32)).astype(BF16)


def add(own, received):
    return call(add_kernel, "add", jax.ShapeDtypeStruct(own.shape, BF16), own, received)


def pair_total(own, other):
    return add(own, from_level(other, 1))


def before_last(total):
    offset = 2
    while 2 * offset < lax.axis_size("lev"):
        total = add(total, from_level(total, offset))
        offset *= 2
    return total, from_level(total, offset)


def row_half(which, rows):
    top = lax.axis_index("lev") // (lax.axis_size("lev") // 2)
    return pl.ds(pl.multiple_of((top ^ which) * rows, rows), rows)


def split_kernel(own_ref, received_ref, first_ref, second_ref):
    rows = first_ref.shape[1]
    for which, ref in enumerate((first_ref, second_ref)):
        at = row_half(which, rows)
        total = own_ref[:, at, :].astype(F32) + received_ref[:, at, :].astype(F32)
        ref[...] = total.astype(BF16)


def split_rows(own, received):
    owners, cells, half = own.shape
    rows = cells // 2
    if rows % 16 == 0:
        part = jax.ShapeDtypeStruct((owners, rows, half), BF16)
        return call(split_kernel, "split_rows", [part, part], own, received)
    total = (own.astype(F32) + received.astype(F32)).astype(BF16)
    top = lax.axis_index("lev") // (lax.axis_size("lev") // 2)
    return [lax.dynamic_slice_in_dim(total, (top ^ k) * rows, rows, 1) for k in range(2)]


def add_flow_kernel(first_ref, second_ref, received_ref, _, __, out_ref):
    rows = first_ref.shape[1]
    out_ref[:, row_half(0, rows), :] = first_ref[...]
    second = second_ref[...].astype(F32) + received_ref[...].astype(F32)
    out_ref[:, row_half(1, rows), :] = second.astype(BF16)


def add_flow(first, second, received, *after):
    owners, rows, half = first.shape
    if rows % 16:
        second = (second.astype(F32) + received.astype(F32)).astype(BF16)
        top = lax.axis_index("lev") // (lax.axis_size("lev") // 2)
        pair = jnp.where(top == 0, jnp.stack([first, second]), jnp.stack([second, first]))
        return jnp.concatenate([pair[0], pair[1]], axis=1)
    whole = pl.BlockSpec(memory_space=pltpu.VMEM)
    return pl.pallas_call(
        add_flow_kernel,
        out_shape=jax.ShapeDtypeStruct((owners, 2 * rows, half), BF16),
        in_specs=[whole] * 3 + [pl.BlockSpec(memory_space=pl.ANY)] * 2,
        out_specs=whole,
        compiler_params=params(),
        name="add_flow",
    )(first, second, received, *after)


def join_kernel(first_ref, second_ref, out_ref):
    count = first_ref.shape[0]
    out_ref[:count] = first_ref[...]
    out_ref[count:] = second_ref[...]


def join(first, second):
    shape = jax.ShapeDtypeStruct((2 * first.shape[0],) + first.shape[1:], BF16)
    return call(join_kernel, "join", shape, first, second)


def from_owner(block, offset):
    return lax.ppermute(block, "lat", [(i, i ^ offset) for i in range(lax.axis_size("lat"))])


def gather_offsets(owners):
    offsets = [owners // 4, owners // 2]
    while len(offsets) < owners.bit_length() - 1:
        offsets.append(owners >> (len(offsets) + 1))
    return offsets


def arrange_kernel(first_ref, second_ref, _, out_ref):
    owners = out_ref.shape[1]
    half = owners // 2
    offsets = gather_offsets(owners)
    for u in range(owners):
        band = lax.axis_index("lat") ^ sum(o for k, o in enumerate(offsets) if u >> k & 1)
        ref = first_ref if u < half else second_ref
        out_ref[:, band] = ref[u % half]


def arrange(first, second, after):
    _, owners, rows, half = first.shape
    whole = pl.BlockSpec(memory_space=pltpu.VMEM)
    return pl.pallas_call(
        arrange_kernel,
        out_shape=jax.ShapeDtypeStruct((owners, owners, rows, half), BF16),
        in_specs=[whole, whole, pl.BlockSpec(memory_space=pl.ANY)],
        out_specs=whole,
        compiler_params=params(),
        name="arrange",
    )(first, second, after)


def add_mixed_kernel(own_ref, received_ref, back_ref, out_ref):
    width = back_ref.shape[-1]
    out_ref[:, :width] = back_ref[...]
    out_ref[:, width:] = (own_ref[...].astype(F32) + received_ref[...].astype(F32)).astype(BF16)


def add_mixed(own, received, back):
    count, width = back.shape
    shape = jax.ShapeDtypeStruct((count, width + own.shape[-1]), BF16)
    return call(add_mixed_kernel, "add_mixed", shape, own, received, back)


def cut_kernel(in_ref, _, out_ref):
    out_ref[...] = in_ref[:, :, in_ref.shape[-1] - out_ref.shape[-1] :]


def cut_mixed(received, after):
    owners, cells, wide = received.shape
    whole = pl.BlockSpec(memory_space=pltpu.VMEM)
    return pl.pallas_call(
        cut_kernel,
        out_shape=jax.ShapeDtypeStruct((owners, cells, wide // 3), BF16),
        in_specs=[whole, pl.BlockSpec(memory_space=pl.ANY)],
        out_specs=whole,
        compiler_params=params(),
        name="cut_mixed",
    )(received, after)


def on_device(tokens, key_mask, w_qkv, w_mix, level_scale, cotangent):
    batch, _, rows, lon, width = tokens.shape
    owners = lax.axis_size("lat")
    parts = owners // batch
    chunk = lon // parts
    cells = rows * chunk
    count = batch * rows * lon
    half = width // 2
    tok_band = tokens.reshape(batch, rows, parts, chunk, width)
    cot_band = cotangent.reshape(batch, rows, parts, chunk, width)
    w_mix = w_mix.reshape(width, width)

    tok_send, cot_own, cot_other = pack(tok_band, cot_band, level_scale)
    tok_col = swap(tok_send).reshape(count, width)
    last = lax.axis_size("lev") // 2
    received = from_level(cot_other, 1)
    offset = 2
    while offset < last:
        cot_own = add(cot_own, received)
        received = from_level(cot_own, offset)
        offset *= 2
    first, second = split_rows(cot_own, received)
    first, received = add(first, from_level(second, last)), from_level(first, last)
    rows = cells // last
    offsets = gather_offsets(owners)
    flow_rows = first
    if last > 2:
        part = lax.axis_index("lev") // 2 % (last // 2)
        flow_rows = lax.dynamic_slice_in_dim(first, part * rows, rows, 1)
    flow_rows = flow_rows[None]
    flow_rows = join(flow_rows, from_owner(flow_rows, offsets[0]))
    flow_band = add_flow(first, second, received, tok_col, flow_rows)
    flow_own = swap(flow_band).reshape(count, half)
    flow = (flow_own, from_level(flow_own, 1))
    chip = lax.shift_right_logical(lax.axis_index("lev"), 1)
    chips = lax.axis_size("lev") // 2

    *saved, attended, mix_own, mix_other = forward(
        tok_col, key_mask, w_qkv, w_mix, chunk, owners, flow_band
    )
    attended = swap(attended)
    mix_terms = before_last(pair_total(mix_own, mix_other))
    for offset in offsets[1:-1]:
        flow_rows = join(flow_rows, from_owner(flow_rows, offset))
    received = from_owner(flow_rows, offsets[-1])
    back_col = backward(tok_col, flow, w_mix, w_qkv, saved, mix_terms[0], flow_rows)
    sent = add_mixed(*mix_terms, back_col)
    back = swap(sent.reshape(owners, cells, width + half))
    d_tokens = make_gradient(cot_band, back)

    factor = 1.0 / math.sqrt(count * owners)
    features = width // owners
    attended = attended.reshape(owners, owners, cells, features)
    attended = [chip_rows(attended, 2, chip ^ k).reshape(-1, features) for k in range(chips)]
    attended[1:] = [from_level(attended[k], 2 * k) for k in range(1, chips)]
    flow_rows = arrange(flow_rows, received, sent).reshape(-1, half)
    grads = mix_gradient(attended, (flow_rows, from_level(flow_rows, 1)), factor)
    mix_grad = grads[0]
    for k in range(1, chips):
        mix_grad += from_level(grads[k], 2 * k).astype(F32)

    mix_band = cut_mixed(back, mix_grad)
    output = make_output(tok_band, level_scale, (mix_band, from_level(mix_band, 1)))
    return (
        output.reshape(tokens.shape),
        d_tokens.reshape(tokens.shape),
        mix_grad.reshape(1, width // owners, width),
    )


def solution(mesh):
    return jax.shard_map(
        on_device,
        mesh=mesh,
        in_specs=(
            P(None, "lev", "lat", None, None),
            P(),
            P(),
            P("lev", None, None),
            P("lev", None),
            P(None, "lev", "lat", None, None),
        ),
        out_specs=(
            P(None, "lev", "lat", None, None),
            P(None, "lev", "lat", None, None),
            P("lev", "lat", None),
        ),
        check_vma=False,
    )
```

```python
import functools
import math

import jax
import jax.numpy as jnp
from jax import lax
from jax.experimental import pallas as pl
from jax.experimental.pallas import tpu as pltpu
from jax.sharding import PartitionSpec as P

HEADS = 16
GROUP = 256

epsilon = 1e-06
score_scale = 0.25

F32 = jnp.float32
BF16 = jnp.bfloat16


def nn(a, b):
    return lax.dot_general(a, b, (((1,), (0,)), ((), ())), preferred_element_type=F32)


def nt(a, b):
    return lax.dot_general(a, b, (((1,), (1,)), ((), ())), preferred_element_type=F32)


def tn(a, b):
    return lax.dot_general(a, b, (((0,), (0,)), ((), ())), preferred_element_type=F32)


def block_mean(head_width):
    row = lax.broadcasted_iota(jnp.int32, (GROUP, GROUP), 0) // head_width
    col = lax.broadcasted_iota(jnp.int32, (GROUP, GROUP), 1) // head_width
    return jnp.where(row == col, 1.0 / head_width, 0.0).astype(BF16)


def params():
    return pltpu.CompilerParams(vmem_limit_bytes=36 * 1024 * 1024)


def half_cols(which, width):
    half = width // 2
    core = lax.axis_index("lev") % 2
    return pl.ds(pl.multiple_of((core ^ which) * half, half), half)


def in_hbm(array):
    return pltpu.with_memory_space_constraint(array, pltpu.HBM)


def call(kernel, name, out_shape, *operands):
    return pl.pallas_call(
        kernel, out_shape=out_shape, compiler_params=params(), name=name
    )(*operands)


def pack_kernel(tok_ref, cot_ref, gain_ref, tok_out, *cot_outs):
    batch, rows, parts, chunk, width = tok_ref.shape
    for b in range(batch):
        for q in range(parts):
            for r in range(rows):
                tok_out[b * parts + q, r * chunk : (r + 1) * chunk, :] = tok_ref[b, r, q]
    for s in range(2):
        cols = half_cols(s, width)
        gain = gain_ref[:, cols]
        for b in range(batch):
            for q in range(parts):
                for r in range(rows):
                    piece = cot_ref[b, r, q, :, cols].astype(F32)
                    cot_outs[s][b * parts + q, r * chunk : (r + 1) * chunk, :] = (
                        piece * gain
                    ).astype(BF16)


def pack(tokens, cot, gain):
    batch, rows, parts, chunk, width = tokens.shape
    shape = (batch * parts, rows * chunk)
    return call(
        pack_kernel,
        "pack",
        [jax.ShapeDtypeStruct(shape + (width,), BF16)]
        + [jax.ShapeDtypeStruct(shape + (width // 2,), BF16)] * 2,
        in_hbm(tokens),
        in_hbm(cot),
        in_hbm(gain),
    )


def output_kernel(tok_ref, gain_ref, own_ref, other_ref, out_ref):
    batch, rows, parts, chunk, width = tok_ref.shape
    for s, ref in enumerate((own_ref, other_ref)):
        cols = half_cols(s, width)
        gain = gain_ref[:, cols]
        for t in range(batch * parts):
            b, q = t // parts, t % parts
            for r in range(rows):
                mixed = ref[t, r * chunk : (r + 1) * chunk, :].astype(F32)
                out_ref[b, r, q, :, cols] = (
                    tok_ref[b, r, q, :, cols].astype(F32) + gain * mixed
                ).astype(BF16)


def make_output(tokens, gain, mixed):
    return call(
        output_kernel,
        "make_output",
        jax.ShapeDtypeStruct(tokens.shape, BF16),
        tokens,
        gain,
        *mixed,
    )


def gradient_kernel(cot_ref, back_ref, out_ref):
    batch, rows, parts, chunk, width = cot_ref.shape
    for b in range(batch):
        for q in range(parts):
            for r in range(rows):
                back = back_ref[b * parts + q, r * chunk : (r + 1) * chunk, :width].astype(F32)
                out_ref[b, r, q] = (cot_ref[b, r, q].astype(F32) + back).astype(BF16)


def make_gradient(cot, back):
    return call(
        gradient_kernel, "make_gradient", jax.ShapeDtypeStruct(cot.shape, BF16), cot, back
    )


def by_head(tile, lane):
    zero = jnp.zeros_like(tile)
    return jnp.concatenate([jnp.where(lane == 0, tile, zero), jnp.where(lane == 1, tile, zero)], axis=0)


def one_head(stacked, lane):
    count = lane.shape[0]
    return jnp.where(lane == 0, stacked[:count], stacked[count:])


def side_by_side(stacked):
    count = stacked.shape[0] // 2
    return jnp.concatenate([stacked[:count], stacked[count:]], axis=1)


def forward_kernel(
    samples, lat_count, chunk, owners,
    tok_ref, mask_ref, wq_ref, wk_ref, wv_ref, wm_ref, _,
    qn_ref, kn_ref, v_ref, rq_ref, rk_ref, ri_ref, p_ref, att_ref, own_ref, other_ref,
    normed_ref, acc_ref, keep_ref,
):
    step = pl.program_id(0)
    count, width = normed_ref.shape
    head_width = width // HEADS

    @pl.when(step == 0)
    def _():
        x = tok_ref[...].astype(F32)
        rx = lax.rsqrt(jnp.mean(x * x, axis=-1, keepdims=True) + epsilon)
        normed_ref[...] = (x * rx).astype(BF16)
        acc_ref[...] = jnp.zeros_like(acc_ref)
        spread = (
            lax.broadcasted_iota(jnp.int32, (lat_count, count), 0)
            == lax.broadcasted_iota(jnp.int32, (lat_count, count), 1) // chunk
        ).astype(F32)
        per_sample = nn(mask_ref[...].astype(F32), spread)
        mine = lax.axis_index("lat") // (owners // samples)
        pick = lax.broadcasted_iota(jnp.int32, (samples, count), 0) == mine
        valid = jnp.sum(jnp.where(pick, per_sample, 0.0), axis=0, keepdims=True)
        same = (
            lax.broadcasted_iota(jnp.int32, (count, count), 0) % chunk
            == lax.broadcasted_iota(jnp.int32, (count, count), 1) % chunk
        )
        keep_ref[...] = jnp.where(same, valid, 0.0)

    normed = normed_ref[...]
    mean_mat = block_mean(head_width)
    q = nn(normed, wq_ref[...])
    k = nn(normed, wk_ref[...])
    v = nn(normed, wv_ref[...]).astype(BF16)
    rq = lax.rsqrt(nn((q * q).astype(BF16), mean_mat) + epsilon)
    rk = lax.rsqrt(nn((k * k).astype(BF16), mean_mat) + epsilon)
    qn = (q * rq).astype(BF16)
    kn = (k * rk).astype(BF16)
    qn_ref[...] = qn
    kn_ref[...] = kn
    v_ref[...] = v
    rq_ref[...] = rq.astype(BF16)
    rk_ref[...] = rk.astype(BF16)
    keep = keep_ref[...]
    keep = jnp.concatenate([keep, keep], axis=0)
    lane = lax.broadcasted_iota(jnp.int32, (count, 128), 1) // head_width
    ones = jnp.ones((count, 128), BF16)
    tiles = []
    for t in range(GROUP // 128):
        cols = slice(t * 128, (t + 1) * 128)
        v_ones = jnp.concatenate([v[:, cols], ones], axis=1)
        e = jnp.exp(nt(by_head(qn[:, cols] * score_scale, lane), kn[:, cols])) * keep
        e = e.astype(BF16)
        p_ref[t] = e
        o = nn(e, v_ones)
        inverse = 1.0 / o[:, 128:]
        tiles.append(one_head(o[:, :128] * inverse, lane))
        ri_ref[:, cols] = one_head(inverse, lane)
    att = jnp.concatenate(tiles, axis=1).astype(BF16)
    features = att_ref.shape[-1]
    for f in range(GROUP // features):
        att_ref[f] = att[:, f * features : (f + 1) * features]
    acc_ref[...] += nn(att, wm_ref[...])

    @pl.when(step == pl.num_programs(0) - 1)
    def _():
        for s, ref in enumerate((own_ref, other_ref)):
            ref[...] = acc_ref[:, half_cols(s, width)].astype(BF16)


def forward(tok_col, key_mask, w_qkv, w_mix, chunk, owners, after):
    count, width = tok_col.shape
    samples, lat_count = key_mask.shape
    steps = width // GROUP
    features = width // owners
    same = lambda shape: pl.BlockSpec(shape, lambda i: (0, 0))
    cols = pl.BlockSpec((count, GROUP), lambda i: (0, i))
    weight = lambda which: pl.BlockSpec((width, GROUP), lambda i: (0, i + which * steps))
    return pl.pallas_call(
        functools.partial(forward_kernel, samples, lat_count, chunk, owners),
        out_shape=(
            [pltpu.HBM((count, width), BF16)] * 5
            + [pltpu.HBM((count, width), F32)]
            + [pltpu.HBM((width // 128, 2 * count, count), BF16)]
            + [jax.ShapeDtypeStruct((owners, count, features), BF16)]
            + [jax.ShapeDtypeStruct((count, width // 2), BF16)] * 2
        ),
        grid=(steps,),
        in_specs=[
            same((count, width)),
            same((samples, lat_count)),
            weight(0),
            weight(1),
            weight(2),
            pl.BlockSpec((GROUP, width), lambda i: (i, 0)),
            pl.BlockSpec(memory_space=pl.ANY),
        ],
        out_specs=(
            [cols] * 6
            + [pl.BlockSpec((GROUP // 128, 2 * count, count), lambda i: (i, 0, 0))]
            + [pl.BlockSpec((GROUP // features, count, features), lambda i: (i, 0, 0))]
            + [same((count, width // 2))] * 2
        ),
        scratch_shapes=[
            pltpu.VMEM((count, width), BF16),
            pltpu.VMEM((count, width), F32),
            pltpu.VMEM((count, count), F32),
        ],
        compiler_params=params(),
        cost_estimate=pl.CostEstimate(
            flops=2 * count * width * (4 * width + 2 * count * 4),
            bytes_accessed=20 * count * width + 8 * width * width,
            transcendentals=HEADS * count * count,
        ),
        name="forward",
    )(tok_col, key_mask, *[in_hbm(w_qkv)] * 3, in_hbm(w_mix), after)


def backward_kernel(
    tok_ref, own_ref, other_ref, wm_ref, wq_ref, wk_ref, wv_ref,
    qn_ref, kn_ref, v_ref, rq_ref, rk_ref, ri_ref, p_ref, *rest,
):
    out_ref, acc_ref, flow_t_ref = rest[-3:]
    step = pl.program_id(0)
    width, count = acc_ref.shape
    head_width = width // HEADS

    @pl.when(step == 0)
    def _():
        for s, ref in enumerate((own_ref, other_ref)):
            flow_t_ref[half_cols(s, width), :] = ref[...].T

    d_att = nn(wm_ref[...], flow_t_ref[...]).T
    inverse = ri_ref[...]
    d_att = (d_att * inverse).astype(BF16)
    qn, kn, v = qn_ref[...], kn_ref[...], v_ref[...]
    lane = lax.broadcasted_iota(jnp.int32, (count, 128), 1) // head_width
    dq_tiles, dk_tiles, dv_tiles = [], [], []
    for t in range(GROUP // 128):
        cols = slice(t * 128, (t + 1) * 128)
        d_t = d_att[:, cols]
        d_p = nt(by_head(d_t, lane), v[:, cols])
        e = p_ref[t]
        e_wide = e.astype(F32)
        first = t * 128
        second = first + head_width
        row_inverse = jnp.concatenate(
            [inverse[:, first : first + 1], inverse[:, second : second + 1]], axis=0
        )
        weighted = e_wide * d_p
        inner = jnp.sum(weighted, axis=-1, keepdims=True) * row_inverse
        d_s = (weighted - e_wide * inner).astype(BF16)
        dq_tiles.append(one_head(nn(d_s, kn[:, cols]), lane) * score_scale)
        dk_tiles.append(one_head(tn(side_by_side(d_s), qn[:, cols]), lane) * score_scale)
        dv_tiles.append(one_head(tn(side_by_side(e), d_t), lane))
    mean_mat = block_mean(head_width)
    dq = jnp.concatenate(dq_tiles, axis=1)
    dk = jnp.concatenate(dk_tiles, axis=1)
    dv = jnp.concatenate(dv_tiles, axis=1).astype(BF16)

    def through_norm(upstream, unit, factor):
        unit = unit.astype(F32)
        inner = nn((upstream * unit).astype(BF16), mean_mat)
        return (factor.astype(F32) * (upstream - unit * inner)).astype(BF16)

    gq = through_norm(dq, qn, rq_ref[...])
    gk = through_norm(dk, kn, rk_ref[...])
    total = nt(wq_ref[...], gq) + nt(wk_ref[...], gk) + nt(wv_ref[...], dv)

    @pl.when(step == 0)
    def _():
        acc_ref[...] = total

    @pl.when(step > 0)
    def _():
        acc_ref[...] += total

    @pl.when(step == pl.num_programs(0) - 1)
    def _():
        x = tok_ref[...].astype(F32)
        rx = lax.rsqrt(jnp.mean(x * x, axis=-1, keepdims=True) + epsilon)
        d = acc_ref[...].T
        inner = jnp.mean(d * x, axis=-1, keepdims=True)
        out_ref[...] = (rx * d - x * (rx * rx * rx * inner)).astype(BF16)


def backward(tok_col, flow, w_mix, w_qkv, saved, *after):
    count, width = tok_col.shape
    steps = width // GROUP
    same = lambda shape: pl.BlockSpec(shape, lambda i: (0, 0))
    cols = pl.BlockSpec((count, GROUP), lambda i: (0, i))
    weight = lambda which: pl.BlockSpec((width, GROUP), lambda i: (0, i + which * steps))
    return pl.pallas_call(
        backward_kernel,
        out_shape=jax.ShapeDtypeStruct((count, width), BF16),
        grid=(steps,),
        in_specs=[
            same((count, width)),
            same((count, width // 2)),
            same((count, width // 2)),
            pl.BlockSpec((GROUP, width), lambda i: (i, 0)),
            weight(0),
            weight(1),
            weight(2),
            *([cols] * 6),
            pl.BlockSpec((GROUP // 128, 2 * count, count), lambda i: (i, 0, 0)),
        ]
        + [pl.BlockSpec(memory_space=pl.ANY)] * len(after),
        out_specs=same((count, width)),
        scratch_shapes=[pltpu.VMEM((width, count), F32), pltpu.VMEM((width, count), BF16)],
        compiler_params=params(),
        cost_estimate=pl.CostEstimate(
            flops=2 * count * width * (4 * width + 4 * count * 4),
            bytes_accessed=20 * count * width + 8 * width * width,
            transcendentals=0,
        ),
        name="backward",
    )(tok_col, *flow, in_hbm(w_mix), *[in_hbm(w_qkv)] * 3, *map(in_hbm, saved), *after)


def mix_gradient_kernel(factor, own_flow_ref, other_flow_ref, *refs):
    att_refs, out_refs = refs[: len(refs) // 2], refs[len(refs) // 2 :]
    width = out_refs[0].shape[-1]
    for att_ref, out_ref in zip(att_refs, out_refs):
        att = att_ref[...]
        for s, flow_ref in enumerate((own_flow_ref, other_flow_ref)):
            term = tn(att, flow_ref[...]) * factor
            out_ref[:, half_cols(s, width)] = term.astype(out_ref.dtype)


def mix_gradient(attended, flow, factor):
    rows, features = attended[0].shape
    width = 2 * flow[0].shape[-1]
    out = [jax.ShapeDtypeStruct((features, width), F32)]
    out += [jax.ShapeDtypeStruct((features, width), BF16)] * (len(attended) - 1)
    return pl.pallas_call(
        functools.partial(mix_gradient_kernel, factor),
        out_shape=out,
        compiler_params=params(),
        cost_estimate=pl.CostEstimate(
            flops=2 * rows * features * width * len(attended),
            bytes_accessed=2 * rows * (features * len(attended) + width),
            transcendentals=0,
        ),
        name="mix_gradient",
    )(*flow, *attended)


def chip_rows(array, axis, chip):
    rows = array.shape[axis] // (lax.axis_size("lev") // 2)
    return lax.dynamic_slice_in_dim(array, (chip * rows).astype(jnp.uint32), rows, axis)


def swap(block):
    return lax.all_to_all(block, "lat", split_axis=0, concat_axis=0, tiled=True)


def from_level(block, offset):
    return lax.ppermute(block, "lev", [(i, i ^ offset) for i in range(lax.axis_size("lev"))])


def add_kernel(own_ref, received_ref, out_ref):
    out_ref[...] = (own_ref[...].astype(F32) + received_ref[...].astype(F32)).astype(BF16)


def add(own, received):
    return call(add_kernel, "add", jax.ShapeDtypeStruct(own.shape, BF16), own, received)


def pair_total(own, other):
    return add(own, from_level(other, 1))


def before_last(total):
    offset = 2
    while 2 * offset < lax.axis_size("lev"):
        total = add(total, from_level(total, offset))
        offset *= 2
    return total, from_level(total, offset)


def row_half(which, rows):
    top = lax.axis_index("lev") // (lax.axis_size("lev") // 2)
    return pl.ds(pl.multiple_of((top ^ which) * rows, rows), rows)


def split_kernel(own_ref, received_ref, first_ref, second_ref):
    rows = first_ref.shape[1]
    for which, ref in enumerate((first_ref, second_ref)):
        at = row_half(which, rows)
        total = own_ref[:, at, :].astype(F32) + received_ref[:, at, :].astype(F32)
        ref[...] = total.astype(BF16)


def split_rows(own, received):
    owners, cells, half = own.shape
    rows = cells // 2
    if rows % 16 == 0:
        part = jax.ShapeDtypeStruct((owners, rows, half), BF16)
        return call(split_kernel, "split_rows", [part, part], own, received)
    total = (own.astype(F32) + received.astype(F32)).astype(BF16)
    top = lax.axis_index("lev") // (lax.axis_size("lev") // 2)
    return [lax.dynamic_slice_in_dim(total, (top ^ k) * rows, rows, 1) for k in range(2)]


def add_flow_kernel(first_ref, second_ref, received_ref, _, __, out_ref):
    rows = first_ref.shape[1]
    out_ref[:, row_half(0, rows), :] = first_ref[...]
    second = second_ref[...].astype(F32) + received_ref[...].astype(F32)
    out_ref[:, row_half(1, rows), :] = second.astype(BF16)


def add_flow(first, second, received, *after):
    owners, rows, half = first.shape
    if rows % 16:
        second = (second.astype(F32) + received.astype(F32)).astype(BF16)
        top = lax.axis_index("lev") // (lax.axis_size("lev") // 2)
        pair = jnp.where(top == 0, jnp.stack([first, second]), jnp.stack([second, first]))
        return jnp.concatenate([pair[0], pair[1]], axis=1)
    whole = pl.BlockSpec(memory_space=pltpu.VMEM)
    return pl.pallas_call(
        add_flow_kernel,
        out_shape=jax.ShapeDtypeStruct((owners, 2 * rows, half), BF16),
        in_specs=[whole] * 3 + [pl.BlockSpec(memory_space=pl.ANY)] * 2,
        out_specs=whole,
        compiler_params=params(),
        name="add_flow",
    )(first, second, received, *after)


def join_kernel(first_ref, second_ref, out_ref):
    count = first_ref.shape[0]
    out_ref[:count] = first_ref[...]
    out_ref[count:] = second_ref[...]


def join(first, second):
    shape = jax.ShapeDtypeStruct((2 * first.shape[0],) + first.shape[1:], BF16)
    return call(join_kernel, "join", shape, first, second)


def from_owner(block, offset):
    return lax.ppermute(block, "lat", [(i, i ^ offset) for i in range(lax.axis_size("lat"))])


def gather_offsets(owners):
    offsets = [owners // 4, owners // 2]
    while len(offsets) < owners.bit_length() - 1:
        offsets.append(owners >> (len(offsets) + 1))
    return offsets


def arrange_kernel(first_ref, second_ref, _, out_ref):
    owners = out_ref.shape[1]
    half = owners // 2
    offsets = gather_offsets(owners)
    for u in range(owners):
        band = lax.axis_index("lat") ^ sum(o for k, o in enumerate(offsets) if u >> k & 1)
        ref = first_ref if u < half else second_ref
        out_ref[:, band] = ref[u % half]


def arrange(first, second, after):
    _, owners, rows, half = first.shape
    whole = pl.BlockSpec(memory_space=pltpu.VMEM)
    return pl.pallas_call(
        arrange_kernel,
        out_shape=jax.ShapeDtypeStruct((owners, owners, rows, half), BF16),
        in_specs=[whole, whole, pl.BlockSpec(memory_space=pl.ANY)],
        out_specs=whole,
        compiler_params=params(),
        name="arrange",
    )(first, second, after)


def add_mixed_kernel(own_ref, received_ref, back_ref, out_ref):
    width = back_ref.shape[-1]
    out_ref[:, :width] = back_ref[...]
    out_ref[:, width:] = (own_ref[...].astype(F32) + received_ref[...].astype(F32)).astype(BF16)


def add_mixed(own, received, back):
    count, width = back.shape
    shape = jax.ShapeDtypeStruct((count, width + own.shape[-1]), BF16)
    return call(add_mixed_kernel, "add_mixed", shape, own, received, back)


def cut_kernel(in_ref, _, out_ref):
    out_ref[...] = in_ref[:, :, in_ref.shape[-1] - out_ref.shape[-1] :]


def cut_mixed(received, after):
    owners, cells, wide = received.shape
    whole = pl.BlockSpec(memory_space=pltpu.VMEM)
    return pl.pallas_call(
        cut_kernel,
        out_shape=jax.ShapeDtypeStruct((owners, cells, wide // 3), BF16),
        in_specs=[whole, pl.BlockSpec(memory_space=pl.ANY)],
        out_specs=whole,
        compiler_params=params(),
        name="cut_mixed",
    )(received, after)


def on_device(tokens, key_mask, w_qkv, w_mix, level_scale, cotangent):
    batch, _, rows, lon, width = tokens.shape
    owners = lax.axis_size("lat")
    parts = owners // batch
    chunk = lon // parts
    cells = rows * chunk
    count = batch * rows * lon
    half = width // 2
    tok_band = tokens.reshape(batch, rows, parts, chunk, width)
    cot_band = cotangent.reshape(batch, rows, parts, chunk, width)
    w_mix = w_mix.reshape(width, width)

    tok_send, cot_own, cot_other = pack(tok_band, cot_band, level_scale)
    tok_col = swap(tok_send).reshape(count, width)
    last = lax.axis_size("lev") // 2
    received = from_level(cot_other, 1)
    offset = 2
    while offset < last:
        cot_own = add(cot_own, received)
        received = from_level(cot_own, offset)
        offset *= 2
    first, second = split_rows(cot_own, received)
    first, received = add(first, from_level(second, last)), from_level(first, last)
    rows = cells // last
    offsets = gather_offsets(owners)
    flow_rows = first
    if last > 2:
        part = lax.axis_index("lev") // 2 % (last // 2)
        flow_rows = lax.dynamic_slice_in_dim(first, part * rows, rows, 1)
    flow_rows = flow_rows[None]
    flow_rows = join(flow_rows, from_owner(flow_rows, offsets[0]))
    flow_band = add_flow(first, second, received, tok_col, flow_rows)
    flow_own = swap(flow_band).reshape(count, half)
    flow = (flow_own, from_level(flow_own, 1))
    chip = lax.shift_right_logical(lax.axis_index("lev"), 1)
    chips = lax.axis_size("lev") // 2

    *saved, attended, mix_own, mix_other = forward(
        tok_col, key_mask, w_qkv, w_mix, chunk, owners, flow_band
    )
    attended = swap(attended)
    mix_terms = before_last(pair_total(mix_own, mix_other))
    for offset in offsets[1:-1]:
        flow_rows = join(flow_rows, from_owner(flow_rows, offset))
    received = from_owner(flow_rows, offsets[-1])
    back_col = backward(tok_col, flow, w_mix, w_qkv, saved, mix_terms[0], flow_rows)
    sent = add_mixed(*mix_terms, back_col)
    back = swap(sent.reshape(owners, cells, width + half))
    d_tokens = make_gradient(cot_band, back)

    factor = 1.0 / math.sqrt(count * owners)
    features = width // owners
    attended = attended.reshape(owners, owners, cells, features)
    attended = [chip_rows(attended, 2, chip ^ k).reshape(-1, features) for k in range(chips)]
    attended[1:] = [from_level(attended[k], 2 * k) for k in range(1, chips)]
    flow_rows = arrange(flow_rows, received, sent).reshape(-1, half)
    grads = mix_gradient(attended, (flow_rows, from_level(flow_rows, 1)), factor)
    mix_grad = grads[0]
    for k in range(1, chips):
        mix_grad += from_level(grads[k], 2 * k).astype(F32)

    mix_band = cut_mixed(back, mix_grad)
    output = make_output(tok_band, level_scale, (mix_band, from_level(mix_band, 1)))
    return (
        output.reshape(tokens.shape),
        d_tokens.reshape(tokens.shape),
        mix_grad.reshape(1, width // owners, width),
    )


def solution(mesh):
    return jax.shard_map(
        on_device,
        mesh=mesh,
        in_specs=(
            P(None, "lev", "lat", None, None),
            P(),
            P(),
            P("lev", None, None),
            P("lev", None),
            P(None, "lev", "lat", None, None),
        ),
        out_specs=(
            P(None, "lev", "lat", None, None),
            P(None, "lev", "lat", None, None),
            P("lev", "lat", None),
        ),
        check_vma=False,
    )
```

```python
import functools
import math

import jax
import jax.numpy as jnp
from jax import lax
from jax.experimental import pallas as pl
from jax.experimental.pallas import tpu as pltpu
from jax.sharding import PartitionSpec as P

HEADS = 16
GROUP = 256

epsilon = 1e-06
score_scale = 0.25

F32 = jnp.float32
BF16 = jnp.bfloat16


def nn(a, b):
    return lax.dot_general(a, b, (((1,), (0,)), ((), ())), preferred_element_type=F32)


def nt(a, b):
    return lax.dot_general(a, b, (((1,), (1,)), ((), ())), preferred_element_type=F32)


def tn(a, b):
    return lax.dot_general(a, b, (((0,), (0,)), ((), ())), preferred_element_type=F32)


def block_mean(head_width):
    row = lax.broadcasted_iota(jnp.int32, (GROUP, GROUP), 0) // head_width
    col = lax.broadcasted_iota(jnp.int32, (GROUP, GROUP), 1) // head_width
    return jnp.where(row == col, 1.0 / head_width, 0.0).astype(BF16)


def params():
    return pltpu.CompilerParams(vmem_limit_bytes=36 * 1024 * 1024)


def half_cols(which, width):
    half = width // 2
    core = lax.axis_index("lev") % 2
    return pl.ds(pl.multiple_of((core ^ which) * half, half), half)


def in_hbm(array):
    return pltpu.with_memory_space_constraint(array, pltpu.HBM)


def call(kernel, name, out_shape, *operands):
    return pl.pallas_call(
        kernel, out_shape=out_shape, compiler_params=params(), name=name
    )(*operands)


def pack_kernel(tok_ref, cot_ref, gain_ref, tok_out, *cot_outs):
    batch, rows, parts, chunk, width = tok_ref.shape
    for b in range(batch):
        for q in range(parts):
            for r in range(rows):
                tok_out[b * parts + q, r * chunk : (r + 1) * chunk, :] = tok_ref[b, r, q]
    for s in range(2):
        cols = half_cols(s, width)
        gain = gain_ref[:, cols]
        for b in range(batch):
            for q in range(parts):
                for r in range(rows):
                    piece = cot_ref[b, r, q, :, cols].astype(F32)
                    cot_outs[s][b * parts + q, r * chunk : (r + 1) * chunk, :] = (
                        piece * gain
                    ).astype(BF16)


def pack(tokens, cot, gain):
    batch, rows, parts, chunk, width = tokens.shape
    shape = (batch * parts, rows * chunk)
    return call(
        pack_kernel,
        "pack",
        [jax.ShapeDtypeStruct(shape + (width,), BF16)]
        + [jax.ShapeDtypeStruct(shape + (width // 2,), BF16)] * 2,
        in_hbm(tokens),
        in_hbm(cot),
        in_hbm(gain),
    )


def output_kernel(tok_ref, gain_ref, own_ref, other_ref, out_ref):
    batch, rows, parts, chunk, width = tok_ref.shape
    for s, ref in enumerate((own_ref, other_ref)):
        cols = half_cols(s, width)
        gain = gain_ref[:, cols]
        for t in range(batch * parts):
            b, q = t // parts, t % parts
            for r in range(rows):
                mixed = ref[t, r * chunk : (r + 1) * chunk, :].astype(F32)
                out_ref[b, r, q, :, cols] = (
                    tok_ref[b, r, q, :, cols].astype(F32) + gain * mixed
                ).astype(BF16)


def make_output(tokens, gain, mixed):
    return call(
        output_kernel,
        "make_output",
        jax.ShapeDtypeStruct(tokens.shape, BF16),
        tokens,
        gain,
        *mixed,
    )


def gradient_kernel(cot_ref, back_ref, out_ref):
    batch, rows, parts, chunk, width = cot_ref.shape
    for b in range(batch):
        for q in range(parts):
            for r in range(rows):
                back = back_ref[b * parts + q, r * chunk : (r + 1) * chunk, :width].astype(F32)
                out_ref[b, r, q] = (cot_ref[b, r, q].astype(F32) + back).astype(BF16)


def make_gradient(cot, back):
    return call(
        gradient_kernel, "make_gradient", jax.ShapeDtypeStruct(cot.shape, BF16), cot, back
    )


def by_head(tile, lane):
    zero = jnp.zeros_like(tile)
    return jnp.concatenate([jnp.where(lane == 0, tile, zero), jnp.where(lane == 1, tile, zero)], axis=0)


def own_rows(turned, head_width):
    count = turned.shape[1] // 2
    return [turned[:head_width, :count], turned[head_width:, count:]]


def side_by_side(stacked):
    count = stacked.shape[0] // 2
    return jnp.concatenate([stacked[:count], stacked[count:]], axis=1)


def forward_kernel(
    samples, lat_count, chunk, owners,
    tok_ref, mask_ref, wq_ref, wk_ref, wv_ref, wm_ref, _,
    qn_ref, kn_ref, v_ref, rq_ref, rk_ref, ri_ref, p_ref, att_ref, own_ref, other_ref,
    normed_ref, acc_ref, keep_ref,
):
    step = pl.program_id(0)
    count, width = normed_ref.shape
    head_width = width // HEADS

    @pl.when(step == 0)
    def _():
        x = tok_ref[...].astype(F32)
        rx = lax.rsqrt(jnp.mean(x * x, axis=-1, keepdims=True) + epsilon)
        normed_ref[...] = (x * rx).astype(BF16)
        acc_ref[...] = jnp.zeros_like(acc_ref)
        spread = (
            lax.broadcasted_iota(jnp.int32, (lat_count, count), 0)
            == lax.broadcasted_iota(jnp.int32, (lat_count, count), 1) // chunk
        ).astype(F32)
        per_sample = nn(mask_ref[...].astype(F32), spread)
        mine = lax.axis_index("lat") // (owners // samples)
        pick = lax.broadcasted_iota(jnp.int32, (samples, count), 0) == mine
        valid = jnp.sum(jnp.where(pick, per_sample, 0.0), axis=0, keepdims=True)
        same = (
            lax.broadcasted_iota(jnp.int32, (count, count), 0) % chunk
            == lax.broadcasted_iota(jnp.int32, (count, count), 1) % chunk
        )
        keep_ref[...] = jnp.where(same, valid, 0.0)

    normed = normed_ref[...]
    mean_mat = block_mean(head_width)
    q = nn(normed, wq_ref[...])
    k = nn(normed, wk_ref[...])
    v = nn(normed, wv_ref[...]).astype(BF16)
    rq = lax.rsqrt(nn((q * q).astype(BF16), mean_mat) + epsilon)
    rk = lax.rsqrt(nn((k * k).astype(BF16), mean_mat) + epsilon)
    qn = (q * rq).astype(BF16)
    kn = (k * rk).astype(BF16)
    qn_ref[...] = qn
    kn_ref[...] = kn
    v_ref[...] = v
    rq_ref[...] = rq.astype(BF16)
    rk_ref[...] = rk.astype(BF16)
    keep = keep_ref[...]
    keep = jnp.concatenate([keep, keep], axis=0)
    lane = lax.broadcasted_iota(jnp.int32, (count, 128), 1) // head_width
    ones = by_head(jnp.ones((count, 128), BF16), lane)
    tiles = []
    for t in range(GROUP // 128):
        cols = slice(t * 128, (t + 1) * 128)
        v_ones = jnp.concatenate([by_head(v[:, cols], lane), ones], axis=1)
        e = jnp.exp(nt(by_head(qn[:, cols] * score_scale, lane), kn[:, cols])) * keep
        e = e.astype(BF16)
        p_ref[t] = e
        o = nn(side_by_side(e), v_ones)
        inverse = 1.0 / o[:, 128:]
        tiles.append(o[:, :128] * inverse)
        ri_ref[:, cols] = inverse
    att = jnp.concatenate(tiles, axis=1).astype(BF16)
    features = att_ref.shape[-1]
    for f in range(GROUP // features):
        att_ref[f] = att[:, f * features : (f + 1) * features]
    acc_ref[...] += nn(att, wm_ref[...])

    @pl.when(step == pl.num_programs(0) - 1)
    def _():
        for s, ref in enumerate((own_ref, other_ref)):
            ref[...] = acc_ref[:, half_cols(s, width)].astype(BF16)


def forward(tok_col, key_mask, w_qkv, w_mix, chunk, owners, after):
    count, width = tok_col.shape
    samples, lat_count = key_mask.shape
    steps = width // GROUP
    features = width // owners
    same = lambda shape: pl.BlockSpec(shape, lambda i: (0, 0))
    cols = pl.BlockSpec((count, GROUP), lambda i: (0, i))
    weight = lambda which: pl.BlockSpec((width, GROUP), lambda i: (0, i + which * steps))
    return pl.pallas_call(
        functools.partial(forward_kernel, samples, lat_count, chunk, owners),
        out_shape=(
            [pltpu.HBM((count, width), BF16)] * 5
            + [pltpu.HBM((count, width), F32)]
            + [pltpu.HBM((width // 128, 2 * count, count), BF16)]
            + [jax.ShapeDtypeStruct((owners, count, features), BF16)]
            + [jax.ShapeDtypeStruct((count, width // 2), BF16)] * 2
        ),
        grid=(steps,),
        in_specs=[
            same((count, width)),
            same((samples, lat_count)),
            weight(0),
            weight(1),
            weight(2),
            pl.BlockSpec((GROUP, width), lambda i: (i, 0)),
            pl.BlockSpec(memory_space=pl.ANY),
        ],
        out_specs=(
            [cols] * 6
            + [pl.BlockSpec((GROUP // 128, 2 * count, count), lambda i: (i, 0, 0))]
            + [pl.BlockSpec((GROUP // features, count, features), lambda i: (i, 0, 0))]
            + [same((count, width // 2))] * 2
        ),
        scratch_shapes=[
            pltpu.VMEM((count, width), BF16),
            pltpu.VMEM((count, width), F32),
            pltpu.VMEM((count, count), F32),
        ],
        compiler_params=params(),
        cost_estimate=pl.CostEstimate(
            flops=2 * count * width * (4 * width + 2 * count * 4),
            bytes_accessed=20 * count * width + 8 * width * width,
            transcendentals=HEADS * count * count,
        ),
        name="forward",
    )(tok_col, key_mask, *[in_hbm(w_qkv)] * 3, in_hbm(w_mix), after)


def backward_kernel(
    tok_ref, own_ref, other_ref, wm_ref, wq_ref, wk_ref, wv_ref,
    qn_ref, kn_ref, v_ref, rq_ref, rk_ref, ri_ref, p_ref, *rest,
):
    out_ref, acc_ref = rest[-2:]
    step = pl.program_id(0)
    count, width = acc_ref.shape
    head_width = width // HEADS
    d_att = nt(own_ref[...], wm_ref[:, half_cols(0, width)])
    d_att += nt(other_ref[...], wm_ref[:, half_cols(1, width)])
    inverse = ri_ref[...]
    d_att = (d_att * inverse).astype(BF16)
    qn, kn, v = qn_ref[...], kn_ref[...], v_ref[...]
    lane = lax.broadcasted_iota(jnp.int32, (count, 128), 1) // head_width
    dq_tiles, dk_tiles, dv_tiles = [], [], []
    for t in range(GROUP // 128):
        cols = slice(t * 128, (t + 1) * 128)
        d_t = d_att[:, cols]
        d_p = nt(by_head(d_t, lane), v[:, cols])
        e = p_ref[t]
        e_wide = e.astype(F32)
        first = t * 128
        second = first + head_width
        row_inverse = jnp.concatenate(
            [inverse[:, first : first + 1], inverse[:, second : second + 1]], axis=0
        )
        weighted = e_wide * d_p
        inner = jnp.sum(weighted, axis=-1, keepdims=True) * row_inverse
        d_s = (weighted - e_wide * inner).astype(BF16)
        d_s = side_by_side(d_s)
        dq_tiles.append(nn(d_s, by_head(kn[:, cols], lane)))
        dk_tiles += own_rows(tn(qn[:, cols], d_s), head_width)
        dv_tiles += own_rows(tn(d_t, side_by_side(e)), head_width)
    mean_mat = block_mean(head_width)
    dq = jnp.concatenate(dq_tiles, axis=1) * score_scale
    dk = jnp.concatenate(dk_tiles, axis=0).T * score_scale
    dv = jnp.concatenate(dv_tiles, axis=0).T.astype(BF16)

    def through_norm(upstream, unit, factor):
        unit = unit.astype(F32)
        inner = nn((upstream * unit).astype(BF16), mean_mat)
        return (factor.astype(F32) * (upstream - unit * inner)).astype(BF16)

    gq = through_norm(dq, qn, rq_ref[...])
    gk = through_norm(dk, kn, rk_ref[...])
    total = nt(gq, wq_ref[...]) + nt(gk, wk_ref[...]) + nt(dv, wv_ref[...])

    @pl.when(step == 0)
    def _():
        acc_ref[...] = total

    @pl.when(step > 0)
    def _():
        acc_ref[...] += total

    @pl.when(step == pl.num_programs(0) - 1)
    def _():
        x = tok_ref[...].astype(F32)
        rx = lax.rsqrt(jnp.mean(x * x, axis=-1, keepdims=True) + epsilon)
        d = acc_ref[...]
        inner = jnp.mean(d * x, axis=-1, keepdims=True)
        out_ref[...] = (rx * d - x * (rx * rx * rx * inner)).astype(BF16)


def backward(tok_col, flow, w_mix, w_qkv, saved, *after):
    count, width = tok_col.shape
    steps = width // GROUP
    same = lambda shape: pl.BlockSpec(shape, lambda i: (0, 0))
    cols = pl.BlockSpec((count, GROUP), lambda i: (0, i))
    weight = lambda which: pl.BlockSpec((width, GROUP), lambda i: (0, i + which * steps))
    return pl.pallas_call(
        backward_kernel,
        out_shape=jax.ShapeDtypeStruct((count, width), BF16),
        grid=(steps,),
        in_specs=[
            same((count, width)),
            same((count, width // 2)),
            same((count, width // 2)),
            pl.BlockSpec((GROUP, width), lambda i: (i, 0)),
            weight(0),
            weight(1),
            weight(2),
            *([cols] * 6),
            pl.BlockSpec((GROUP // 128, 2 * count, count), lambda i: (i, 0, 0)),
        ]
        + [pl.BlockSpec(memory_space=pl.ANY)] * len(after),
        out_specs=same((count, width)),
        scratch_shapes=[pltpu.VMEM((count, width), F32)],
        compiler_params=params(),
        cost_estimate=pl.CostEstimate(
            flops=2 * count * width * (4 * width + 4 * count * 4),
            bytes_accessed=20 * count * width + 8 * width * width,
            transcendentals=0,
        ),
        name="backward",
    )(tok_col, *flow, in_hbm(w_mix), *[in_hbm(w_qkv)] * 3, *map(in_hbm, saved), *after)


def mix_gradient_kernel(factor, own_flow_ref, other_flow_ref, *refs):
    att_refs, out_refs = refs[: len(refs) // 2], refs[len(refs) // 2 :]
    width = out_refs[0].shape[-1]
    for att_ref, out_ref in zip(att_refs, out_refs):
        att = att_ref[...]
        for s, flow_ref in enumerate((own_flow_ref, other_flow_ref)):
            term = tn(att, flow_ref[...]) * factor
            out_ref[:, half_cols(s, width)] = term.astype(out_ref.dtype)


def mix_gradient(attended, flow, factor):
    rows, features = attended[0].shape
    width = 2 * flow[0].shape[-1]
    out = [jax.ShapeDtypeStruct((features, width), F32)]
    out += [jax.ShapeDtypeStruct((features, width), BF16)] * (len(attended) - 1)
    return pl.pallas_call(
        functools.partial(mix_gradient_kernel, factor),
        out_shape=out,
        compiler_params=params(),
        cost_estimate=pl.CostEstimate(
            flops=2 * rows * features * width * len(attended),
            bytes_accessed=2 * rows * (features * len(attended) + width),
            transcendentals=0,
        ),
        name="mix_gradient",
    )(*flow, *attended)


def chip_rows(array, axis, chip):
    rows = array.shape[axis] // (lax.axis_size("lev") // 2)
    return lax.dynamic_slice_in_dim(array, (chip * rows).astype(jnp.uint32), rows, axis)


def swap(block):
    return lax.all_to_all(block, "lat", split_axis=0, concat_axis=0, tiled=True)


def from_level(block, offset):
    return lax.ppermute(block, "lev", [(i, i ^ offset) for i in range(lax.axis_size("lev"))])


def add_kernel(own_ref, received_ref, out_ref):
    out_ref[...] = (own_ref[...].astype(F32) + received_ref[...].astype(F32)).astype(BF16)


def add(own, received):
    return call(add_kernel, "add", jax.ShapeDtypeStruct(own.shape, BF16), own, received)


def pair_total(own, other):
    return add(own, from_level(other, 1))


def before_last(total):
    offset = 2
    while 2 * offset < lax.axis_size("lev"):
        total = add(total, from_level(total, offset))
        offset *= 2
    return total, from_level(total, offset)


def row_half(which, rows):
    top = lax.axis_index("lev") // (lax.axis_size("lev") // 2)
    return pl.ds(pl.multiple_of((top ^ which) * rows, rows), rows)


def split_kernel(own_ref, received_ref, first_ref, second_ref):
    rows = first_ref.shape[1]
    for which, ref in enumerate((first_ref, second_ref)):
        at = row_half(which, rows)
        total = own_ref[:, at, :].astype(F32) + received_ref[:, at, :].astype(F32)
        ref[...] = total.astype(BF16)


def split_rows(own, received):
    owners, cells, half = own.shape
    rows = cells // 2
    if rows % 16 == 0:
        part = jax.ShapeDtypeStruct((owners, rows, half), BF16)
        return call(split_kernel, "split_rows", [part, part], own, received)
    total = (own.astype(F32) + received.astype(F32)).astype(BF16)
    top = lax.axis_index("lev") // (lax.axis_size("lev") // 2)
    return [lax.dynamic_slice_in_dim(total, (top ^ k) * rows, rows, 1) for k in range(2)]


def add_flow_kernel(first_ref, second_ref, received_ref, _, __, out_ref):
    rows = first_ref.shape[1]
    out_ref[:, row_half(0, rows), :] = first_ref[...]
    second = second_ref[...].astype(F32) + received_ref[...].astype(F32)
    out_ref[:, row_half(1, rows), :] = second.astype(BF16)


def add_flow(first, second, received, *after):
    owners, rows, half = first.shape
    if rows % 16:
        second = (second.astype(F32) + received.astype(F32)).astype(BF16)
        top = lax.axis_index("lev") // (lax.axis_size("lev") // 2)
        pair = jnp.where(top == 0, jnp.stack([first, second]), jnp.stack([second, first]))
        return jnp.concatenate([pair[0], pair[1]], axis=1)
    whole = pl.BlockSpec(memory_space=pltpu.VMEM)
    return pl.pallas_call(
        add_flow_kernel,
        out_shape=jax.ShapeDtypeStruct((owners, 2 * rows, half), BF16),
        in_specs=[whole] * 3 + [pl.BlockSpec(memory_space=pl.ANY)] * 2,
        out_specs=whole,
        compiler_params=params(),
        name="add_flow",
    )(first, second, received, *after)


def join_kernel(first_ref, second_ref, out_ref):
    count = first_ref.shape[0]
    out_ref[:count] = first_ref[...]
    out_ref[count:] = second_ref[...]


def join(first, second):
    shape = jax.ShapeDtypeStruct((2 * first.shape[0],) + first.shape[1:], BF16)
    return call(join_kernel, "join", shape, first, second)


def from_owner(block, offset):
    return lax.ppermute(block, "lat", [(i, i ^ offset) for i in range(lax.axis_size("lat"))])


def gather_offsets(owners):
    offsets = [owners // 4, owners // 2]
    while len(offsets) < owners.bit_length() - 1:
        offsets.append(owners >> (len(offsets) + 1))
    return offsets


def arrange_kernel(first_ref, second_ref, _, out_ref):
    owners = out_ref.shape[1]
    half = owners // 2
    offsets = gather_offsets(owners)
    for u in range(owners):
        band = lax.axis_index("lat") ^ sum(o for k, o in enumerate(offsets) if u >> k & 1)
        ref = first_ref if u < half else second_ref
        out_ref[:, band] = ref[u % half]


def arrange(first, second, after):
    _, owners, rows, half = first.shape
    whole = pl.BlockSpec(memory_space=pltpu.VMEM)
    return pl.pallas_call(
        arrange_kernel,
        out_shape=jax.ShapeDtypeStruct((owners, owners, rows, half), BF16),
        in_specs=[whole, whole, pl.BlockSpec(memory_space=pl.ANY)],
        out_specs=whole,
        compiler_params=params(),
        name="arrange",
    )(first, second, after)


def add_mixed_kernel(own_ref, received_ref, back_ref, out_ref):
    width = back_ref.shape[-1]
    out_ref[:, :width] = back_ref[...]
    out_ref[:, width:] = (own_ref[...].astype(F32) + received_ref[...].astype(F32)).astype(BF16)


def add_mixed(own, received, back):
    count, width = back.shape
    shape = jax.ShapeDtypeStruct((count, width + own.shape[-1]), BF16)
    return call(add_mixed_kernel, "add_mixed", shape, own, received, back)


def cut_kernel(in_ref, _, out_ref):
    out_ref[...] = in_ref[:, :, in_ref.shape[-1] - out_ref.shape[-1] :]


def cut_mixed(received, after):
    owners, cells, wide = received.shape
    whole = pl.BlockSpec(memory_space=pltpu.VMEM)
    return pl.pallas_call(
        cut_kernel,
        out_shape=jax.ShapeDtypeStruct((owners, cells, wide // 3), BF16),
        in_specs=[whole, pl.BlockSpec(memory_space=pl.ANY)],
        out_specs=whole,
        compiler_params=params(),
        name="cut_mixed",
    )(received, after)


def on_device(tokens, key_mask, w_qkv, w_mix, level_scale, cotangent):
    batch, _, rows, lon, width = tokens.shape
    owners = lax.axis_size("lat")
    parts = owners // batch
    chunk = lon // parts
    cells = rows * chunk
    count = batch * rows * lon
    half = width // 2
    tok_band = tokens.reshape(batch, rows, parts, chunk, width)
    cot_band = cotangent.reshape(batch, rows, parts, chunk, width)
    w_mix = w_mix.reshape(width, width)

    tok_send, cot_own, cot_other = pack(tok_band, cot_band, level_scale)
    tok_col = swap(tok_send).reshape(count, width)
    last = lax.axis_size("lev") // 2
    received = from_level(cot_other, 1)
    offset = 2
    while offset < last:
        cot_own = add(cot_own, received)
        received = from_level(cot_own, offset)
        offset *= 2
    first, second = split_rows(cot_own, received)
    first, received = add(first, from_level(second, last)), from_level(first, last)
    rows = cells // last
    offsets = gather_offsets(owners)
    flow_rows = first
    if last > 2:
        part = lax.axis_index("lev") // 2 % (last // 2)
        flow_rows = lax.dynamic_slice_in_dim(first, part * rows, rows, 1)
    flow_rows = flow_rows[None]
    flow_rows = join(flow_rows, from_owner(flow_rows, offsets[0]))
    flow_band = add_flow(first, second, received, tok_col, flow_rows)
    flow_own = swap(flow_band).reshape(count, half)
    flow = (flow_own, from_level(flow_own, 1))
    chip = lax.shift_right_logical(lax.axis_index("lev"), 1)
    chips = lax.axis_size("lev") // 2

    *saved, attended, mix_own, mix_other = forward(
        tok_col, key_mask, w_qkv, w_mix, chunk, owners, flow_band
    )
    attended = swap(attended)
    mix_terms = before_last(pair_total(mix_own, mix_other))
    for offset in offsets[1:-1]:
        flow_rows = join(flow_rows, from_owner(flow_rows, offset))
    received = from_owner(flow_rows, offsets[-1])
    back_col = backward(tok_col, flow, w_mix, w_qkv, saved, mix_terms[0], flow_rows)
    sent = add_mixed(*mix_terms, back_col)
    back = swap(sent.reshape(owners, cells, width + half))
    d_tokens = make_gradient(cot_band, back)

    factor = 1.0 / math.sqrt(count * owners)
    features = width // owners
    attended = attended.reshape(owners, owners, cells, features)
    attended = [chip_rows(attended, 2, chip ^ k).reshape(-1, features) for k in range(chips)]
    attended[1:] = [from_level(attended[k], 2 * k) for k in range(1, chips)]
    flow_rows = arrange(flow_rows, received, sent).reshape(-1, half)
    grads = mix_gradient(attended, (flow_rows, from_level(flow_rows, 1)), factor)
    mix_grad = grads[0]
    for k in range(1, chips):
        mix_grad += from_level(grads[k], 2 * k).astype(F32)

    mix_band = cut_mixed(back, mix_grad)
    output = make_output(tok_band, level_scale, (mix_band, from_level(mix_band, 1)))
    return (
        output.reshape(tokens.shape),
        d_tokens.reshape(tokens.shape),
        mix_grad.reshape(1, width // owners, width),
    )


def solution(mesh):
    return jax.shard_map(
        on_device,
        mesh=mesh,
        in_specs=(
            P(None, "lev", "lat", None, None),
            P(),
            P(),
            P("lev", None, None),
            P("lev", None),
            P(None, "lev", "lat", None, None),
        ),
        out_specs=(
            P(None, "lev", "lat", None, None),
            P(None, "lev", "lat", None, None),
            P("lev", "lat", None),
        ),
        check_vma=False,
    )
```

```python
import functools
import math

import jax
import jax.numpy as jnp
from jax import lax
from jax.experimental import pallas as pl
from jax.experimental.pallas import tpu as pltpu
from jax.sharding import PartitionSpec as P

HEADS = 16
GROUP = 256

epsilon = 1e-06
score_scale = 0.25

F32 = jnp.float32
BF16 = jnp.bfloat16


def nn(a, b):
    return lax.dot_general(a, b, (((1,), (0,)), ((), ())), preferred_element_type=F32)


def nt(a, b):
    return lax.dot_general(a, b, (((1,), (1,)), ((), ())), preferred_element_type=F32)


def tn(a, b):
    return lax.dot_general(a, b, (((0,), (0,)), ((), ())), preferred_element_type=F32)


def block_mean(head_width):
    row = lax.broadcasted_iota(jnp.int32, (GROUP, GROUP), 0) // head_width
    col = lax.broadcasted_iota(jnp.int32, (GROUP, GROUP), 1) // head_width
    return jnp.where(row == col, 1.0 / head_width, 0.0).astype(BF16)


def params():
    return pltpu.CompilerParams(vmem_limit_bytes=36 * 1024 * 1024)


def half_cols(which, width):
    half = width // 2
    core = lax.axis_index("lev") % 2
    return pl.ds(pl.multiple_of((core ^ which) * half, half), half)


def in_hbm(array):
    return pltpu.with_memory_space_constraint(array, pltpu.HBM)


def call(kernel, name, out_shape, *operands):
    return pl.pallas_call(
        kernel, out_shape=out_shape, compiler_params=params(), name=name
    )(*operands)


def pack_kernel(tok_ref, cot_ref, gain_ref, tok_out, *cot_outs):
    batch, rows, parts, chunk, width = tok_ref.shape
    for b in range(batch):
        for q in range(parts):
            for r in range(rows):
                tok_out[b * parts + q, r * chunk : (r + 1) * chunk, :] = tok_ref[b, r, q]
    for s in range(2):
        cols = half_cols(s, width)
        gain = gain_ref[:, cols]
        for b in range(batch):
            for q in range(parts):
                for r in range(rows):
                    piece = cot_ref[b, r, q, :, cols].astype(F32)
                    cot_outs[s][b * parts + q, r * chunk : (r + 1) * chunk, :] = (
                        piece * gain
                    ).astype(BF16)


def pack(tokens, cot, gain):
    batch, rows, parts, chunk, width = tokens.shape
    shape = (batch * parts, rows * chunk)
    return call(
        pack_kernel,
        "pack",
        [jax.ShapeDtypeStruct(shape + (width,), BF16)]
        + [jax.ShapeDtypeStruct(shape + (width // 2,), BF16)] * 2,
        in_hbm(tokens),
        in_hbm(cot),
        in_hbm(gain),
    )


def output_kernel(tok_ref, gain_ref, own_ref, other_ref, out_ref):
    batch, rows, parts, chunk, width = tok_ref.shape
    for s, ref in enumerate((own_ref, other_ref)):
        cols = half_cols(s, width)
        gain = gain_ref[:, cols]
        for t in range(batch * parts):
            b, q = t // parts, t % parts
            for r in range(rows):
                mixed = ref[t, r * chunk : (r + 1) * chunk, :].astype(F32)
                out_ref[b, r, q, :, cols] = (
                    tok_ref[b, r, q, :, cols].astype(F32) + gain * mixed
                ).astype(BF16)


def make_output(tokens, gain, mixed):
    return call(
        output_kernel,
        "make_output",
        jax.ShapeDtypeStruct(tokens.shape, BF16),
        tokens,
        gain,
        *mixed,
    )


def gradient_kernel(cot_ref, back_ref, out_ref):
    batch, rows, parts, chunk, width = cot_ref.shape
    for b in range(batch):
        for q in range(parts):
            for r in range(rows):
                back = back_ref[b * parts + q, r * chunk : (r + 1) * chunk, :width].astype(F32)
                out_ref[b, r, q] = (cot_ref[b, r, q].astype(F32) + back).astype(BF16)


def make_gradient(cot, back):
    return call(
        gradient_kernel, "make_gradient", jax.ShapeDtypeStruct(cot.shape, BF16), cot, back
    )


def by_head(tile, lane):
    zero = jnp.zeros_like(tile)
    return jnp.concatenate([jnp.where(lane == 0, tile, zero), jnp.where(lane == 1, tile, zero)], axis=0)


def own_rows(turned, head_width):
    count = turned.shape[1] // 2
    return [turned[:head_width, :count], turned[head_width:, count:]]


def side_by_side(stacked):
    count = stacked.shape[0] // 2
    return jnp.concatenate([stacked[:count], stacked[count:]], axis=1)


def forward_kernel(
    samples, lat_count, chunk, owners,
    tok_ref, mask_ref, wq_ref, wk_ref, wv_ref, wm_ref, _,
    qn_ref, kn_ref, v_ref, rq_ref, rk_ref, at_ref, ri_ref, p_ref, att_ref, own_ref, other_ref,
    normed_ref, acc_ref, keep_ref,
):
    step = pl.program_id(0)
    count, width = normed_ref.shape
    head_width = width // HEADS

    @pl.when(step == 0)
    def _():
        x = tok_ref[...].astype(F32)
        rx = lax.rsqrt(jnp.mean(x * x, axis=-1, keepdims=True) + epsilon)
        normed_ref[...] = (x * rx).astype(BF16)
        acc_ref[...] = jnp.zeros_like(acc_ref)
        spread = (
            lax.broadcasted_iota(jnp.int32, (lat_count, count), 0)
            == lax.broadcasted_iota(jnp.int32, (lat_count, count), 1) // chunk
        ).astype(F32)
        per_sample = nn(mask_ref[...].astype(F32), spread)
        mine = lax.axis_index("lat") // (owners // samples)
        pick = lax.broadcasted_iota(jnp.int32, (samples, count), 0) == mine
        valid = jnp.sum(jnp.where(pick, per_sample, 0.0), axis=0, keepdims=True)
        same = (
            lax.broadcasted_iota(jnp.int32, (count, count), 0) % chunk
            == lax.broadcasted_iota(jnp.int32, (count, count), 1) % chunk
        )
        keep_ref[...] = jnp.where(same, valid, 0.0)

    normed = normed_ref[...]
    mean_mat = block_mean(head_width)
    q = nn(normed, wq_ref[...])
    k = nn(normed, wk_ref[...])
    v = nn(normed, wv_ref[...]).astype(BF16)
    rq = lax.rsqrt(nn((q * q).astype(BF16), mean_mat) + epsilon)
    rk = lax.rsqrt(nn((k * k).astype(BF16), mean_mat) + epsilon)
    qn = (q * rq).astype(BF16)
    kn = (k * rk).astype(BF16)
    qn_ref[...] = qn
    kn_ref[...] = kn
    v_ref[...] = v
    rq_ref[...] = rq.astype(BF16)
    rk_ref[...] = rk.astype(BF16)
    keep = keep_ref[...]
    keep = jnp.concatenate([keep, keep], axis=0)
    lane = lax.broadcasted_iota(jnp.int32, (count, 128), 1) // head_width
    ones = by_head(jnp.ones((count, 128), BF16), lane)
    tiles = []
    for t in range(GROUP // 128):
        cols = slice(t * 128, (t + 1) * 128)
        v_ones = jnp.concatenate([by_head(v[:, cols], lane), ones], axis=1)
        e = jnp.exp(nt(by_head(qn[:, cols] * score_scale, lane), kn[:, cols])) * keep
        e = e.astype(BF16)
        p_ref[t] = e
        o = nn(side_by_side(e), v_ones)
        inverse = 1.0 / o[:, 128:]
        tiles.append(o[:, :128] * inverse)
        ri_ref[:, cols] = inverse
    att = jnp.concatenate(tiles, axis=1).astype(BF16)
    at_ref[...] = att
    features = att_ref.shape[-1]
    for f in range(GROUP // features):
        att_ref[f] = att[:, f * features : (f + 1) * features]
    acc_ref[...] += nn(att, wm_ref[...])

    @pl.when(step == pl.num_programs(0) - 1)
    def _():
        for s, ref in enumerate((own_ref, other_ref)):
            ref[...] = acc_ref[:, half_cols(s, width)].astype(BF16)


def forward(tok_col, key_mask, w_qkv, w_mix, chunk, owners, after):
    count, width = tok_col.shape
    samples, lat_count = key_mask.shape
    steps = width // GROUP
    features = width // owners
    same = lambda shape: pl.BlockSpec(shape, lambda i: (0, 0))
    cols = pl.BlockSpec((count, GROUP), lambda i: (0, i))
    weight = lambda which: pl.BlockSpec((width, GROUP), lambda i: (0, i + which * steps))
    return pl.pallas_call(
        functools.partial(forward_kernel, samples, lat_count, chunk, owners),
        out_shape=(
            [pltpu.HBM((count, width), BF16)] * 6
            + [pltpu.HBM((count, width), F32)]
            + [pltpu.HBM((width // 128, 2 * count, count), BF16)]
            + [jax.ShapeDtypeStruct((owners, count, features), BF16)]
            + [jax.ShapeDtypeStruct((count, width // 2), BF16)] * 2
        ),
        grid=(steps,),
        in_specs=[
            same((count, width)),
            same((samples, lat_count)),
            weight(0),
            weight(1),
            weight(2),
            pl.BlockSpec((GROUP, width), lambda i: (i, 0)),
            pl.BlockSpec(memory_space=pl.ANY),
        ],
        out_specs=(
            [cols] * 7
            + [pl.BlockSpec((GROUP // 128, 2 * count, count), lambda i: (i, 0, 0))]
            + [pl.BlockSpec((GROUP // features, count, features), lambda i: (i, 0, 0))]
            + [same((count, width // 2))] * 2
        ),
        scratch_shapes=[
            pltpu.VMEM((count, width), BF16),
            pltpu.VMEM((count, width), F32),
            pltpu.VMEM((count, count), F32),
        ],
        compiler_params=params(),
        cost_estimate=pl.CostEstimate(
            flops=2 * count * width * (4 * width + 2 * count * 4),
            bytes_accessed=20 * count * width + 8 * width * width,
            transcendentals=HEADS * count * count,
        ),
        name="forward",
    )(tok_col, key_mask, *[in_hbm(w_qkv)] * 3, in_hbm(w_mix), after)


def backward_kernel(
    tok_ref, own_ref, other_ref, wm_ref, wq_ref, wk_ref, wv_ref,
    qn_ref, kn_ref, v_ref, rq_ref, rk_ref, at_ref, ri_ref, p_ref, *rest,
):
    out_ref, acc_ref = rest[-2:]
    step = pl.program_id(0)
    count, width = acc_ref.shape
    head_width = width // HEADS
    d_att = nt(own_ref[...], wm_ref[:, half_cols(0, width)])
    d_att += nt(other_ref[...], wm_ref[:, half_cols(1, width)])
    inverse = ri_ref[...]
    d_att = (d_att * inverse).astype(BF16)
    mean_mat = block_mean(head_width)
    product = d_att.astype(F32) * at_ref[...].astype(F32)
    coarse = product.astype(BF16)
    rest_of = (product - coarse.astype(F32)).astype(BF16)
    inner_all = (nn(coarse, mean_mat) + nn(rest_of, mean_mat)) * float(head_width)
    qn, kn, v = qn_ref[...], kn_ref[...], v_ref[...]
    lane = lax.broadcasted_iota(jnp.int32, (count, 128), 1) // head_width
    dq_tiles, dk_tiles, dv_tiles = [], [], []
    for t in range(GROUP // 128):
        cols = slice(t * 128, (t + 1) * 128)
        d_t = d_att[:, cols]
        d_p = nt(by_head(d_t, lane), v[:, cols])
        e = p_ref[t]
        e_wide = e.astype(F32)
        first = t * 128
        second = first + head_width
        inner = jnp.concatenate(
            [inner_all[:, first : first + 1], inner_all[:, second : second + 1]], axis=0
        )
        d_s = (e_wide * (d_p - inner)).astype(BF16)
        d_s = side_by_side(d_s)
        dq_tiles.append(nn(d_s, by_head(kn[:, cols], lane)))
        dk_tiles += own_rows(tn(qn[:, cols], d_s), head_width)
        dv_tiles += own_rows(tn(d_t, side_by_side(e)), head_width)
    dq = jnp.concatenate(dq_tiles, axis=1) * score_scale
    dk = jnp.concatenate(dk_tiles, axis=0).T * score_scale
    dv = jnp.concatenate(dv_tiles, axis=0).T.astype(BF16)

    def through_norm(upstream, unit, factor):
        unit = unit.astype(F32)
        inner = nn((upstream * unit).astype(BF16), mean_mat)
        return (factor.astype(F32) * (upstream - unit * inner)).astype(BF16)

    gq = through_norm(dq, qn, rq_ref[...])
    gk = through_norm(dk, kn, rk_ref[...])
    total = nt(gq, wq_ref[...]) + nt(gk, wk_ref[...]) + nt(dv, wv_ref[...])

    @pl.when(step == 0)
    def _():
        acc_ref[...] = total

    @pl.when(step > 0)
    def _():
        acc_ref[...] += total

    @pl.when(step == pl.num_programs(0) - 1)
    def _():
        x = tok_ref[...].astype(F32)
        rx = lax.rsqrt(jnp.mean(x * x, axis=-1, keepdims=True) + epsilon)
        d = acc_ref[...]
        inner = jnp.mean(d * x, axis=-1, keepdims=True)
        out_ref[...] = (rx * d - x * (rx * rx * rx * inner)).astype(BF16)


def backward(tok_col, flow, w_mix, w_qkv, saved, *after):
    count, width = tok_col.shape
    steps = width // GROUP
    same = lambda shape: pl.BlockSpec(shape, lambda i: (0, 0))
    cols = pl.BlockSpec((count, GROUP), lambda i: (0, i))
    weight = lambda which: pl.BlockSpec((width, GROUP), lambda i: (0, i + which * steps))
    return pl.pallas_call(
        backward_kernel,
        out_shape=jax.ShapeDtypeStruct((count, width), BF16),
        grid=(steps,),
        in_specs=[
            same((count, width)),
            same((count, width // 2)),
            same((count, width // 2)),
            pl.BlockSpec((GROUP, width), lambda i: (i, 0)),
            weight(0),
            weight(1),
            weight(2),
            *([cols] * 7),
            pl.BlockSpec((GROUP // 128, 2 * count, count), lambda i: (i, 0, 0)),
        ]
        + [pl.BlockSpec(memory_space=pl.ANY)] * len(after),
        out_specs=same((count, width)),
        scratch_shapes=[pltpu.VMEM((count, width), F32)],
        compiler_params=params(),
        cost_estimate=pl.CostEstimate(
            flops=2 * count * width * (4 * width + 4 * count * 4),
            bytes_accessed=20 * count * width + 8 * width * width,
            transcendentals=0,
        ),
        name="backward",
    )(tok_col, *flow, in_hbm(w_mix), *[in_hbm(w_qkv)] * 3, *map(in_hbm, saved), *after)


def mix_gradient_kernel(factor, own_flow_ref, other_flow_ref, *refs):
    att_refs, out_refs = refs[: len(refs) // 2], refs[len(refs) // 2 :]
    width = out_refs[0].shape[-1]
    for att_ref, out_ref in zip(att_refs, out_refs):
        att = att_ref[...]
        for s, flow_ref in enumerate((own_flow_ref, other_flow_ref)):
            term = tn(att, flow_ref[...]) * factor
            out_ref[:, half_cols(s, width)] = term.astype(out_ref.dtype)


def mix_gradient(attended, flow, factor):
    rows, features = attended[0].shape
    width = 2 * flow[0].shape[-1]
    out = [jax.ShapeDtypeStruct((features, width), F32)]
    out += [jax.ShapeDtypeStruct((features, width), BF16)] * (len(attended) - 1)
    return pl.pallas_call(
        functools.partial(mix_gradient_kernel, factor),
        out_shape=out,
        compiler_params=params(),
        cost_estimate=pl.CostEstimate(
            flops=2 * rows * features * width * len(attended),
            bytes_accessed=2 * rows * (features * len(attended) + width),
            transcendentals=0,
        ),
        name="mix_gradient",
    )(*flow, *attended)


def chip_rows(array, axis, chip):
    rows = array.shape[axis] // (lax.axis_size("lev") // 2)
    return lax.dynamic_slice_in_dim(array, (chip * rows).astype(jnp.uint32), rows, axis)


def swap(block):
    return lax.all_to_all(block, "lat", split_axis=0, concat_axis=0, tiled=True)


def from_level(block, offset):
    return lax.ppermute(block, "lev", [(i, i ^ offset) for i in range(lax.axis_size("lev"))])


def add_kernel(own_ref, received_ref, out_ref):
    out_ref[...] = (own_ref[...].astype(F32) + received_ref[...].astype(F32)).astype(BF16)


def add(own, received):
    return call(add_kernel, "add", jax.ShapeDtypeStruct(own.shape, BF16), own, received)


def pair_total(own, other):
    return add(own, from_level(other, 1))


def before_last(total):
    offset = 2
    while 2 * offset < lax.axis_size("lev"):
        total = add(total, from_level(total, offset))
        offset *= 2
    return total, from_level(total, offset)


def row_half(which, rows):
    top = lax.axis_index("lev") // (lax.axis_size("lev") // 2)
    return pl.ds(pl.multiple_of((top ^ which) * rows, rows), rows)


def split_kernel(own_ref, received_ref, first_ref, second_ref):
    rows = first_ref.shape[1]
    for which, ref in enumerate((first_ref, second_ref)):
        at = row_half(which, rows)
        total = own_ref[:, at, :].astype(F32) + received_ref[:, at, :].astype(F32)
        ref[...] = total.astype(BF16)


def split_rows(own, received):
    owners, cells, half = own.shape
    rows = cells // 2
    if rows % 16 == 0:
        part = jax.ShapeDtypeStruct((owners, rows, half), BF16)
        return call(split_kernel, "split_rows", [part, part], own, received)
    total = (own.astype(F32) + received.astype(F32)).astype(BF16)
    top = lax.axis_index("lev") // (lax.axis_size("lev") // 2)
    return [lax.dynamic_slice_in_dim(total, (top ^ k) * rows, rows, 1) for k in range(2)]


def add_flow_kernel(first_ref, second_ref, received_ref, _, __, out_ref):
    rows = first_ref.shape[1]
    out_ref[:, row_half(0, rows), :] = first_ref[...]
    second = second_ref[...].astype(F32) + received_ref[...].astype(F32)
    out_ref[:, row_half(1, rows), :] = second.astype(BF16)


def add_flow(first, second, received, *after):
    owners, rows, half = first.shape
    if rows % 16:
        second = (second.astype(F32) + received.astype(F32)).astype(BF16)
        top = lax.axis_index("lev") // (lax.axis_size("lev") // 2)
        pair = jnp.where(top == 0, jnp.stack([first, second]), jnp.stack([second, first]))
        return jnp.concatenate([pair[0], pair[1]], axis=1)
    whole = pl.BlockSpec(memory_space=pltpu.VMEM)
    return pl.pallas_call(
        add_flow_kernel,
        out_shape=jax.ShapeDtypeStruct((owners, 2 * rows, half), BF16),
        in_specs=[whole] * 3 + [pl.BlockSpec(memory_space=pl.ANY)] * 2,
        out_specs=whole,
        compiler_params=params(),
        name="add_flow",
    )(first, second, received, *after)


def join_kernel(first_ref, second_ref, out_ref):
    count = first_ref.shape[0]
    out_ref[:count] = first_ref[...]
    out_ref[count:] = second_ref[...]


def join(first, second):
    shape = jax.ShapeDtypeStruct((2 * first.shape[0],) + first.shape[1:], BF16)
    return call(join_kernel, "join", shape, first, second)


def from_owner(block, offset):
    return lax.ppermute(block, "lat", [(i, i ^ offset) for i in range(lax.axis_size("lat"))])


def gather_offsets(owners):
    offsets = [owners // 4, owners // 2]
    while len(offsets) < owners.bit_length() - 1:
        offsets.append(owners >> (len(offsets) + 1))
    return offsets


def arrange_kernel(first_ref, second_ref, _, out_ref):
    owners = out_ref.shape[1]
    half = owners // 2
    offsets = gather_offsets(owners)
    for u in range(owners):
        band = lax.axis_index("lat") ^ sum(o for k, o in enumerate(offsets) if u >> k & 1)
        ref = first_ref if u < half else second_ref
        out_ref[:, band] = ref[u % half]


def arrange(first, second, after):
    _, owners, rows, half = first.shape
    whole = pl.BlockSpec(memory_space=pltpu.VMEM)
    return pl.pallas_call(
        arrange_kernel,
        out_shape=jax.ShapeDtypeStruct((owners, owners, rows, half), BF16),
        in_specs=[whole, whole, pl.BlockSpec(memory_space=pl.ANY)],
        out_specs=whole,
        compiler_params=params(),
        name="arrange",
    )(first, second, after)


def add_mixed_kernel(own_ref, received_ref, back_ref, out_ref):
    width = back_ref.shape[-1]
    out_ref[:, :width] = back_ref[...]
    out_ref[:, width:] = (own_ref[...].astype(F32) + received_ref[...].astype(F32)).astype(BF16)


def add_mixed(own, received, back):
    count, width = back.shape
    shape = jax.ShapeDtypeStruct((count, width + own.shape[-1]), BF16)
    return call(add_mixed_kernel, "add_mixed", shape, own, received, back)


def cut_kernel(in_ref, _, out_ref):
    out_ref[...] = in_ref[:, :, in_ref.shape[-1] - out_ref.shape[-1] :]


def cut_mixed(received, after):
    owners, cells, wide = received.shape
    whole = pl.BlockSpec(memory_space=pltpu.VMEM)
    return pl.pallas_call(
        cut_kernel,
        out_shape=jax.ShapeDtypeStruct((owners, cells, wide // 3), BF16),
        in_specs=[whole, pl.BlockSpec(memory_space=pl.ANY)],
        out_specs=whole,
        compiler_params=params(),
        name="cut_mixed",
    )(received, after)


def on_device(tokens, key_mask, w_qkv, w_mix, level_scale, cotangent):
    batch, _, rows, lon, width = tokens.shape
    owners = lax.axis_size("lat")
    parts = owners // batch
    chunk = lon // parts
    cells = rows * chunk
    count = batch * rows * lon
    half = width // 2
    tok_band = tokens.reshape(batch, rows, parts, chunk, width)
    cot_band = cotangent.reshape(batch, rows, parts, chunk, width)
    w_mix = w_mix.reshape(width, width)

    tok_send, cot_own, cot_other = pack(tok_band, cot_band, level_scale)
    tok_col = swap(tok_send).reshape(count, width)
    last = lax.axis_size("lev") // 2
    received = from_level(cot_other, 1)
    offset = 2
    while offset < last:
        cot_own = add(cot_own, received)
        received = from_level(cot_own, offset)
        offset *= 2
    first, second = split_rows(cot_own, received)
    first, received = add(first, from_level(second, last)), from_level(first, last)
    rows = cells // last
    offsets = gather_offsets(owners)
    flow_rows = first
    if last > 2:
        part = lax.axis_index("lev") // 2 % (last // 2)
        flow_rows = lax.dynamic_slice_in_dim(first, part * rows, rows, 1)
    flow_rows = flow_rows[None]
    flow_rows = join(flow_rows, from_owner(flow_rows, offsets[0]))
    flow_band = add_flow(first, second, received, tok_col, flow_rows)
    flow_own = swap(flow_band).reshape(count, half)
    flow = (flow_own, from_level(flow_own, 1))
    chip = lax.shift_right_logical(lax.axis_index("lev"), 1)
    chips = lax.axis_size("lev") // 2

    *saved, attended, mix_own, mix_other = forward(
        tok_col, key_mask, w_qkv, w_mix, chunk, owners, flow_band
    )
    attended = swap(attended)
    mix_terms = before_last(pair_total(mix_own, mix_other))
    for offset in offsets[1:-1]:
        flow_rows = join(flow_rows, from_owner(flow_rows, offset))
    received = from_owner(flow_rows, offsets[-1])
    back_col = backward(tok_col, flow, w_mix, w_qkv, saved, mix_terms[0], flow_rows)
    sent = add_mixed(*mix_terms, back_col)
    back = swap(sent.reshape(owners, cells, width + half))
    d_tokens = make_gradient(cot_band, back)

    factor = 1.0 / math.sqrt(count * owners)
    features = width // owners
    attended = attended.reshape(owners, owners, cells, features)
    attended = [chip_rows(attended, 2, chip ^ k).reshape(-1, features) for k in range(chips)]
    attended[1:] = [from_level(attended[k], 2 * k) for k in range(1, chips)]
    flow_rows = arrange(flow_rows, received, sent).reshape(-1, half)
    grads = mix_gradient(attended, (flow_rows, from_level(flow_rows, 1)), factor)
    mix_grad = grads[0]
    for k in range(1, chips):
        mix_grad += from_level(grads[k], 2 * k).astype(F32)

    mix_band = cut_mixed(back, mix_grad)
    output = make_output(tok_band, level_scale, (mix_band, from_level(mix_band, 1)))
    return (
        output.reshape(tokens.shape),
        d_tokens.reshape(tokens.shape),
        mix_grad.reshape(1, width // owners, width),
    )


def solution(mesh):
    return jax.shard_map(
        on_device,
        mesh=mesh,
        in_specs=(
            P(None, "lev", "lat", None, None),
            P(),
            P(),
            P("lev", None, None),
            P("lev", None),
            P(None, "lev", "lat", None, None),
        ),
        out_specs=(
            P(None, "lev", "lat", None, None),
            P(None, "lev", "lat", None, None),
            P("lev", "lat", None),
        ),
        check_vma=False,
    )
```

```python
import functools
import math

import jax
import jax.numpy as jnp
from jax import lax
from jax.experimental import pallas as pl
from jax.experimental.pallas import tpu as pltpu
from jax.sharding import PartitionSpec as P

HEADS = 16
GROUP = 256

epsilon = 1e-06
score_scale = 0.25

F32 = jnp.float32
BF16 = jnp.bfloat16


def nn(a, b):
    return lax.dot_general(a, b, (((1,), (0,)), ((), ())), preferred_element_type=F32)


def nt(a, b):
    return lax.dot_general(a, b, (((1,), (1,)), ((), ())), preferred_element_type=F32)


def tn(a, b):
    return lax.dot_general(a, b, (((0,), (0,)), ((), ())), preferred_element_type=F32)


def block_mean(head_width):
    row = lax.broadcasted_iota(jnp.int32, (GROUP, GROUP), 0) // head_width
    col = lax.broadcasted_iota(jnp.int32, (GROUP, GROUP), 1) // head_width
    return jnp.where(row == col, 1.0 / head_width, 0.0).astype(BF16)


def params():
    return pltpu.CompilerParams(vmem_limit_bytes=36 * 1024 * 1024)


def half_cols(which, width):
    half = width // 2
    core = lax.axis_index("lev") % 2
    return pl.ds(pl.multiple_of((core ^ which) * half, half), half)


def in_hbm(array):
    return pltpu.with_memory_space_constraint(array, pltpu.HBM)


def call(kernel, name, out_shape, *operands):
    return pl.pallas_call(
        kernel, out_shape=out_shape, compiler_params=params(), name=name
    )(*operands)


def pack_kernel(tok_ref, cot_ref, gain_ref, tok_out, *cot_outs):
    batch, rows, parts, chunk, width = tok_ref.shape
    for b in range(batch):
        for q in range(parts):
            for r in range(rows):
                tok_out[b * parts + q, r * chunk : (r + 1) * chunk, :] = tok_ref[b, r, q]
    for s in range(2):
        cols = half_cols(s, width)
        gain = gain_ref[:, cols]
        for b in range(batch):
            for q in range(parts):
                for r in range(rows):
                    piece = cot_ref[b, r, q, :, cols].astype(F32)
                    cot_outs[s][b * parts + q, r * chunk : (r + 1) * chunk, :] = (
                        piece * gain
                    ).astype(BF16)


def pack(tokens, cot, gain):
    batch, rows, parts, chunk, width = tokens.shape
    shape = (batch * parts, rows * chunk)
    return call(
        pack_kernel,
        "pack",
        [jax.ShapeDtypeStruct(shape + (width,), BF16)]
        + [jax.ShapeDtypeStruct(shape + (width // 2,), BF16)] * 2,
        in_hbm(tokens),
        in_hbm(cot),
        in_hbm(gain),
    )


def output_kernel(tok_ref, gain_ref, own_ref, other_ref, out_ref):
    batch, rows, parts, chunk, width = tok_ref.shape
    for s, ref in enumerate((own_ref, other_ref)):
        cols = half_cols(s, width)
        gain = gain_ref[:, cols]
        for t in range(batch * parts):
            b, q = t // parts, t % parts
            for r in range(rows):
                mixed = ref[t, r * chunk : (r + 1) * chunk, :].astype(F32)
                out_ref[b, r, q, :, cols] = (
                    tok_ref[b, r, q, :, cols].astype(F32) + gain * mixed
                ).astype(BF16)


def make_output(tokens, gain, mixed):
    return call(
        output_kernel,
        "make_output",
        jax.ShapeDtypeStruct(tokens.shape, BF16),
        tokens,
        gain,
        *mixed,
    )


def gradient_kernel(cot_ref, back_ref, out_ref):
    batch, rows, parts, chunk, width = cot_ref.shape
    for b in range(batch):
        for q in range(parts):
            for r in range(rows):
                back = back_ref[b * parts + q, r * chunk : (r + 1) * chunk, :width].astype(F32)
                out_ref[b, r, q] = (cot_ref[b, r, q].astype(F32) + back).astype(BF16)


def make_gradient(cot, back):
    return call(
        gradient_kernel, "make_gradient", jax.ShapeDtypeStruct(cot.shape, BF16), cot, back
    )


def by_head(tile, lane):
    zero = jnp.zeros_like(tile)
    return jnp.concatenate([jnp.where(lane == 0, tile, zero), jnp.where(lane == 1, tile, zero)], axis=0)


def own_rows(turned, head_width):
    count = turned.shape[1] // 2
    return [turned[:head_width, :count], turned[head_width:, count:]]


def side_by_side(stacked):
    count = stacked.shape[0] // 2
    return jnp.concatenate([stacked[:count], stacked[count:]], axis=1)


def forward_kernel(
    samples, lat_count, chunk, owners,
    tok_ref, mask_ref, wq_ref, wk_ref, wv_ref, wm_ref, _,
    qn_ref, kn_ref, v_ref, rq_ref, rk_ref, at_ref, ri_ref, p_ref, att_ref, own_ref, other_ref,
    normed_ref, acc_ref, keep_ref,
):
    step = pl.program_id(0)
    count, width = normed_ref.shape
    head_width = width // HEADS

    @pl.when(step == 0)
    def _():
        x = tok_ref[...].astype(F32)
        rx = lax.rsqrt(jnp.mean(x * x, axis=-1, keepdims=True) + epsilon)
        normed_ref[...] = (x * rx).astype(BF16)
        acc_ref[...] = jnp.zeros_like(acc_ref)
        spread = (
            lax.broadcasted_iota(jnp.int32, (lat_count, count), 0)
            == lax.broadcasted_iota(jnp.int32, (lat_count, count), 1) // chunk
        ).astype(F32)
        per_sample = nn(mask_ref[...].astype(F32), spread)
        mine = lax.axis_index("lat") // (owners // samples)
        pick = lax.broadcasted_iota(jnp.int32, (samples, count), 0) == mine
        valid = jnp.sum(jnp.where(pick, per_sample, 0.0), axis=0, keepdims=True)
        same = (
            lax.broadcasted_iota(jnp.int32, (count, count), 0) % chunk
            == lax.broadcasted_iota(jnp.int32, (count, count), 1) % chunk
        )
        keep_ref[...] = jnp.where(same, valid, 0.0)

    normed = normed_ref[...]
    mean_mat = block_mean(head_width)
    q = nn(normed, wq_ref[...])
    k = nn(normed, wk_ref[...])
    v = nn(normed, wv_ref[...]).astype(BF16)
    rq = lax.rsqrt(nn((q * q).astype(BF16), mean_mat) + epsilon)
    rk = lax.rsqrt(nn((k * k).astype(BF16), mean_mat) + epsilon)
    qn = (q * rq).astype(BF16)
    kn = (k * rk).astype(BF16)
    qn_ref[...] = qn
    kn_ref[...] = kn
    v_ref[...] = v
    rq_ref[...] = rq.astype(BF16)
    rk_ref[...] = rk.astype(BF16)
    keep = keep_ref[...]
    keep = jnp.concatenate([keep, keep], axis=0)
    lane = lax.broadcasted_iota(jnp.int32, (count, 128), 1) // head_width
    ones = by_head(jnp.ones((count, 128), BF16), lane)
    tiles = []
    for t in range(GROUP // 128):
        cols = slice(t * 128, (t + 1) * 128)
        v_ones = jnp.concatenate([by_head(v[:, cols], lane), ones], axis=1)
        e = jnp.exp(nt(by_head(qn[:, cols] * score_scale, lane), kn[:, cols])) * keep
        e = e.astype(BF16)
        p_ref[t] = e
        o = nn(side_by_side(e), v_ones)
        inverse = 1.0 / o[:, 128:]
        tiles.append(o[:, :128] * inverse)
        ri_ref[:, cols] = inverse
    att = jnp.concatenate(tiles, axis=1).astype(BF16)
    at_ref[...] = att
    features = att_ref.shape[-1]
    for f in range(GROUP // features):
        att_ref[f] = att[:, f * features : (f + 1) * features]
    acc_ref[...] += nn(att, wm_ref[...])

    @pl.when(step == pl.num_programs(0) - 1)
    def _():
        for s, ref in enumerate((own_ref, other_ref)):
            ref[...] = acc_ref[:, half_cols(s, width)].astype(BF16)


def forward(tok_col, key_mask, w_qkv, w_mix, chunk, owners, after):
    count, width = tok_col.shape
    samples, lat_count = key_mask.shape
    steps = width // GROUP
    features = width // owners
    same = lambda shape: pl.BlockSpec(shape, lambda i: (0, 0))
    cols = pl.BlockSpec((count, GROUP), lambda i: (0, i))
    weight = lambda which: pl.BlockSpec((width, GROUP), lambda i: (0, i + which * steps))
    return pl.pallas_call(
        functools.partial(forward_kernel, samples, lat_count, chunk, owners),
        out_shape=(
            [pltpu.HBM((count, width), BF16)] * 6
            + [pltpu.HBM((count, width), F32)]
            + [pltpu.HBM((width // 128, 2 * count, count), BF16)]
            + [jax.ShapeDtypeStruct((owners, count, features), BF16)]
            + [jax.ShapeDtypeStruct((count, width // 2), BF16)] * 2
        ),
        grid=(steps,),
        in_specs=[
            same((count, width)),
            same((samples, lat_count)),
            weight(0),
            weight(1),
            weight(2),
            pl.BlockSpec((GROUP, width), lambda i: (i, 0)),
            pl.BlockSpec(memory_space=pl.ANY),
        ],
        out_specs=(
            [cols] * 7
            + [pl.BlockSpec((GROUP // 128, 2 * count, count), lambda i: (i, 0, 0))]
            + [pl.BlockSpec((GROUP // features, count, features), lambda i: (i, 0, 0))]
            + [same((count, width // 2))] * 2
        ),
        scratch_shapes=[
            pltpu.VMEM((count, width), BF16),
            pltpu.VMEM((count, width), F32),
            pltpu.VMEM((count, count), F32),
        ],
        compiler_params=params(),
        cost_estimate=pl.CostEstimate(
            flops=2 * count * width * (4 * width + 2 * count * 4),
            bytes_accessed=20 * count * width + 8 * width * width,
            transcendentals=HEADS * count * count,
        ),
        name="forward",
    )(tok_col, key_mask, *[in_hbm(w_qkv)] * 3, in_hbm(w_mix), after)


def backward_kernel(
    tok_ref, own_ref, other_ref, wm_ref, wq_ref, wk_ref, wv_ref,
    qn_ref, kn_ref, v_ref, rq_ref, rk_ref, at_ref, ri_ref, p_ref, *rest,
):
    out_ref, acc_ref = rest[-2:]
    step = pl.program_id(0)
    count, width = acc_ref.shape
    head_width = width // HEADS
    d_att = nt(own_ref[...], wm_ref[:, half_cols(0, width)])
    d_att += nt(other_ref[...], wm_ref[:, half_cols(1, width)])
    inverse = ri_ref[...]
    d_att = (d_att * inverse).astype(BF16)
    mean_mat = block_mean(head_width)
    product = d_att.astype(F32) * at_ref[...].astype(F32)
    coarse = product.astype(BF16)
    rest_of = (product - coarse.astype(F32)).astype(BF16)
    inner_all = (nn(coarse, mean_mat) + nn(rest_of, mean_mat)) * float(head_width)
    qn, kn, v = qn_ref[...], kn_ref[...], v_ref[...]
    lane = lax.broadcasted_iota(jnp.int32, (count, 128), 1) // head_width
    dq_tiles, dk_tiles, dv_tiles = [], [], []
    for t in range(GROUP // 128):
        cols = slice(t * 128, (t + 1) * 128)
        d_t = d_att[:, cols]
        d_p = nt(by_head(d_t, lane), v[:, cols])
        e = p_ref[t]
        e_wide = e.astype(F32)
        first = t * 128
        second = first + head_width
        inner = jnp.concatenate(
            [inner_all[:, first : first + 1], inner_all[:, second : second + 1]], axis=0
        )
        d_s = (e_wide * (d_p - inner)).astype(BF16)
        d_s = side_by_side(d_s)
        dq_tiles.append(nn(d_s, by_head(kn[:, cols], lane)))
        dk_tiles += own_rows(tn(qn[:, cols], d_s), head_width)
        dv_tiles += own_rows(tn(d_t, side_by_side(e)), head_width)
    dq = jnp.concatenate(dq_tiles, axis=1) * score_scale
    dk = jnp.concatenate(dk_tiles, axis=0).T * score_scale
    dv = jnp.concatenate(dv_tiles, axis=0).T.astype(BF16)

    def through_norm(upstream, unit, factor):
        unit = unit.astype(F32)
        inner = nn((upstream * unit).astype(BF16), mean_mat)
        return (factor.astype(F32) * (upstream - unit * inner)).astype(BF16)

    gq = through_norm(dq, qn, rq_ref[...])
    gk = through_norm(dk, kn, rk_ref[...])
    total = nt(gq, wq_ref[...]) + nt(gk, wk_ref[...]) + nt(dv, wv_ref[...])

    @pl.when(step == 0)
    def _():
        acc_ref[...] = total

    @pl.when(step > 0)
    def _():
        acc_ref[...] += total

    @pl.when(step == pl.num_programs(0) - 1)
    def _():
        x = tok_ref[...].astype(F32)
        rx = lax.rsqrt(jnp.mean(x * x, axis=-1, keepdims=True) + epsilon)
        d = acc_ref[...]
        inner = jnp.mean(d * x, axis=-1, keepdims=True)
        out_ref[...] = (rx * d - x * (rx * rx * rx * inner)).astype(BF16)


def backward(tok_col, flow, w_mix, w_qkv, saved, *after):
    count, width = tok_col.shape
    steps = width // GROUP
    same = lambda shape: pl.BlockSpec(shape, lambda i: (0, 0))
    cols = pl.BlockSpec((count, GROUP), lambda i: (0, i))
    weight = lambda which: pl.BlockSpec((width, GROUP), lambda i: (0, i + which * steps))
    return pl.pallas_call(
        backward_kernel,
        out_shape=jax.ShapeDtypeStruct((count, width), BF16),
        grid=(steps,),
        in_specs=[
            same((count, width)),
            same((count, width // 2)),
            same((count, width // 2)),
            pl.BlockSpec((GROUP, width), lambda i: (i, 0)),
            weight(0),
            weight(1),
            weight(2),
            *([cols] * 7),
            pl.BlockSpec((GROUP // 128, 2 * count, count), lambda i: (i, 0, 0)),
        ]
        + [pl.BlockSpec(memory_space=pl.ANY)] * len(after),
        out_specs=same((count, width)),
        scratch_shapes=[pltpu.VMEM((count, width), F32)],
        compiler_params=params(),
        cost_estimate=pl.CostEstimate(
            flops=2 * count * width * width,
            bytes_accessed=2 * count * width,
            transcendentals=0,
        ),
        name="backward",
    )(tok_col, *flow, in_hbm(w_mix), *[in_hbm(w_qkv)] * 3, *map(in_hbm, saved), *after)


def mix_gradient_kernel(factor, own_flow_ref, other_flow_ref, *refs):
    att_refs, out_refs = refs[: len(refs) // 2], refs[len(refs) // 2 :]
    width = out_refs[0].shape[-1]
    for att_ref, out_ref in zip(att_refs, out_refs):
        att = att_ref[...]
        for s, flow_ref in enumerate((own_flow_ref, other_flow_ref)):
            term = tn(att, flow_ref[...]) * factor
            out_ref[:, half_cols(s, width)] = term.astype(out_ref.dtype)


def mix_gradient(attended, flow, factor):
    rows, features = attended[0].shape
    width = 2 * flow[0].shape[-1]
    out = [jax.ShapeDtypeStruct((features, width), F32)]
    out += [jax.ShapeDtypeStruct((features, width), BF16)] * (len(attended) - 1)
    return pl.pallas_call(
        functools.partial(mix_gradient_kernel, factor),
        out_shape=out,
        compiler_params=params(),
        cost_estimate=pl.CostEstimate(
            flops=2 * rows * features * width * len(attended),
            bytes_accessed=2 * rows * (features * len(attended) + width),
            transcendentals=0,
        ),
        name="mix_gradient",
    )(*flow, *attended)


def chip_rows(array, axis, chip):
    rows = array.shape[axis] // (lax.axis_size("lev") // 2)
    return lax.dynamic_slice_in_dim(array, (chip * rows).astype(jnp.uint32), rows, axis)


def swap(block):
    return lax.all_to_all(block, "lat", split_axis=0, concat_axis=0, tiled=True)


def from_level(block, offset):
    return lax.ppermute(block, "lev", [(i, i ^ offset) for i in range(lax.axis_size("lev"))])


def add_kernel(own_ref, received_ref, out_ref):
    out_ref[...] = (own_ref[...].astype(F32) + received_ref[...].astype(F32)).astype(BF16)


def add(own, received):
    return call(add_kernel, "add", jax.ShapeDtypeStruct(own.shape, BF16), own, received)


def pair_total(own, other):
    return add(own, from_level(other, 1))


def before_last(total):
    offset = 2
    while 2 * offset < lax.axis_size("lev"):
        total = add(total, from_level(total, offset))
        offset *= 2
    return total, from_level(total, offset)


def row_half(which, rows):
    top = lax.axis_index("lev") // (lax.axis_size("lev") // 2)
    return pl.ds(pl.multiple_of((top ^ which) * rows, rows), rows)


def split_kernel(own_ref, received_ref, first_ref, second_ref):
    rows = first_ref.shape[1]
    for which, ref in enumerate((first_ref, second_ref)):
        at = row_half(which, rows)
        total = own_ref[:, at, :].astype(F32) + received_ref[:, at, :].astype(F32)
        ref[...] = total.astype(BF16)


def split_rows(own, received):
    owners, cells, half = own.shape
    rows = cells // 2
    if rows % 16 == 0:
        part = jax.ShapeDtypeStruct((owners, rows, half), BF16)
        return call(split_kernel, "split_rows", [part, part], own, received)
    total = (own.astype(F32) + received.astype(F32)).astype(BF16)
    top = lax.axis_index("lev") // (lax.axis_size("lev") // 2)
    return [lax.dynamic_slice_in_dim(total, (top ^ k) * rows, rows, 1) for k in range(2)]


def add_flow_kernel(first_ref, second_ref, received_ref, _, __, out_ref):
    rows = first_ref.shape[1]
    out_ref[:, row_half(0, rows), :] = first_ref[...]
    second = second_ref[...].astype(F32) + received_ref[...].astype(F32)
    out_ref[:, row_half(1, rows), :] = second.astype(BF16)


def add_flow(first, second, received, *after):
    owners, rows, half = first.shape
    if rows % 16:
        second = (second.astype(F32) + received.astype(F32)).astype(BF16)
        top = lax.axis_index("lev") // (lax.axis_size("lev") // 2)
        pair = jnp.where(top == 0, jnp.stack([first, second]), jnp.stack([second, first]))
        return jnp.concatenate([pair[0], pair[1]], axis=1)
    whole = pl.BlockSpec(memory_space=pltpu.VMEM)
    return pl.pallas_call(
        add_flow_kernel,
        out_shape=jax.ShapeDtypeStruct((owners, 2 * rows, half), BF16),
        in_specs=[whole] * 3 + [pl.BlockSpec(memory_space=pl.ANY)] * 2,
        out_specs=whole,
        compiler_params=params(),
        name="add_flow",
    )(first, second, received, *after)


def join_kernel(first_ref, second_ref, out_ref):
    count = first_ref.shape[0]
    out_ref[:count] = first_ref[...]
    out_ref[count:] = second_ref[...]


def join(first, second):
    shape = jax.ShapeDtypeStruct((2 * first.shape[0],) + first.shape[1:], BF16)
    return call(join_kernel, "join", shape, first, second)


def from_owner(block, offset):
    return lax.ppermute(block, "lat", [(i, i ^ offset) for i in range(lax.axis_size("lat"))])


def gather_offsets(owners):
    offsets = [owners // 4, owners // 2]
    while len(offsets) < owners.bit_length() - 1:
        offsets.append(owners >> (len(offsets) + 1))
    return offsets


def arrange_kernel(first_ref, second_ref, _, out_ref):
    owners = out_ref.shape[1]
    half = owners // 2
    offsets = gather_offsets(owners)
    for u in range(owners):
        band = lax.axis_index("lat") ^ sum(o for k, o in enumerate(offsets) if u >> k & 1)
        ref = first_ref if u < half else second_ref
        out_ref[:, band] = ref[u % half]


def arrange(first, second, after):
    _, owners, rows, half = first.shape
    whole = pl.BlockSpec(memory_space=pltpu.VMEM)
    return pl.pallas_call(
        arrange_kernel,
        out_shape=jax.ShapeDtypeStruct((owners, owners, rows, half), BF16),
        in_specs=[whole, whole, pl.BlockSpec(memory_space=pl.ANY)],
        out_specs=whole,
        compiler_params=params(),
        name="arrange",
    )(first, second, after)


def add_mixed_kernel(own_ref, received_ref, back_ref, out_ref):
    width = back_ref.shape[-1]
    out_ref[:, :width] = back_ref[...]
    out_ref[:, width:] = (own_ref[...].astype(F32) + received_ref[...].astype(F32)).astype(BF16)


def add_mixed(own, received, back):
    count, width = back.shape
    shape = jax.ShapeDtypeStruct((count, width + own.shape[-1]), BF16)
    return call(add_mixed_kernel, "add_mixed", shape, own, received, back)


def cut_kernel(in_ref, _, out_ref):
    out_ref[...] = in_ref[:, :, in_ref.shape[-1] - out_ref.shape[-1] :]


def cut_mixed(received, after):
    owners, cells, wide = received.shape
    whole = pl.BlockSpec(memory_space=pltpu.VMEM)
    return pl.pallas_call(
        cut_kernel,
        out_shape=jax.ShapeDtypeStruct((owners, cells, wide // 3), BF16),
        in_specs=[whole, pl.BlockSpec(memory_space=pl.ANY)],
        out_specs=whole,
        compiler_params=params(),
        name="cut_mixed",
    )(received, after)


def on_device(tokens, key_mask, w_qkv, w_mix, level_scale, cotangent):
    batch, _, rows, lon, width = tokens.shape
    owners = lax.axis_size("lat")
    parts = owners // batch
    chunk = lon // parts
    cells = rows * chunk
    count = batch * rows * lon
    half = width // 2
    tok_band = tokens.reshape(batch, rows, parts, chunk, width)
    cot_band = cotangent.reshape(batch, rows, parts, chunk, width)
    w_mix = w_mix.reshape(width, width)

    tok_send, cot_own, cot_other = pack(tok_band, cot_band, level_scale)
    tok_col = swap(tok_send).reshape(count, width)
    last = lax.axis_size("lev") // 2
    received = from_level(cot_other, 1)
    offset = 2
    while offset < last:
        cot_own = add(cot_own, received)
        received = from_level(cot_own, offset)
        offset *= 2
    first, second = split_rows(cot_own, received)
    first, received = add(first, from_level(second, last)), from_level(first, last)
    rows = cells // last
    offsets = gather_offsets(owners)
    flow_rows = first
    if last > 2:
        part = lax.axis_index("lev") // 2 % (last // 2)
        flow_rows = lax.dynamic_slice_in_dim(first, part * rows, rows, 1)
    flow_rows = flow_rows[None]
    flow_rows = join(flow_rows, from_owner(flow_rows, offsets[0]))
    flow_band = add_flow(first, second, received, tok_col, flow_rows)
    flow_own = swap(flow_band).reshape(count, half)
    flow = (flow_own, from_level(flow_own, 1))
    chip = lax.shift_right_logical(lax.axis_index("lev"), 1)
    chips = lax.axis_size("lev") // 2

    *saved, attended, mix_own, mix_other = forward(
        tok_col, key_mask, w_qkv, w_mix, chunk, owners, flow_band
    )
    attended = swap(attended)
    mix_terms = before_last(pair_total(mix_own, mix_other))
    for offset in offsets[1:-1]:
        flow_rows = join(flow_rows, from_owner(flow_rows, offset))
    received = from_owner(flow_rows, offsets[-1])
    back_col = backward(tok_col, flow, w_mix, w_qkv, saved, mix_terms[0], flow_rows)
    sent = add_mixed(*mix_terms, back_col)
    back = swap(sent.reshape(owners, cells, width + half))
    d_tokens = make_gradient(cot_band, back)

    factor = 1.0 / math.sqrt(count * owners)
    features = width // owners
    attended = attended.reshape(owners, owners, cells, features)
    attended = [chip_rows(attended, 2, chip ^ k).reshape(-1, features) for k in range(chips)]
    attended[1:] = [from_level(attended[k], 2 * k) for k in range(1, chips)]
    flow_rows = arrange(flow_rows, received, sent).reshape(-1, half)
    grads = mix_gradient(attended, (flow_rows, from_level(flow_rows, 1)), factor)
    mix_grad = grads[0]
    for k in range(1, chips):
        mix_grad += from_level(grads[k], 2 * k).astype(F32)

    mix_band = cut_mixed(back, mix_grad)
    output = make_output(tok_band, level_scale, (mix_band, from_level(mix_band, 1)))
    return (
        output.reshape(tokens.shape),
        d_tokens.reshape(tokens.shape),
        mix_grad.reshape(1, width // owners, width),
    )


def solution(mesh):
    return jax.shard_map(
        on_device,
        mesh=mesh,
        in_specs=(
            P(None, "lev", "lat", None, None),
            P(),
            P(),
            P("lev", None, None),
            P("lev", None),
            P(None, "lev", "lat", None, None),
        ),
        out_specs=(
            P(None, "lev", "lat", None, None),
            P(None, "lev", "lat", None, None),
            P("lev", "lat", None),
        ),
        check_vma=False,
    )
```

```python
import functools
import math

import jax
import jax.numpy as jnp
from jax import lax
from jax.experimental import pallas as pl
from jax.experimental.pallas import tpu as pltpu
from jax.sharding import PartitionSpec as P

HEADS = 16
GROUP = 256

epsilon = 1e-06
score_scale = 0.25

F32 = jnp.float32
BF16 = jnp.bfloat16


def nn(a, b):
    return lax.dot_general(a, b, (((1,), (0,)), ((), ())), preferred_element_type=F32)


def nt(a, b):
    return lax.dot_general(a, b, (((1,), (1,)), ((), ())), preferred_element_type=F32)


def tn(a, b):
    return lax.dot_general(a, b, (((0,), (0,)), ((), ())), preferred_element_type=F32)


def block_mean(head_width):
    row = lax.broadcasted_iota(jnp.int32, (GROUP, GROUP), 0) // head_width
    col = lax.broadcasted_iota(jnp.int32, (GROUP, GROUP), 1) // head_width
    return jnp.where(row == col, 1.0 / head_width, 0.0).astype(BF16)


def params():
    return pltpu.CompilerParams(vmem_limit_bytes=36 * 1024 * 1024)


def half_cols(which, width):
    half = width // 2
    core = lax.axis_index("lev") % 2
    return pl.ds(pl.multiple_of((core ^ which) * half, half), half)


def in_hbm(array):
    return pltpu.with_memory_space_constraint(array, pltpu.HBM)


def call(kernel, name, out_shape, *operands):
    return pl.pallas_call(
        kernel, out_shape=out_shape, compiler_params=params(), name=name
    )(*operands)


def pack_kernel(tok_ref, cot_ref, gain_ref, tok_out, *cot_outs):
    batch, rows, parts, chunk, width = tok_ref.shape
    for b in range(batch):
        for q in range(parts):
            for r in range(rows):
                tok_out[b * parts + q, r * chunk : (r + 1) * chunk, :] = tok_ref[b, r, q]
    for s in range(2):
        cols = half_cols(s, width)
        gain = gain_ref[:, cols]
        for b in range(batch):
            for q in range(parts):
                for r in range(rows):
                    piece = cot_ref[b, r, q, :, cols].astype(F32)
                    cot_outs[s][b * parts + q, r * chunk : (r + 1) * chunk, :] = (
                        piece * gain
                    ).astype(BF16)


def pack(tokens, cot, gain):
    batch, rows, parts, chunk, width = tokens.shape
    shape = (batch * parts, rows * chunk)
    return call(
        pack_kernel,
        "pack",
        [jax.ShapeDtypeStruct(shape + (width,), BF16)]
        + [jax.ShapeDtypeStruct(shape + (width // 2,), BF16)] * 2,
        in_hbm(tokens),
        in_hbm(cot),
        in_hbm(gain),
    )


def output_kernel(tok_ref, gain_ref, own_ref, other_ref, out_ref):
    batch, rows, parts, chunk, width = tok_ref.shape
    for s, ref in enumerate((own_ref, other_ref)):
        cols = half_cols(s, width)
        gain = gain_ref[:, cols]
        for t in range(batch * parts):
            b, q = t // parts, t % parts
            for r in range(rows):
                mixed = ref[t, r * chunk : (r + 1) * chunk, :].astype(F32)
                out_ref[b, r, q, :, cols] = (
                    tok_ref[b, r, q, :, cols].astype(F32) + gain * mixed
                ).astype(BF16)


def make_output(tokens, gain, mixed):
    return call(
        output_kernel,
        "make_output",
        jax.ShapeDtypeStruct(tokens.shape, BF16),
        tokens,
        gain,
        *mixed,
    )


def gradient_kernel(cot_ref, back_ref, out_ref):
    batch, rows, parts, chunk, width = cot_ref.shape
    for b in range(batch):
        for q in range(parts):
            for r in range(rows):
                back = back_ref[b * parts + q, r * chunk : (r + 1) * chunk, :width].astype(F32)
                out_ref[b, r, q] = (cot_ref[b, r, q].astype(F32) + back).astype(BF16)


def make_gradient(cot, back):
    return call(
        gradient_kernel, "make_gradient", jax.ShapeDtypeStruct(cot.shape, BF16), cot, back
    )


def by_head(tile, lane):
    zero = jnp.zeros_like(tile)
    return jnp.concatenate([jnp.where(lane == 0, tile, zero), jnp.where(lane == 1, tile, zero)], axis=0)


def own_rows(turned, head_width):
    count = turned.shape[1] // 2
    return [turned[:head_width, :count], turned[head_width:, count:]]


def side_by_side(stacked):
    count = stacked.shape[0] // 2
    return jnp.concatenate([stacked[:count], stacked[count:]], axis=1)


def forward_kernel(
    samples, lat_count, chunk, owners,
    tok_ref, mask_ref, wq_ref, wk_ref, wv_ref, wm_ref, _,
    qn_ref, kn_ref, v_ref, rq_ref, rk_ref, at_ref, ri_ref, p_ref, att_ref, own_ref, other_ref,
    normed_ref, acc_ref, keep_ref,
):
    step = pl.program_id(0)
    count, width = normed_ref.shape
    head_width = width // HEADS

    @pl.when(step == 0)
    def _():
        x = tok_ref[...].astype(F32)
        rx = lax.rsqrt(jnp.mean(x * x, axis=-1, keepdims=True) + epsilon)
        normed_ref[...] = (x * rx).astype(BF16)
        acc_ref[...] = jnp.zeros_like(acc_ref)
        spread = (
            lax.broadcasted_iota(jnp.int32, (lat_count, count), 0)
            == lax.broadcasted_iota(jnp.int32, (lat_count, count), 1) // chunk
        ).astype(F32)
        per_sample = nn(mask_ref[...].astype(F32), spread)
        mine = lax.axis_index("lat") // (owners // samples)
        pick = lax.broadcasted_iota(jnp.int32, (samples, count), 0) == mine
        valid = jnp.sum(jnp.where(pick, per_sample, 0.0), axis=0, keepdims=True)
        same = (
            lax.broadcasted_iota(jnp.int32, (count, count), 0) % chunk
            == lax.broadcasted_iota(jnp.int32, (count, count), 1) % chunk
        )
        keep_ref[...] = jnp.where(same, valid, 0.0)

    normed = normed_ref[...]
    mean_mat = block_mean(head_width)
    q = nn(normed, wq_ref[...])
    k = nn(normed, wk_ref[...])
    v = nn(normed, wv_ref[...]).astype(BF16)
    rq = lax.rsqrt(nn((q * q).astype(BF16), mean_mat) + epsilon)
    rk = lax.rsqrt(nn((k * k).astype(BF16), mean_mat) + epsilon)
    qn = (q * rq).astype(BF16)
    kn = (k * rk).astype(BF16)
    qn_ref[...] = qn
    kn_ref[...] = kn
    v_ref[...] = v
    rq_ref[...] = rq.astype(BF16)
    rk_ref[...] = rk.astype(BF16)
    keep = keep_ref[...]
    keep = jnp.concatenate([keep, keep], axis=0)
    lane = lax.broadcasted_iota(jnp.int32, (count, 128), 1) // head_width
    ones = by_head(jnp.ones((count, 128), BF16), lane)
    tiles = []
    for t in range(GROUP // 128):
        cols = slice(t * 128, (t + 1) * 128)
        v_ones = jnp.concatenate([by_head(v[:, cols], lane), ones], axis=1)
        e = jnp.exp(nt(by_head(qn[:, cols] * score_scale, lane), kn[:, cols])) * keep
        e = e.astype(BF16)
        p_ref[t] = e
        o = nn(side_by_side(e), v_ones)
        inverse = 1.0 / o[:, 128:]
        tiles.append(o[:, :128] * inverse)
        ri_ref[:, cols] = inverse
    att = jnp.concatenate(tiles, axis=1).astype(BF16)
    at_ref[...] = att
    features = att_ref.shape[-1]
    for f in range(GROUP // features):
        att_ref[f] = att[:, f * features : (f + 1) * features]
    acc_ref[...] += nn(att, wm_ref[...])

    @pl.when(step == pl.num_programs(0) - 1)
    def _():
        for s, ref in enumerate((own_ref, other_ref)):
            ref[...] = acc_ref[:, half_cols(s, width)].astype(BF16)


def forward(tok_col, key_mask, w_qkv, w_mix, chunk, owners, after):
    count, width = tok_col.shape
    samples, lat_count = key_mask.shape
    steps = width // GROUP
    features = width // owners
    same = lambda shape: pl.BlockSpec(shape, lambda i: (0, 0))
    cols = pl.BlockSpec((count, GROUP), lambda i: (0, i))
    weight = lambda which: pl.BlockSpec((width, GROUP), lambda i: (0, i + which * steps))
    return pl.pallas_call(
        functools.partial(forward_kernel, samples, lat_count, chunk, owners),
        out_shape=(
            [pltpu.HBM((count, width), BF16)] * 6
            + [pltpu.HBM((count, width), F32)]
            + [pltpu.HBM((width // 128, 2 * count, count), BF16)]
            + [jax.ShapeDtypeStruct((owners, count, features), BF16)]
            + [jax.ShapeDtypeStruct((count, width // 2), BF16)] * 2
        ),
        grid=(steps,),
        in_specs=[
            same((count, width)),
            same((samples, lat_count)),
            weight(0),
            weight(1),
            weight(2),
            pl.BlockSpec((GROUP, width), lambda i: (i, 0)),
            pl.BlockSpec(memory_space=pl.ANY),
        ],
        out_specs=(
            [cols] * 7
            + [pl.BlockSpec((GROUP // 128, 2 * count, count), lambda i: (i, 0, 0))]
            + [pl.BlockSpec((GROUP // features, count, features), lambda i: (i, 0, 0))]
            + [same((count, width // 2))] * 2
        ),
        scratch_shapes=[
            pltpu.VMEM((count, width), BF16),
            pltpu.VMEM((count, width), F32),
            pltpu.VMEM((count, count), F32),
        ],
        compiler_params=params(),
        cost_estimate=pl.CostEstimate(
            flops=2 * count * width * (4 * width + 2 * count * 4),
            bytes_accessed=20 * count * width + 8 * width * width,
            transcendentals=HEADS * count * count,
        ),
        name="forward",
    )(tok_col, key_mask, *[in_hbm(w_qkv)] * 3, in_hbm(w_mix), after)


def backward_kernel(
    tok_ref, own_ref, other_ref, wm_ref, wq_ref, wk_ref, wv_ref,
    qn_ref, kn_ref, v_ref, rq_ref, rk_ref, at_ref, ri_ref, p_ref, *rest,
):
    out_ref, acc_ref = rest[-2:]
    step = pl.program_id(0)
    count, width = acc_ref.shape
    head_width = width // HEADS
    d_att = nt(own_ref[...], wm_ref[:, half_cols(0, width)])
    d_att += nt(other_ref[...], wm_ref[:, half_cols(1, width)])
    inverse = ri_ref[...]
    d_att = (d_att * inverse).astype(BF16)
    mean_mat = block_mean(head_width)
    product = d_att.astype(F32) * at_ref[...].astype(F32)
    coarse = product.astype(BF16)
    rest_of = (product - coarse.astype(F32)).astype(BF16)
    inner_all = (nn(coarse, mean_mat) + nn(rest_of, mean_mat)) * float(head_width)
    qn, kn, v = qn_ref[...], kn_ref[...], v_ref[...]
    lane = lax.broadcasted_iota(jnp.int32, (count, 128), 1) // head_width
    dq_tiles, dk_tiles, dv_tiles = [], [], []
    for t in range(GROUP // 128):
        cols = slice(t * 128, (t + 1) * 128)
        d_t = d_att[:, cols]
        d_p = nt(by_head(d_t, lane), v[:, cols])
        e = p_ref[t]
        e_wide = e.astype(F32)
        first = t * 128
        second = first + head_width
        inner = jnp.concatenate(
            [inner_all[:, first : first + 1], inner_all[:, second : second + 1]], axis=0
        )
        d_s = (e_wide * (d_p - inner)).astype(BF16)
        d_s = side_by_side(d_s)
        dq_tiles.append(nn(d_s, by_head(kn[:, cols], lane)))
        dk_tiles += own_rows(tn(qn[:, cols], d_s), head_width)
        dv_tiles += own_rows(tn(d_t, side_by_side(e)), head_width)
    dq = jnp.concatenate(dq_tiles, axis=1) * score_scale
    dk = jnp.concatenate(dk_tiles, axis=0).T * score_scale
    dv = jnp.concatenate(dv_tiles, axis=0).T.astype(BF16)

    def through_norm(upstream, unit, factor):
        unit = unit.astype(F32)
        inner = nn((upstream * unit).astype(BF16), mean_mat)
        return (factor.astype(F32) * (upstream - unit * inner)).astype(BF16)

    gq = through_norm(dq, qn, rq_ref[...])
    gk = through_norm(dk, kn, rk_ref[...])
    total = nt(gq, wq_ref[...]) + nt(gk, wk_ref[...]) + nt(dv, wv_ref[...])

    @pl.when(step == 0)
    def _():
        acc_ref[...] = total

    @pl.when(step > 0)
    def _():
        acc_ref[...] += total

    @pl.when(step == pl.num_programs(0) - 1)
    def _():
        x = tok_ref[...].astype(F32)
        rx = lax.rsqrt(jnp.mean(x * x, axis=-1, keepdims=True) + epsilon)
        d = acc_ref[...]
        inner = jnp.mean(d * x, axis=-1, keepdims=True)
        out_ref[...] = (rx * d - x * (rx * rx * rx * inner)).astype(BF16)


def backward(tok_col, flow, w_mix, w_qkv, saved, *after):
    count, width = tok_col.shape
    steps = width // GROUP
    same = lambda shape: pl.BlockSpec(shape, lambda i: (0, 0))
    cols = pl.BlockSpec((count, GROUP), lambda i: (0, i))
    weight = lambda which: pl.BlockSpec((width, GROUP), lambda i: (0, i + which * steps))
    return pl.pallas_call(
        backward_kernel,
        out_shape=jax.ShapeDtypeStruct((count, width), BF16),
        grid=(steps,),
        in_specs=[
            same((count, width)),
            same((count, width // 2)),
            same((count, width // 2)),
            pl.BlockSpec((GROUP, width), lambda i: (i, 0)),
            weight(0),
            weight(1),
            weight(2),
            *([cols] * 7),
            pl.BlockSpec((GROUP // 128, 2 * count, count), lambda i: (i, 0, 0)),
        ]
        + [pl.BlockSpec(memory_space=pl.ANY)] * len(after),
        out_specs=same((count, width)),
        scratch_shapes=[pltpu.VMEM((count, width), F32)],
        compiler_params=params(),
        cost_estimate=pl.CostEstimate(
            flops=2 * count * width * (4 * width + 4 * count * 4),
            bytes_accessed=20 * count * width + 8 * width * width,
            transcendentals=0,
        ),
        name="backward",
    )(tok_col, *flow, in_hbm(w_mix), *[in_hbm(w_qkv)] * 3, *map(in_hbm, saved), *after)


def mix_gradient_kernel(factor, own_flow_ref, other_flow_ref, *refs):
    att_refs, out_refs = refs[: len(refs) // 2], refs[len(refs) // 2 :]
    width = out_refs[0].shape[-1]
    for att_ref, out_ref in zip(att_refs, out_refs):
        att = att_ref[...]
        for s, flow_ref in enumerate((own_flow_ref, other_flow_ref)):
            term = tn(att, flow_ref[...]) * factor
            out_ref[:, half_cols(s, width)] = term.astype(out_ref.dtype)


def mix_gradient(attended, flow, factor):
    rows, features = attended[0].shape
    width = 2 * flow[0].shape[-1]
    out = [jax.ShapeDtypeStruct((features, width), F32)]
    out += [jax.ShapeDtypeStruct((features, width), BF16)] * (len(attended) - 1)
    return pl.pallas_call(
        functools.partial(mix_gradient_kernel, factor),
        out_shape=out,
        compiler_params=params(),
        cost_estimate=pl.CostEstimate(
            flops=2 * rows * features * width * len(attended),
            bytes_accessed=2 * rows * (features * len(attended) + width),
            transcendentals=0,
        ),
        name="mix_gradient",
    )(*flow, *attended)


def chip_rows(array, axis, chip):
    rows = array.shape[axis] // (lax.axis_size("lev") // 2)
    return lax.dynamic_slice_in_dim(array, (chip * rows).astype(jnp.uint32), rows, axis)


def swap(block):
    return lax.all_to_all(block, "lat", split_axis=0, concat_axis=0, tiled=True)


def from_level(block, offset):
    return lax.ppermute(block, "lev", [(i, i ^ offset) for i in range(lax.axis_size("lev"))])


def add_kernel(own_ref, received_ref, out_ref):
    out_ref[...] = (own_ref[...].astype(F32) + received_ref[...].astype(F32)).astype(BF16)


def add(own, received):
    return call(add_kernel, "add", jax.ShapeDtypeStruct(own.shape, BF16), own, received)


def pair_total(own, other):
    return add(own, from_level(other, 1))


def before_last(total):
    offset = 2
    while 2 * offset < lax.axis_size("lev"):
        total = add(total, from_level(total, offset))
        offset *= 2
    return total, from_level(total, offset)


def row_half(which, rows):
    top = lax.axis_index("lev") // (lax.axis_size("lev") // 2)
    return pl.ds(pl.multiple_of((top ^ which) * rows, rows), rows)


def split_kernel(own_ref, received_ref, first_ref, second_ref):
    rows = first_ref.shape[1]
    for which, ref in enumerate((first_ref, second_ref)):
        at = row_half(which, rows)
        total = own_ref[:, at, :].astype(F32) + received_ref[:, at, :].astype(F32)
        ref[...] = total.astype(BF16)


def split_rows(own, received):
    owners, cells, half = own.shape
    rows = cells // 2
    if rows % 16 == 0:
        part = jax.ShapeDtypeStruct((owners, rows, half), BF16)
        return call(split_kernel, "split_rows", [part, part], own, received)
    total = (own.astype(F32) + received.astype(F32)).astype(BF16)
    top = lax.axis_index("lev") // (lax.axis_size("lev") // 2)
    return [lax.dynamic_slice_in_dim(total, (top ^ k) * rows, rows, 1) for k in range(2)]


def add_flow_kernel(first_ref, second_ref, received_ref, _, __, out_ref):
    rows = first_ref.shape[1]
    out_ref[:, row_half(0, rows), :] = first_ref[...]
    second = second_ref[...].astype(F32) + received_ref[...].astype(F32)
    out_ref[:, row_half(1, rows), :] = second.astype(BF16)


def add_flow(first, second, received, *after):
    owners, rows, half = first.shape
    if rows % 16:
        second = (second.astype(F32) + received.astype(F32)).astype(BF16)
        top = lax.axis_index("lev") // (lax.axis_size("lev") // 2)
        pair = jnp.where(top == 0, jnp.stack([first, second]), jnp.stack([second, first]))
        return jnp.concatenate([pair[0], pair[1]], axis=1)
    whole = pl.BlockSpec(memory_space=pltpu.VMEM)
    return pl.pallas_call(
        add_flow_kernel,
        out_shape=jax.ShapeDtypeStruct((owners, 2 * rows, half), BF16),
        in_specs=[whole] * 3 + [pl.BlockSpec(memory_space=pl.ANY)] * 2,
        out_specs=whole,
        compiler_params=params(),
        name="add_flow",
    )(first, second, received, *after)


def join_kernel(first_ref, second_ref, out_ref):
    count = first_ref.shape[0]
    out_ref[:count] = first_ref[...]
    out_ref[count:] = second_ref[...]


def join(first, second):
    shape = jax.ShapeDtypeStruct((2 * first.shape[0],) + first.shape[1:], BF16)
    return call(join_kernel, "join", shape, first, second)


def from_owner(block, offset):
    return lax.ppermute(block, "lat", [(i, i ^ offset) for i in range(lax.axis_size("lat"))])


def gather_offsets(owners):
    offsets = [owners // 4, owners // 2]
    while len(offsets) < owners.bit_length() - 1:
        offsets.append(owners >> (len(offsets) + 1))
    return offsets


def arrange_kernel(first_ref, second_ref, _, out_ref):
    owners = out_ref.shape[1]
    half = owners // 2
    offsets = gather_offsets(owners)
    for u in range(owners):
        band = lax.axis_index("lat") ^ sum(o for k, o in enumerate(offsets) if u >> k & 1)
        ref = first_ref if u < half else second_ref
        out_ref[:, band] = ref[u % half]


def arrange(first, second, after):
    _, owners, rows, half = first.shape
    whole = pl.BlockSpec(memory_space=pltpu.VMEM)
    return pl.pallas_call(
        arrange_kernel,
        out_shape=jax.ShapeDtypeStruct((owners, owners, rows, half), BF16),
        in_specs=[whole, whole, pl.BlockSpec(memory_space=pl.ANY)],
        out_specs=whole,
        compiler_params=params(),
        name="arrange",
    )(first, second, after)


def add_mixed_kernel(own_ref, received_ref, back_ref, out_ref):
    width = back_ref.shape[-1]
    out_ref[:, :width] = back_ref[...]
    out_ref[:, width:] = (own_ref[...].astype(F32) + received_ref[...].astype(F32)).astype(BF16)


def add_mixed(own, received, back):
    count, width = back.shape
    shape = jax.ShapeDtypeStruct((count, width + own.shape[-1]), BF16)
    return call(add_mixed_kernel, "add_mixed", shape, own, received, back)


def cut_kernel(in_ref, _, out_ref):
    out_ref[...] = in_ref[:, :, in_ref.shape[-1] - out_ref.shape[-1] :]


def cut_mixed(received, after):
    owners, cells, wide = received.shape
    whole = pl.BlockSpec(memory_space=pltpu.VMEM)
    return pl.pallas_call(
        cut_kernel,
        out_shape=jax.ShapeDtypeStruct((owners, cells, wide // 3), BF16),
        in_specs=[whole, pl.BlockSpec(memory_space=pl.ANY)],
        out_specs=whole,
        compiler_params=params(),
        name="cut_mixed",
    )(received, after)


def on_device(tokens, key_mask, w_qkv, w_mix, level_scale, cotangent):
    batch, _, rows, lon, width = tokens.shape
    owners = lax.axis_size("lat")
    parts = owners // batch
    chunk = lon // parts
    cells = rows * chunk
    count = batch * rows * lon
    half = width // 2
    tok_band = tokens.reshape(batch, rows, parts, chunk, width)
    cot_band = cotangent.reshape(batch, rows, parts, chunk, width)
    w_mix = w_mix.reshape(width, width)

    tok_send, cot_own, cot_other = pack(tok_band, cot_band, level_scale)
    tok_col = swap(tok_send).reshape(count, width)
    last = lax.axis_size("lev") // 2
    received = from_level(cot_other, 1)
    offset = 2
    while offset < last:
        cot_own = add(cot_own, received)
        received = from_level(cot_own, offset)
        offset *= 2
    first, second = split_rows(cot_own, received)
    first, received = add(first, from_level(second, last)), from_level(first, last)
    rows = cells // last
    offsets = gather_offsets(owners)
    flow_rows = first
    if last > 2:
        part = lax.axis_index("lev") // 2 % (last // 2)
        flow_rows = lax.dynamic_slice_in_dim(first, part * rows, rows, 1)
    flow_rows = flow_rows[None]
    flow_rows = join(flow_rows, from_owner(flow_rows, offsets[0]))
    flow_band = add_flow(first, second, received, tok_col, flow_rows)
    flow_own = swap(flow_band).reshape(count, half)
    flow = (flow_own, from_level(flow_own, 1))
    chip = lax.shift_right_logical(lax.axis_index("lev"), 1)
    chips = lax.axis_size("lev") // 2

    *saved, attended, mix_own, mix_other = forward(
        tok_col, key_mask, w_qkv, w_mix, chunk, owners, flow_band
    )
    attended = swap(attended)
    mix_terms = before_last(pair_total(mix_own, mix_other))
    for offset in offsets[1:-1]:
        flow_rows = join(flow_rows, from_owner(flow_rows, offset))
    received = from_owner(flow_rows, offsets[-1])
    back_col = backward(tok_col, flow, w_mix, w_qkv, saved, mix_terms[0], flow_rows)
    sent = add_mixed(*mix_terms, back_col)
    back = swap(sent.reshape(owners, cells, width + half))
    d_tokens = make_gradient(cot_band, back)

    factor = 1.0 / math.sqrt(count * owners)
    features = width // owners
    attended = attended.reshape(owners, owners, cells, features)
    attended = [chip_rows(attended, 2, chip ^ k).reshape(-1, features) for k in range(chips)]
    attended[1:] = [from_level(attended[k], 2 * k) for k in range(1, chips)]
    flow_rows = arrange(flow_rows, received, attended[-1]).reshape(-1, half)
    grads = mix_gradient(attended, (flow_rows, from_level(flow_rows, 1)), factor)
    mix_grad = grads[0]
    for k in range(1, chips):
        mix_grad += from_level(grads[k], 2 * k).astype(F32)

    mix_band = cut_mixed(back, mix_grad)
    output = make_output(tok_band, level_scale, (mix_band, from_level(mix_band, 1)))
    return (
        output.reshape(tokens.shape),
        d_tokens.reshape(tokens.shape),
        mix_grad.reshape(1, width // owners, width),
    )


def solution(mesh):
    return jax.shard_map(
        on_device,
        mesh=mesh,
        in_specs=(
            P(None, "lev", "lat", None, None),
            P(),
            P(),
            P("lev", None, None),
            P("lev", None),
            P(None, "lev", "lat", None, None),
        ),
        out_specs=(
            P(None, "lev", "lat", None, None),
            P(None, "lev", "lat", None, None),
            P("lev", "lat", None),
        ),
        check_vma=False,
    )
```
